32 devices in a mesh: groups: 2 (over y), tok: 4 (over z), blk: 2 (over x), sub: 2 (over core).
Axes of the slice: x: 2, y: 2, z: 4, core: 2. Of those that a mesh axis runs over, the one named last changes fastest.
Arguments:
- features_in: bfloat16 [256, 4096], P(('groups', 'tok'), 'blk'), parts along dimension 0, may hold values from -6 to 6
- gate_tiles: bfloat16 [128, 2, 12, 128, 128], P(('tok', 'sub'), 'blk'), may hold values from -0.125 to 0.125
- up_tiles: bfloat16 [128, 2, 12, 128, 128], P(('tok', 'sub'), 'blk'), may hold values from -0.125 to 0.125
- block_rows: int32 [128, 2, 12], P(('tok', 'sub'), 'blk'), may hold values from 0 to 15, as said below
- block_counts: int32 [128, 2], P(('tok', 'sub'), 'blk'), may hold values from 4 to 12
- d_hidden: bfloat16 [256, 16384], P(('groups', 'blk'), ('tok', 'sub')), parts along dimension 0, may hold values from -6 to 6
Outputs:
- hidden: bfloat16 [256, 16384], P(('groups', 'blk'), ('tok', 'sub')), parts along dimension 0
- gate_tiles_grad: bfloat16 [256, 2, 12, 128, 128], P(('groups', 'tok', 'sub'), 'blk'), parts along dimension 0
- up_tiles_grad: bfloat16 [256, 2, 12, 128, 128], P(('groups', 'tok', 'sub'), 'blk'), parts along dimension 0
- features_grad: bfloat16 [256, 4096], P(('groups', 'tok'), 'blk'), parts along dimension 0
The draws below stay inside these ranges and needn't reach their ends.
There are 2 independent parts, one for each index of `groups`. The reference program is written for one: setup_inputs(seed, part) draws one part's arguments, and reference() takes and returns one part's arrays. A program takes and returns all parts, laid end to end along the dimension named above; an argument that names none is the same for every part. Nothing has to cross between parts.
Inputs may be any that keep to these rules, and one draw needn't show every extreme that they name: `block_rows`: the 12 entries of one list are distinct local row-block indices; only the first block_counts of them are kept.
All inputs are finite; a program needn't handle non-finite values.
Results may differ from the reference program's by a relative error of at most 0.015.
Values may be sent and summed in bfloat16 or wider, within the bound.
No kernel may reach another device: no remote copies, remote signals or barrier semaphores. Data moves between devices by JAX's collectives and lax.ppermute only.
A program may use at most 128 MiB of HBM per device.

```python
import jax
import jax.numpy as jnp
from jax import lax

D = 4096
FF = 16384
TILE = 128
TOKENS = 128
CB = 128
RB_LOC = 16
CAP = 12
LOW = 4
N_BLK = 2


def draw_block_rows(key, part):
    key = jax.random.fold_in(key, 11)
    scores = jax.random.randint(key, (CB, N_BLK, RB_LOC), 0, 1 << 20) * RB_LOC + jnp.arange(RB_LOC, dtype=jnp.int32)
    row_order = jnp.argsort(scores, axis=-1, stable=True).astype(jnp.int32)
    return row_order[:, :, :CAP]


def draw_block_counts(key, part):
    key = jax.random.fold_in(key, 12)
    first_key, second_key = jax.random.split(key)
    counts = jax.random.randint(first_key, (CB * N_BLK,), LOW, CAP + 1)
    forced_idx = jax.random.randint(second_key, (), 0, CB * N_BLK)
    counts = jnp.where(jnp.arange(CB * N_BLK) == forced_idx, CAP, counts)
    return counts.reshape(CB, N_BLK).astype(jnp.int32)


def steps_of(rng, extent, pieces, least, top_value):
    level = 1.0
    for axis_at, parts in pieces:
        heights = jax.random.uniform(jax.random.fold_in(jax.random.fold_in(rng, 6), axis_at), (parts,), jnp.float32, least / len(pieces), top_value / len(pieces))
        level = level * jnp.repeat(jnp.exp(heights), extent[axis_at] // parts).reshape((-1,) + (1,) * (len(extent) - 1 - axis_at))
    return level


def normal_values(own_key, dims, scale, reach, shards=(), held_as=jnp.bfloat16):
    array = scale * jax.random.normal(own_key, dims, jnp.float32)
    if shards:
        array = array * steps_of(own_key, dims, shards, -0.22, 0.18)
    return jnp.clip(array, -reach, reach).astype(held_as)


def setup_inputs(seed: int = 0, part: int = 0) -> dict:
    keys = jax.random.split(jax.random.key(seed), 7)
    part_keys = jax.random.split(jax.random.fold_in(keys[6], part), 7)
    return {
        "features_in": normal_values(part_keys[0], (TOKENS, D), 1.0, 6.0, ((0, 4), (1, 2))),
        "gate_tiles": normal_values(keys[1], (CB, N_BLK, CAP, TILE, TILE), (D // 2) ** -0.5, 0.125, ((0, 8), (1, 2))),
        "up_tiles": normal_values(keys[2], (CB, N_BLK, CAP, TILE, TILE), (D // 2) ** -0.5, 0.125, ((0, 8), (1, 2))),
        "block_rows": draw_block_rows(jax.random.fold_in(keys[6], 71), part),
        "block_counts": draw_block_counts(jax.random.fold_in(keys[6], 71), part),
        "d_hidden": normal_values(part_keys[5], (TOKENS, FF), 1.0, 6.0, ((0, 2), (1, 8))),
    }


def reference(features_in, gate_tiles, up_tiles, block_rows, block_counts, d_hidden):
    row_total = features_in.shape[0]
    feature_blocks = features_in.reshape(row_total, N_BLK * RB_LOC, TILE)
    owner_base = (jnp.arange(N_BLK, dtype=jnp.int32) * RB_LOC)[:, None]
    slot_ids = jnp.arange(CAP, dtype=jnp.int32)

    def select(rows_col, count_col):
        row_index = (rows_col + owner_base).astype(jnp.int32).reshape(-1)
        picked = jnp.take(feature_blocks, row_index, axis=1).reshape(row_total, N_BLK, CAP, TILE).astype(jnp.float32)
        kept_mask = (slot_ids[None, :] < count_col[:, None]).astype(jnp.float32)[:, :, None, None]
        return row_index, picked, kept_mask

    def owner_sum(picked, weights):
        partial_value = jnp.einsum("tbkd,bkde->bte", picked, weights)
        rounded = lax.optimization_barrier(partial_value.astype(jnp.bfloat16))
        return jnp.sum(rounded.astype(jnp.float32), axis=0)

    def forward(inputs):
        rows_col, count_col, gate_col, up_col = inputs
        row_index, picked, kept_mask = select(rows_col, count_col)
        return (owner_sum(picked, gate_col.astype(jnp.float32) * kept_mask),
                owner_sum(picked, up_col.astype(jnp.float32) * kept_mask))

    gate_value, up_value = lax.map(forward, (block_rows, block_counts, gate_tiles, up_tiles))
    gate_value = jnp.transpose(gate_value, (1, 0, 2)).reshape(row_total, FF)
    up_value = jnp.transpose(up_value, (1, 0, 2)).reshape(row_total, FF)
    sig_gate = jax.nn.sigmoid(gate_value)
    act_gate = gate_value * sig_gate
    hidden = (act_gate * up_value).astype(jnp.bfloat16)
    cotangent = d_hidden.astype(jnp.float32)
    gate_grad = (cotangent * up_value * sig_gate * (1.0 + gate_value * (1.0 - sig_gate))).astype(jnp.bfloat16)
    up_grad = (cotangent * act_gate).astype(jnp.bfloat16)
    gate_cols = jnp.transpose(gate_grad.reshape(row_total, CB, TILE), (1, 0, 2))
    up_cols = jnp.transpose(up_grad.reshape(row_total, CB, TILE), (1, 0, 2))

    def backward(dx_carry, inputs):
        rows_col, count_col, gate_col, up_col, gate_rows, up_rows = inputs
        row_index, picked, kept_mask = select(rows_col, count_col)
        gate_f = gate_rows.astype(jnp.float32)
        up_f = up_rows.astype(jnp.float32)
        d_gate = (jnp.einsum("tbkd,te->bkde", picked, gate_f) * kept_mask).astype(jnp.bfloat16)
        d_up = (jnp.einsum("tbkd,te->bkde", picked, up_f) * kept_mask).astype(jnp.bfloat16)
        back_term = jnp.einsum("te,bkde->tbkd", gate_f, gate_col.astype(jnp.float32) * kept_mask)
        back_term = back_term + jnp.einsum("te,bkde->tbkd", up_f, up_col.astype(jnp.float32) * kept_mask)
        dx_carry = dx_carry.at[:, row_index].add(back_term.reshape(row_total, N_BLK * CAP, TILE))
        return dx_carry, (d_gate, d_up)

    zero_carry = jnp.zeros((row_total, N_BLK * RB_LOC, TILE), jnp.float32)
    dx_sum, grads = lax.scan(backward, zero_carry, (block_rows, block_counts, gate_tiles, up_tiles, gate_cols, up_cols))
    return hidden, grads[0], grads[1], dx_sum.reshape(row_total, N_BLK * RB_LOC * TILE).astype(jnp.bfloat16)
```

```python
import functools

import jax
import jax.numpy as jnp
from jax import lax
from jax.experimental import pallas as pl
from jax.experimental.pallas import tpu as pltpu
from jax.sharding import PartitionSpec as P

F32 = jnp.float32
BF16 = jnp.bfloat16
MIB = 1 << 20
VMEM_SPEC = pl.BlockSpec(memory_space=pltpu.VMEM)
SMEM_SPEC = pl.BlockSpec(memory_space=pltpu.SMEM)
ANY_SPEC = pl.BlockSpec(memory_space=pl.ANY)


def limit(mib):
    return pltpu.CompilerParams(vmem_limit_bytes=mib * MIB)


def lanes(index, width):
    return pl.ds(pl.multiple_of(index * width, width), width)


def weights_of(c, gate_ref, up_ref):
    slots, rows, cols = gate_ref.shape[2:]
    return jnp.concatenate(
        [gate_ref[c, 0].reshape(slots * rows, cols), up_ref[c, 0].reshape(slots * rows, cols)], axis=1
    )


def forward_column(c, rows_ref, counts_ref, x_ref, gate_ref, up_ref, part_ref):
    slots, tile = gate_ref.shape[2:4]
    count = counts_ref[c, 0]
    picked = []
    for k in range(slots):
        block = x_ref[:, lanes(rows_ref[c, 0, k], tile)]
        picked.append(jnp.where(k < count, block, jnp.zeros_like(block)))
    part_ref[c] = jnp.dot(
        jnp.concatenate(picked, axis=1), weights_of(c, gate_ref, up_ref), preferred_element_type=F32
    ).astype(BF16)


def load_forward_kernel(rows_ref, counts_ref, x_ref, gate_hbm, up_hbm, part_ref, gate_ref, up_ref, sems):
    cols = gate_ref.shape[0]

    def copies(c):
        return (
            pltpu.make_async_copy(gate_hbm.at[c], gate_ref.at[c], sems.at[0, c]),
            pltpu.make_async_copy(up_hbm.at[c], up_ref.at[c], sems.at[1, c]),
        )

    for c in range(cols):
        for copy in copies(c):
            copy.start()

    def body(c, carry):
        for copy in copies(c):
            copy.wait()
        forward_column(c, rows_ref, counts_ref, x_ref, gate_ref, up_ref, part_ref)
        return carry

    lax.fori_loop(0, cols, body, 0)


def forward_kernel(rows_ref, counts_ref, x_ref, gate_ref, up_ref, part_ref):
    def body(c, carry):
        forward_column(c, rows_ref, counts_ref, x_ref, gate_ref, up_ref, part_ref)
        return carry

    lax.fori_loop(0, gate_ref.shape[0], body, 0, unroll=2)


def backward_kernel(owners, step, meta_ref, rows_ref, counts_ref, gate_ref, up_ref, *refs):
    parts = refs[:owners]
    cots = refs[owners : 2 * owners]
    hidden_ref, grads_ref, dx_ref, cot_ref, acc_ref, sem = refs[2 * owners :]
    cols, _, slots, tile, _ = gate_ref.shape
    shard_rows = cot_ref.shape[0]
    shards_each = cots[0].shape[0] // shard_rows
    shard = meta_ref[0] ^ step
    source = (shard // shards_each) ^ meta_ref[1]
    first_row = pl.multiple_of((shard % shards_each) * shard_rows, shard_rows)
    for i, cot in enumerate(cots):

        @pl.when(source == i)
        def _(cot=cot):
            pltpu.make_async_copy(cot.at[pl.ds(first_row, shard_rows)], cot_ref, sem).start()

    acc_ref[...] = jnp.zeros_like(acc_ref)
    pltpu.make_async_copy(cots[0].at[pl.ds(0, shard_rows)], cot_ref, sem).wait()

    def body(c, carry):
        total = parts[0][c].astype(F32)
        for part in parts[1:]:
            total = total + part[c].astype(F32)
        gate_value, up_value = total[:, :tile], total[:, tile:]
        cotangent = cot_ref[:, lanes(c, tile)].astype(F32)
        sig_gate = jax.nn.sigmoid(gate_value)
        act_gate = gate_value * sig_gate
        hidden_ref[:, lanes(c, tile)] = (act_gate * up_value).astype(BF16)
        gate_grad = (cotangent * up_value * sig_gate * (1.0 + gate_value * (1.0 - sig_gate))).astype(BF16)
        up_grad = (cotangent * act_gate).astype(BF16)
        grads = jnp.concatenate([gate_grad, up_grad], axis=1)
        grads_ref[c] = grads
        back = lax.dot_general(
            grads, weights_of(c, gate_ref, up_ref), (((1,), (1,)), ((), ())), preferred_element_type=F32
        )
        count = counts_ref[c, 0]
        for k in range(slots):
            row = rows_ref[c, 0, k]
            term = back[:, k * tile : (k + 1) * tile]
            acc_ref[row] += jnp.where(k < count, term, jnp.zeros_like(term))
        return carry

    lax.fori_loop(0, cols, body, 0, unroll=2)
    for r in range(acc_ref.shape[0]):
        dx_ref[:, r * tile : (r + 1) * tile] = acc_ref[r].astype(BF16)


def tile_grads_kernel(shards, meta_ref, rows_ref, counts_ref, *refs):
    xs = refs[:shards]
    grads = refs[shards : 2 * shards]
    hiddens = refs[2 * shards : 3 * shards]
    gate_hbm, up_hbm, hidden_hbm, turned_ref, gate_ref, up_ref, sems, hidden_sems = refs[3 * shards :]
    cols, _, slots, tile, _ = gate_ref.shape
    shard_rows = hiddens[0].shape[0]
    shards_each = hidden_hbm.shape[0] // shard_rows

    def hidden_copy(i, source):
        return pltpu.make_async_copy(
            source, hidden_hbm.at[pl.ds(i * shard_rows, shard_rows)], hidden_sems.at[i]
        )

    for i in range(shards_each):
        step = (meta_ref[1] * shards_each + i) ^ meta_ref[0]
        for j in range(shards):

            @pl.when(step == j)
            def _(i=i, j=j):
                hidden_copy(i, hiddens[j]).start()

    for r in range(turned_ref.shape[0]):
        block = jnp.concatenate([x[:, r * tile : (r + 1) * tile] for x in xs], axis=0)
        turned_ref[r] = block.T

    def copies(c):
        return (
            pltpu.make_async_copy(gate_ref.at[c], gate_hbm.at[c], sems.at[0, c]),
            pltpu.make_async_copy(up_ref.at[c], up_hbm.at[c], sems.at[1, c]),
        )

    def body(c, carry):
        picked = jnp.concatenate([turned_ref[rows_ref[c, 0, k]] for k in range(slots)], axis=0)
        grad = jnp.concatenate([g[c] for g in grads], axis=0)
        found = jnp.dot(picked, grad, preferred_element_type=F32)
        count = counts_ref[c, 0]
        for k in range(slots):
            term = found[k * tile : (k + 1) * tile]
            term = jnp.where(k < count, term, jnp.zeros_like(term)).astype(BF16)
            gate_ref[c, 0, k] = term[:, :tile]
            up_ref[c, 0, k] = term[:, tile:]
        for copy in copies(c):
            copy.start()
        return carry

    lax.fori_loop(0, cols, body, 0)

    def finish(c, carry):
        for copy in copies(c):
            copy.wait()
        return carry

    lax.fori_loop(0, cols, finish, 0)
    for i in range(shards_each):
        hidden_copy(i, hiddens[0]).wait()


def swap(x, axis, step):
    return lax.ppermute(x, axis, [(i, i ^ step) for i in range(lax.axis_size(axis))])


def on_device(features_in, gate_tiles, up_tiles, block_rows, block_counts, d_hidden):
    shards, owners = lax.axis_size("tok"), lax.axis_size("blk")
    cols, _, slots, tile, _ = gate_tiles.shape
    shard_rows, width = features_in.shape
    row_blocks = width // tile
    hidden_cols = cols * tile
    meta = jnp.stack([lax.axis_index("tok"), lax.axis_index("blk")]).astype(jnp.int32)

    cots = [d_hidden] + [swap(d_hidden, "blk", s) for s in range(1, owners)]
    xs = [features_in] + [swap(features_in, "tok", s) for s in range(1, shards)]

    part_shape = jax.ShapeDtypeStruct((cols, shard_rows, 2 * tile), BF16)
    macs = shard_rows * cols * slots * tile * tile * 2
    weight_bytes = 2 * cols * slots * tile * tile * 2
    part, gate_held, up_held = pl.pallas_call(
        load_forward_kernel,
        out_shape=(
            part_shape,
            pltpu.VMEM(gate_tiles.shape, BF16),
            pltpu.VMEM(up_tiles.shape, BF16),
        ),
        in_specs=[SMEM_SPEC, SMEM_SPEC, VMEM_SPEC, ANY_SPEC, ANY_SPEC],
        out_specs=(VMEM_SPEC, VMEM_SPEC, VMEM_SPEC),
        scratch_shapes=[pltpu.SemaphoreType.DMA((2, cols))],
        compiler_params=limit(16),
        cost_estimate=pl.CostEstimate(flops=2 * macs, bytes_accessed=weight_bytes, transcendentals=0),
        name="load_forward",
    )(block_rows, block_counts, features_in, gate_tiles, up_tiles)
    parts = [part]
    for s in range(1, shards):
        parts.append(
            pl.pallas_call(
                forward_kernel,
                out_shape=part_shape,
                in_specs=[SMEM_SPEC, SMEM_SPEC, VMEM_SPEC, VMEM_SPEC, VMEM_SPEC],
                out_specs=VMEM_SPEC,
                compiler_params=limit(16),
                cost_estimate=pl.CostEstimate(flops=2 * macs, bytes_accessed=weight_bytes, transcendentals=0),
                name="forward",
            )(block_rows, block_counts, xs[s], gate_held, up_held)
        )
    others = [[swap(part, "blk", s) for s in range(1, owners)] for part in parts]

    hiddens, grads, dxs = [], [], []
    for s in range(shards):
        hidden, grad, dx = pl.pallas_call(
            functools.partial(backward_kernel, owners, s),
            out_shape=(
                jax.ShapeDtypeStruct((shard_rows, hidden_cols), BF16),
                part_shape,
                jax.ShapeDtypeStruct((shard_rows, width), BF16),
            ),
            in_specs=[SMEM_SPEC] * 3 + [VMEM_SPEC] * (2 + owners) + [ANY_SPEC] * owners,
            out_specs=(VMEM_SPEC, VMEM_SPEC, VMEM_SPEC),
            scratch_shapes=[
                pltpu.VMEM((shard_rows, hidden_cols), BF16),
                pltpu.VMEM((row_blocks, shard_rows, tile), F32),
                pltpu.SemaphoreType.DMA,
            ],
            compiler_params=limit(16),
            cost_estimate=pl.CostEstimate(flops=2 * macs, bytes_accessed=weight_bytes, transcendentals=0),
            name="backward",
        )(meta, block_rows, block_counts, gate_held, up_held, parts[s], *others[s], *cots)
        hiddens.append(hidden)
        grads.append(grad)
        dxs.append(dx)

    arrived = [dxs[0]] + [swap(dxs[s], "tok", s) for s in range(1, shards)]

    gate_out, up_out, hidden_out = pl.pallas_call(
        functools.partial(tile_grads_kernel, shards),
        out_shape=(
            jax.ShapeDtypeStruct(gate_tiles.shape, BF16),
            jax.ShapeDtypeStruct(up_tiles.shape, BF16),
            jax.ShapeDtypeStruct(d_hidden.shape, BF16),
        ),
        in_specs=[SMEM_SPEC] * 3 + [VMEM_SPEC] * (2 * shards) + [ANY_SPEC] * shards,
        out_specs=(ANY_SPEC, ANY_SPEC, ANY_SPEC),
        scratch_shapes=[
            pltpu.VMEM((row_blocks, tile, shards * shard_rows), BF16),
            pltpu.VMEM(gate_tiles.shape, BF16),
            pltpu.VMEM(up_tiles.shape, BF16),
            pltpu.SemaphoreType.DMA((2, cols)),
            pltpu.SemaphoreType.DMA((d_hidden.shape[0] // shard_rows,)),
        ],
        compiler_params=limit(24),
        cost_estimate=pl.CostEstimate(flops=2 * shards * macs, bytes_accessed=weight_bytes, transcendentals=0),
        name="tile_grads",
    )(meta, block_rows, block_counts, *xs, *grads, *hiddens)

    mine = sum(dx.astype(F32) for dx in arrived)
    others_dx = [swap(mine.astype(BF16), "sub", s) for s in range(1, lax.axis_size("sub"))]
    features_grad = (mine + sum(dx.astype(F32) for dx in others_dx)).astype(BF16)
    return (hidden_out, gate_out, up_out, features_grad)


def solution(mesh):
    return jax.shard_map(
        on_device,
        mesh=mesh,
        in_specs=(
            P(("groups", "tok"), "blk"),
            P(("tok", "sub"), "blk", None, None, None),
            P(("tok", "sub"), "blk", None, None, None),
            P(("tok", "sub"), "blk", None),
            P(("tok", "sub"), "blk"),
            P(("groups", "blk"), ("tok", "sub")),
        ),
        out_specs=(
            P(("groups", "blk"), ("tok", "sub")),
            P(("groups", "tok", "sub"), "blk", None, None, None),
            P(("groups", "tok", "sub"), "blk", None, None, None),
            P(("groups", "tok"), "blk"),
        ),
        check_vma=False,
    )
```

```python
import functools

import jax
import jax.numpy as jnp
from jax import lax
from jax.experimental import pallas as pl
from jax.experimental.pallas import tpu as pltpu
from jax.sharding import PartitionSpec as P

F32 = jnp.float32
BF16 = jnp.bfloat16
MIB = 1 << 20
VMEM_SPEC = pl.BlockSpec(memory_space=pltpu.VMEM)
SMEM_SPEC = pl.BlockSpec(memory_space=pltpu.SMEM)
ANY_SPEC = pl.BlockSpec(memory_space=pl.ANY)


def limit(mib):
    return pltpu.CompilerParams(vmem_limit_bytes=mib * MIB)


def lanes(index, width):
    return pl.ds(pl.multiple_of(index * width, width), width)


def chunks_of(shards):
    return [[s] for s in range(min(2, shards))] + [list(range(s, min(s + 2, shards))) for s in range(2, shards, 2)]


def for_columns(cols, body):
    def step(c, carry):
        body(c)
        return carry

    lax.fori_loop(0, cols, step, 0, unroll=cols <= 16)


def weights_of(c, gate_ref, up_ref):
    slots, rows, cols = gate_ref.shape[2:]
    return jnp.concatenate(
        [gate_ref[c, 0].reshape(slots * rows, cols), up_ref[c, 0].reshape(slots * rows, cols)], axis=1
    )


def forward_column(c, rows_ref, counts_ref, xs, gate_ref, up_ref, part_ref):
    slots, tile = gate_ref.shape[2:4]
    count = counts_ref[0, c]
    picked = []
    for k in range(slots):
        where = lanes(rows_ref[k, 0, c], tile)
        block = jnp.concatenate([x[:, where] for x in xs], axis=0)
        picked.append(jnp.where(k < count, block, jnp.zeros_like(block)))
    part_ref[c] = jnp.dot(
        jnp.concatenate(picked, axis=1), weights_of(c, gate_ref, up_ref), preferred_element_type=F32
    ).astype(BF16)


def load_forward_kernel(rows_ref, counts_ref, x_ref, gate_hbm, up_hbm, part_ref, gate_ref, up_ref, sems):
    cols = gate_ref.shape[0]

    def copies(c):
        return (
            pltpu.make_async_copy(gate_hbm.at[c], gate_ref.at[c], sems.at[0, c]),
            pltpu.make_async_copy(up_hbm.at[c], up_ref.at[c], sems.at[1, c]),
        )

    for c in range(cols):
        for copy in copies(c):
            copy.start()

    def body(c):
        for copy in copies(c):
            copy.wait()
        forward_column(c, rows_ref, counts_ref, [x_ref], gate_ref, up_ref, part_ref)

    for_columns(cols, body)


def forward_kernel(members, rows_ref, counts_ref, *refs):
    xs = refs[:members]
    gate_ref, up_ref, *_, part_ref = refs[members:]
    for_columns(
        gate_ref.shape[0], lambda c: forward_column(c, rows_ref, counts_ref, xs, gate_ref, up_ref, part_ref)
    )


def backward_kernel(owners, chunk, meta_ref, rows_ref, counts_ref, gate_ref, up_ref, *refs):
    members = len(chunk)
    parts = refs[:owners]
    cots = refs[owners : 2 * owners]
    grads_ref, hidden_ref = refs[2 * owners + 1 : 2 * owners + 3]
    dxs = refs[2 * owners + 3 : 2 * owners + 3 + members]
    cot_ref, acc_ref, sems = refs[2 * owners + 3 + members :]
    cols, _, slots, tile, _ = gate_ref.shape
    shard_rows = cot_ref.shape[0] // members
    shards_each = cots[0].shape[0] // shard_rows

    def cot_copy(m, cot, first_row):
        return pltpu.make_async_copy(
            cot.at[pl.ds(first_row, shard_rows)], cot_ref.at[pl.ds(m * shard_rows, shard_rows)], sems.at[m]
        )

    for m, step in enumerate(chunk):
        shard = meta_ref[0] ^ step
        source = (shard // shards_each) ^ meta_ref[1]
        first_row = pl.multiple_of((shard % shards_each) * shard_rows, shard_rows)
        for i, cot in enumerate(cots):

            @pl.when(source == i)
            def _(m=m, cot=cot, first_row=first_row):
                cot_copy(m, cot, first_row).start()

    acc_ref[...] = jnp.zeros_like(acc_ref)
    for m in range(members):
        cot_copy(m, cots[0], 0).wait()

    def body(c):
        total = parts[0][c].astype(F32)
        for part in parts[1:]:
            total = total + part[c].astype(F32)
        gate_value, up_value = total[:, :tile], total[:, tile:]
        cotangent = cot_ref[:, lanes(c, tile)].astype(F32)
        sig_gate = jax.nn.sigmoid(gate_value)
        act_gate = gate_value * sig_gate
        hidden_ref[:, lanes(c, tile)] = (act_gate * up_value).astype(BF16)
        gate_grad = (cotangent * up_value * sig_gate * (1.0 + gate_value * (1.0 - sig_gate))).astype(BF16)
        up_grad = (cotangent * act_gate).astype(BF16)
        grads = jnp.concatenate([gate_grad, up_grad], axis=1)
        grads_ref[c] = grads
        back = lax.dot_general(
            grads, weights_of(c, gate_ref, up_ref), (((1,), (1,)), ((), ())), preferred_element_type=F32
        )
        count = counts_ref[0, c]
        rows = [rows_ref[k, 0, c] for k in range(slots)]
        sums = []
        for k in range(slots):
            term = back[:, k * tile : (k + 1) * tile]
            sums.append(acc_ref[rows[k]] + jnp.where(k < count, term, jnp.zeros_like(term)))
        for k in range(slots):
            acc_ref[rows[k]] = sums[k]

    for_columns(cols, body)
    for r in range(acc_ref.shape[0]):
        block = acc_ref[r].astype(BF16)
        for m in range(members):
            dxs[m][:, r * tile : (r + 1) * tile] = block[m * shard_rows : (m + 1) * shard_rows]


def tile_grads_kernel(shards, chunks, meta_ref, rows_ref, counts_ref, *refs):
    xs = refs[:shards]
    grads = refs[shards : shards + len(chunks)]
    hiddens = refs[shards + len(chunks) : shards + 2 * len(chunks)]
    gate_hbm, up_hbm, hidden_hbm, turned_ref, gate_ref, up_ref, sems, hidden_sems = refs[
        shards + 2 * len(chunks) :
    ]
    cols, _, slots, tile, _ = gate_ref.shape
    shard_rows = xs[0].shape[0]
    shards_each = hidden_hbm.shape[0] // shard_rows

    def hidden_copy(i, n, m):
        return pltpu.make_async_copy(
            hiddens[n].at[pl.ds(m * shard_rows, shard_rows)],
            hidden_hbm.at[pl.ds(i * shard_rows, shard_rows)],
            hidden_sems.at[i],
        )

    for i in range(shards_each):
        step = (meta_ref[1] * shards_each + i) ^ meta_ref[0]
        for n, chunk in enumerate(chunks):
            for m, j in enumerate(chunk):

                @pl.when(step == j)
                def _(i=i, n=n, m=m):
                    hidden_copy(i, n, m).start()

    for r in range(turned_ref.shape[0]):
        block = jnp.concatenate([x[:, r * tile : (r + 1) * tile] for x in xs], axis=0)
        turned_ref[r] = block.T

    def copies(c):
        return (
            pltpu.make_async_copy(gate_ref.at[c], gate_hbm.at[c], sems.at[0, c]),
            pltpu.make_async_copy(up_ref.at[c], up_hbm.at[c], sems.at[1, c]),
        )

    def body(c):
        picked = jnp.concatenate([turned_ref[rows_ref[k, 0, c]] for k in range(slots)], axis=0)
        grad = jnp.concatenate([g[c] for g in grads], axis=0)
        found = jnp.dot(picked, grad, preferred_element_type=F32)
        count = counts_ref[0, c]
        for k in range(slots):
            term = found[k * tile : (k + 1) * tile]
            term = jnp.where(k < count, term, jnp.zeros_like(term)).astype(BF16)
            gate_ref[c, 0, k] = term[:, :tile]
            up_ref[c, 0, k] = term[:, tile:]
        for copy in copies(c):
            copy.start()

    for_columns(cols, body)
    for c in range(cols):
        for copy in copies(c):
            copy.wait()
    for i in range(shards_each):
        hidden_copy(i, 0, 0).wait()


def swap(x, axis, step):
    return lax.ppermute(x, axis, [(i, i ^ step) for i in range(lax.axis_size(axis))])


def on_device(features_in, gate_tiles, up_tiles, block_rows, block_counts, d_hidden):
    shards, owners = lax.axis_size("tok"), lax.axis_size("blk")
    chunks = chunks_of(shards)
    cols, _, slots, tile, _ = gate_tiles.shape
    shard_rows, width = features_in.shape
    row_blocks = width // tile
    meta = jnp.stack([lax.axis_index("tok"), lax.axis_index("blk")]).astype(jnp.int32)
    lists = (jnp.transpose(block_rows, (2, 1, 0)), jnp.transpose(block_counts, (1, 0)))

    xs = [features_in] + [swap(features_in, "tok", s) for s in range(1, shards)]
    cots = [d_hidden] + [swap(d_hidden, "blk", s) for s in range(1, owners)]

    macs = shard_rows * cols * slots * tile * tile * 2
    weight_bytes = 2 * cols * slots * tile * tile * 2

    def part_shape(chunk):
        return jax.ShapeDtypeStruct((cols, len(chunk) * shard_rows, 2 * tile), BF16)

    def cost(members):
        return pl.CostEstimate(flops=2 * members * macs, bytes_accessed=weight_bytes, transcendentals=0)

    part, gate_held, up_held = pl.pallas_call(
        load_forward_kernel,
        out_shape=(
            part_shape(chunks[0]),
            pltpu.VMEM(gate_tiles.shape, BF16),
            pltpu.VMEM(up_tiles.shape, BF16),
        ),
        in_specs=[SMEM_SPEC, SMEM_SPEC, VMEM_SPEC, ANY_SPEC, ANY_SPEC],
        out_specs=(VMEM_SPEC, VMEM_SPEC, VMEM_SPEC),
        scratch_shapes=[pltpu.SemaphoreType.DMA((2, cols))],
        compiler_params=limit(8),
        cost_estimate=cost(1),
        name="load_forward",
    )(
        *lists,
        features_in,
        pltpu.with_memory_space_constraint(gate_tiles, pltpu.HBM),
        pltpu.with_memory_space_constraint(up_tiles, pltpu.HBM),
    )
    def to_owners(part):
        return [swap(part, "blk", s) for s in range(1, owners)]

    parts, others = [part], [to_owners(part)]
    for n, chunk in enumerate(chunks[1:]):
        before = [cots[-1]] if n == 0 else [parts[-1], others[n - 1][-1]]
        parts.append(
            pl.pallas_call(
                functools.partial(forward_kernel, len(chunk)),
                out_shape=part_shape(chunk),
                in_specs=[SMEM_SPEC] * 2 + [VMEM_SPEC] * (len(chunk) + 2) + [ANY_SPEC] * len(before),
                out_specs=VMEM_SPEC,
                compiler_params=limit(8),
                cost_estimate=cost(len(chunk)),
                name="forward",
            )(*lists, *[xs[s] for s in chunk], gate_held, up_held, *before)
        )
        others.append(to_owners(parts[-1]))

    hiddens, grads, dxs = [], [], []
    for n, chunk in enumerate(chunks):
        rows_here = len(chunk) * shard_rows
        grad, hidden, *dx = pl.pallas_call(
            functools.partial(backward_kernel, owners, chunk),
            out_shape=(
                part_shape(chunk),
                jax.ShapeDtypeStruct((rows_here, cols * tile), BF16),
                *[jax.ShapeDtypeStruct((shard_rows, width), BF16) for _ in chunk],
            ),
            in_specs=[SMEM_SPEC] * 3 + [VMEM_SPEC] * (2 + owners) + [ANY_SPEC] * (owners + 1),
            out_specs=(VMEM_SPEC,) * (2 + len(chunk)),
            scratch_shapes=[
                pltpu.VMEM((rows_here, cols * tile), BF16),
                pltpu.VMEM((row_blocks, rows_here, tile), F32),
                pltpu.SemaphoreType.DMA((len(chunk),)),
            ],
            compiler_params=limit(8),
            cost_estimate=cost(len(chunk)),
            name="backward",
        )(meta, *lists, gate_held, up_held, parts[n], *others[n], *cots, grads[-1] if grads else part)
        hiddens.append(hidden)
        grads.append(grad)
        dxs.extend(dx)

    arrived = [dxs[0]] + [swap(dxs[s], "tok", s) for s in range(1, shards)]

    gate_out, up_out, hidden_out = pl.pallas_call(
        functools.partial(tile_grads_kernel, shards, chunks),
        out_shape=(
            jax.ShapeDtypeStruct(gate_tiles.shape, BF16),
            jax.ShapeDtypeStruct(up_tiles.shape, BF16),
            jax.ShapeDtypeStruct(d_hidden.shape, BF16),
        ),
        in_specs=[SMEM_SPEC] * 3 + [VMEM_SPEC] * (shards + len(chunks)) + [ANY_SPEC] * len(chunks),
        out_specs=(ANY_SPEC, ANY_SPEC, ANY_SPEC),
        scratch_shapes=[
            pltpu.VMEM((row_blocks, tile, shards * shard_rows), BF16),
            pltpu.VMEM(gate_tiles.shape, BF16),
            pltpu.VMEM(up_tiles.shape, BF16),
            pltpu.SemaphoreType.DMA((2, cols)),
            pltpu.SemaphoreType.DMA((d_hidden.shape[0] // shard_rows,)),
        ],
        compiler_params=limit(20),
        cost_estimate=cost(shards),
        name="tile_grads",
    )(meta, *lists, *xs, *grads, *hiddens)

    mine = sum(dx.astype(F32) for dx in arrived)
    others_dx = [swap(mine.astype(BF16), "sub", s) for s in range(1, lax.axis_size("sub"))]
    features_grad = (mine + sum(dx.astype(F32) for dx in others_dx)).astype(BF16)
    return (hidden_out, gate_out, up_out, features_grad)


def solution(mesh):
    return jax.shard_map(
        on_device,
        mesh=mesh,
        in_specs=(
            P(("groups", "tok"), "blk"),
            P(("tok", "sub"), "blk", None, None, None),
            P(("tok", "sub"), "blk", None, None, None),
            P(("tok", "sub"), "blk", None),
            P(("tok", "sub"), "blk"),
            P(("groups", "blk"), ("tok", "sub")),
        ),
        out_specs=(
            P(("groups", "blk"), ("tok", "sub")),
            P(("groups", "tok", "sub"), "blk", None, None, None),
            P(("groups", "tok", "sub"), "blk", None, None, None),
            P(("groups", "tok"), "blk"),
        ),
        check_vma=False,
    )
```

```python
import functools

import jax
import jax.numpy as jnp
from jax import lax
from jax.experimental import pallas as pl
from jax.experimental.pallas import tpu as pltpu
from jax.sharding import PartitionSpec as P

F32 = jnp.float32
BF16 = jnp.bfloat16
MIB = 1 << 20
VMEM_SPEC = pl.BlockSpec(memory_space=pltpu.VMEM)
SMEM_SPEC = pl.BlockSpec(memory_space=pltpu.SMEM)
ANY_SPEC = pl.BlockSpec(memory_space=pl.ANY)


def limit(mib):
    return pltpu.CompilerParams(vmem_limit_bytes=mib * MIB)


def lanes(index, width):
    return pl.ds(pl.multiple_of(index * width, width), width)


def weights_of(c, gate_ref, up_ref):
    slots, rows, cols = gate_ref.shape[2:]
    return jnp.concatenate(
        [gate_ref[c, 0].reshape(slots * rows, cols), up_ref[c, 0].reshape(slots * rows, cols)], axis=1
    )


def keep(k, count, block):
    return jnp.where(k < count, block, jnp.zeros_like(block))


def forward_column(c, first, lists, xs, gate_ref, up_ref):
    rows_ref, counts_ref = lists
    slots, tile = gate_ref.shape[2:4]
    count = counts_ref[0, first + c]
    picked = []
    for k in range(slots):
        where = lanes(rows_ref[k, 0, first + c], tile)
        picked.append(keep(k, count, jnp.concatenate([x[:, where] for x in xs], axis=0)))
    return jnp.dot(
        jnp.concatenate(picked, axis=1), weights_of(c, gate_ref, up_ref), preferred_element_type=F32
    ).astype(BF16)


def forward_kernel(members, first, rows_ref, counts_ref, *refs):
    xs = refs[:members]
    gate_ref, up_ref = refs[members : members + 2]
    part_ref = refs[-1]
    for c in range(gate_ref.shape[0]):
        part_ref[c] = forward_column(c, first, (rows_ref, counts_ref), xs, gate_ref, up_ref)


def forward_own_kernel(x_hbm, rows_hbm, counts_hbm, gate_hbm, up_hbm, part_ref, gate_ref, up_ref, *scratch):
    x_ref, rows_ref, counts_ref, sems, small_sems = scratch
    cols = gate_ref.shape[0]

    def copies(c):
        return (
            pltpu.make_async_copy(gate_hbm.at[c], gate_ref.at[c], sems.at[0, c]),
            pltpu.make_async_copy(up_hbm.at[c], up_ref.at[c], sems.at[1, c]),
        )

    small = [
        pltpu.make_async_copy(source, target, small_sems.at[i])
        for i, (source, target) in enumerate(((rows_hbm, rows_ref), (counts_hbm, counts_ref), (x_hbm, x_ref)))
    ]
    for copy in small:
        copy.start()
    for c in range(cols):
        for copy in copies(c):
            copy.start()
    for copy in small:
        copy.wait()
    for c in range(cols):
        for copy in copies(c):
            copy.wait()
        part_ref[c] = forward_column(c, 0, (rows_ref, counts_ref), [x_ref], gate_ref, up_ref)


def load_forward_kernel(members, groups, first, turn, rows_ref, counts_ref, *refs):
    xs = refs[:members]
    gate_hbm, up_hbm = refs[members : members + 2]
    outs = refs[-(len(groups) + 3 + turn) :]
    parts, gate_ref, up_ref, sems = outs[: len(groups)], outs[-3 - turn], outs[-2 - turn], outs[-1]
    cols, _, _, tile, _ = gate_ref.shape

    def copies(c):
        return (
            pltpu.make_async_copy(gate_hbm.at[first + c], gate_ref.at[c], sems.at[0, c]),
            pltpu.make_async_copy(up_hbm.at[first + c], up_ref.at[c], sems.at[1, c]),
        )

    for c in range(cols):
        for copy in copies(c):
            copy.start()
    if turn:
        turned_ref = outs[-2]
        for r in range(turned_ref.shape[0]):
            turned_ref[r] = jnp.concatenate([x[:, r * tile : (r + 1) * tile] for x in xs], axis=0).T
    for c in range(cols):
        for copy in copies(c):
            copy.wait()
        part = forward_column(c, first, (rows_ref, counts_ref), xs, gate_ref, up_ref)
        for (start, stop), part_ref in zip(groups, parts):
            part_ref[c] = part[start:stop]


def shard_of(member, meta_ref):
    if member < 2:
        return meta_ref[0] ^ member
    return meta_ref[0] ^ ((member & ~1) + ((member & 1) ^ meta_ref[2]))


def start_cots(members, first, meta_ref, cots, cot_ref, sems):
    count = len(members)
    shard_rows, width = cot_ref.shape[0] // count, cot_ref.shape[1]
    shards_each = cots[0].shape[0] // shard_rows

    def copy(i, cot, first_row):
        return pltpu.make_async_copy(
            cot.at[pl.ds(first_row, shard_rows), pl.ds(first, width)],
            cot_ref.at[pl.ds(i * shard_rows, shard_rows)],
            sems.at[i],
        )

    for i, member in enumerate(members):
        shard = shard_of(member, meta_ref)
        source = (shard // shards_each) ^ meta_ref[1]
        first_row = pl.multiple_of((shard % shards_each) * shard_rows, shard_rows)
        for j, cot in enumerate(cots):

            @pl.when(source == j)
            def _(i=i, cot=cot, first_row=first_row):
                copy(i, cot, first_row).start()

    return [copy(i, cots[0], 0) for i in range(count)]


def nonlinear(total, cotangent):
    tile = total.shape[1] // 2
    gate_value, up_value = total[:, :tile], total[:, tile:]
    sig_gate = jax.nn.sigmoid(gate_value)
    act_gate = gate_value * sig_gate
    hidden = (act_gate * up_value).astype(BF16)
    gate_grad = (cotangent * up_value * sig_gate * (1.0 + gate_value * (1.0 - sig_gate))).astype(BF16)
    up_grad = (cotangent * act_gate).astype(BF16)
    return hidden, jnp.concatenate([gate_grad, up_grad], axis=1)


def total_of(c, parts):
    total = parts[0][c].astype(F32)
    for part in parts[1:]:
        total = total + part[c].astype(F32)
    return total


def back_terms(c, grads, gate_ref, up_ref):
    return lax.dot_general(
        grads, weights_of(c, gate_ref, up_ref), (((1,), (1,)), ((), ())), preferred_element_type=F32
    )


def add_back(c, lists, back, accs, slots, tile):
    rows_ref, counts_ref = lists
    rows = [rows_ref[k, 0, c] for k in range(slots)]
    start = 0
    for acc in accs:
        stop = start + acc.shape[1]
        sums = [
            acc[rows[k]] + keep(k, counts_ref[0, c], back[start:stop, k * tile : (k + 1) * tile])
            for k in range(slots)
        ]
        for k in range(slots):
            acc[rows[k]] = sums[k]
        start = stop


def tile_grads(c, first, lists, turned_ref, grads, gate_ref, up_ref):
    rows_ref, counts_ref = lists
    slots, tile = gate_ref.shape[2:4]
    picked = jnp.concatenate([turned_ref[rows_ref[k, 0, first + c]] for k in range(slots)], axis=0)
    found = jnp.dot(picked, grads, preferred_element_type=F32)
    for k in range(slots):
        term = keep(k, counts_ref[0, first + c], found[k * tile : (k + 1) * tile]).astype(BF16)
        gate_ref[c, 0, k] = term[:, :tile]
        up_ref[c, 0, k] = term[:, tile:]


def start_hidden(members, first, meta_ref, source_of, hidden_hbm, shard_rows, sems):
    width = source_of(0).shape[1]
    shards_each = hidden_hbm.shape[0] // shard_rows

    def copy(i, member):
        return pltpu.make_async_copy(
            source_of(member), hidden_hbm.at[pl.ds(i * shard_rows, shard_rows), pl.ds(first, width)], sems.at[i]
        )

    for i in range(shards_each):
        wanted = meta_ref[1] * shards_each + i
        for member in members:

            @pl.when(shard_of(member, meta_ref) == wanted)
            def _(i=i, member=member):
                copy(i, member).start()

    return [copy(i, 0) for i in range(shards_each)]


def first_half_kernel(members, owners, meta_ref, rows_ref, counts_ref, gate_w, up_w, turned_ref, *refs):
    near, rest, cots = refs[:owners], refs[owners : 2 * owners], refs[2 * owners : 3 * owners]
    (gate_hbm, up_hbm, hidden_hbm, acc_near, acc_far, cot_ref, hidden_ref, gate_ref, up_ref, sems, cot_sems, hidden_sems) = refs[
        -12:
    ]
    cols, _, slots, tile, _ = gate_w.shape
    shard_rows = cot_ref.shape[0] // members
    lists = (rows_ref, counts_ref)
    waits = start_cots(range(members), 0, meta_ref, cots, cot_ref, cot_sems)
    acc_near[...] = jnp.zeros_like(acc_near)
    acc_far[...] = jnp.zeros_like(acc_far)
    for wait in waits:
        wait.wait()
    copies = []
    for c in range(cols):
        total = jnp.concatenate([total_of(c, near), total_of(c, rest)], axis=0)
        where = slice(c * tile, (c + 1) * tile)
        hidden, grads = nonlinear(total, cot_ref[:, where].astype(F32))
        hidden_ref[:, where] = hidden
        tile_grads(c, 0, lists, turned_ref, grads, gate_ref, up_ref)
        copies.append(pltpu.make_async_copy(gate_ref.at[c], gate_hbm.at[c], sems.at[0, c]))
        copies.append(pltpu.make_async_copy(up_ref.at[c], up_hbm.at[c], sems.at[1, c]))
        copies[-2].start()
        copies[-1].start()
        add_back(c, lists, back_terms(c, grads, gate_w, up_w), (acc_near, acc_far), slots, tile)
    waits = start_hidden(
        range(members),
        0,
        meta_ref,
        lambda m: hidden_ref.at[pl.ds(m * shard_rows, shard_rows)],
        hidden_hbm,
        shard_rows,
        hidden_sems,
    )
    for wait in copies + waits:
        wait.wait()


def second_half_kernel(members, owners, first, meta_ref, rows_ref, counts_ref, gate_w, up_w, acc_in, *refs):
    parts, cots = refs[:owners], refs[owners : 2 * owners]
    outs = refs[-(2 + len(members) + 3) :]
    grads_ref, hidden_ref = outs[:2]
    dxs = outs[2 : 2 + len(members)]
    cot_ref, acc_ref, cot_sems = outs[-3:]
    cols, _, slots, tile, _ = gate_w.shape
    shard_rows = cot_ref.shape[0] // len(members)
    waits = start_cots(members, first * tile, meta_ref, cots, cot_ref, cot_sems)
    acc_ref[...] = acc_in[...]
    for wait in waits:
        wait.wait()
    for c in range(cols):
        where = slice(c * tile, (c + 1) * tile)
        hidden, grads = nonlinear(total_of(c, parts), cot_ref[:, where].astype(F32))
        hidden_ref[:, where] = hidden
        grads_ref[c] = grads
        add_back(first + c, (rows_ref, counts_ref), back_terms(c, grads, gate_w, up_w), (acc_ref,), slots, tile)
    for r in range(acc_ref.shape[0]):
        block = acc_ref[r].astype(BF16)
        for m, dx in enumerate(dxs):
            dx[:, r * tile : (r + 1) * tile] = block[m * shard_rows : (m + 1) * shard_rows]


def last_grads_kernel(members, first, start, with_hidden, meta_ref, rows_ref, counts_ref, turned_ref, *refs):
    near_grads, far_grads, near_hidden, far_hidden = refs[:4]
    gate_hbm, up_hbm, hidden_hbm, token_ref, gate_ref, up_ref, sems, hidden_sems = refs[-8:]
    cols, _, _, tile, _ = gate_ref.shape
    shard_rows = near_hidden.shape[0] // 2
    token_ref[...] = jnp.zeros_like(token_ref)

    def hidden_of(m):
        if m < 2:
            return near_hidden.at[pl.ds(m * shard_rows, shard_rows)]
        return far_hidden.at[pl.ds((m - 2) * shard_rows, shard_rows)]

    waits = []
    if with_hidden:
        waits = start_hidden(
            range(members), first * tile, meta_ref, hidden_of, hidden_hbm, shard_rows, hidden_sems
        )
    for c in range(cols):
        grads = jnp.concatenate([near_grads[start + c], far_grads[start + c]], axis=0)
        at = first + start + c
        tile_grads(c, first + start, (rows_ref, counts_ref), turned_ref, grads, gate_ref, up_ref)
        waits.append(pltpu.make_async_copy(gate_ref.at[c], gate_hbm.at[at], sems.at[0, c]))
        waits.append(pltpu.make_async_copy(up_ref.at[c], up_hbm.at[at], sems.at[1, c]))
        waits[-2].start()
        waits[-1].start()
    for wait in waits:
        wait.wait()


def sum_kernel(count, *refs):
    total = sum(ref[...].astype(F32) for ref in refs[:count])
    refs[-2][...] = total
    refs[-1][...] = total.astype(BF16)


def swap(x, axis, step):
    return lax.ppermute(x, axis, [(i, i ^ step) for i in range(lax.axis_size(axis))])


def swap_far(x, base):
    shards, cores = lax.axis_size("tok"), lax.axis_size("sub")
    pairs = [(t * cores + s, (t ^ (base + s)) * cores + s) for t in range(shards) for s in range(cores)]
    return lax.ppermute(x, ("tok", "sub"), pairs)


def on_device(features_in, gate_tiles, up_tiles, block_rows, block_counts, d_hidden):
    shards, owners = lax.axis_size("tok"), lax.axis_size("blk")
    cols, _, slots, tile, _ = gate_tiles.shape
    shard_rows, width = features_in.shape
    row_blocks = width // tile
    row_total = shards * shard_rows
    near_rows = 2 * shard_rows
    half = cols // 2
    bases = range(2, shards, 2)
    meta = jnp.stack([lax.axis_index("tok"), lax.axis_index("blk"), lax.axis_index("sub")]).astype(jnp.int32)
    lists = (jnp.transpose(block_rows, (2, 1, 0)), jnp.transpose(block_counts, (1, 0)))

    def held(weights):
        return [pltpu.with_memory_space_constraint(w, pltpu.VMEM) for w in weights]

    def shape(*dims, dtype=BF16):
        return jax.ShapeDtypeStruct(dims, dtype)

    def cost(tokens, columns, products, tile_bytes):
        tiles = columns * slots
        return pl.CostEstimate(
            flops=4 * tokens * tiles * tile * tile * products,
            bytes_accessed=4 * tiles * tile * tile * tile_bytes,
            transcendentals=0,
        )

    def to_owners(part):
        return [part] + [swap(part, "blk", s) for s in range(1, owners)]

    fars = [swap_far(features_in, base) for base in bases]
    xs = [features_in, swap(features_in, "tok", 1)]
    cots = [d_hidden] + [swap(d_hidden, "blk", s) for s in range(1, owners)]

    def tile_shape(columns):
        return pltpu.VMEM((columns, 1, slots, tile, tile), BF16)

    def from_hbm(*arrays):
        return [pltpu.with_memory_space_constraint(array, pltpu.HBM) for array in arrays]

    near_a, *weights_a = pl.pallas_call(
        forward_own_kernel,
        out_shape=(shape(half, shard_rows, 2 * tile), tile_shape(half), tile_shape(half)),
        in_specs=[ANY_SPEC] * 5,
        out_specs=(VMEM_SPEC,) * 3,
        scratch_shapes=[
            pltpu.VMEM((shard_rows, width), BF16),
            pltpu.SMEM(lists[0].shape, jnp.int32),
            pltpu.SMEM(lists[1].shape, jnp.int32),
            pltpu.SemaphoreType.DMA((2, half)),
            pltpu.SemaphoreType.DMA((3,)),
        ],
        compiler_params=limit(8),
        cost_estimate=cost(shard_rows, half, 1, 1),
        name="forward_own_a",
    )(*from_hbm(features_in, *lists, gate_tiles, up_tiles))
    near_a = to_owners(near_a)

    for far in fars:
        xs += [far, swap(far, "sub", 1)]

    rest_a = pl.pallas_call(
        functools.partial(forward_kernel, shards - 1, 0),
        out_shape=shape(half, row_total - shard_rows, 2 * tile),
        in_specs=[SMEM_SPEC] * 2 + [VMEM_SPEC] * (shards + 1) + [ANY_SPEC] * 2,
        out_specs=VMEM_SPEC,
        compiler_params=limit(8),
        cost_estimate=cost(row_total, half, 1, 1),
        name="forward_rest_a",
    )(*lists, *xs[1:], *held(weights_a), cots[-1], near_a[-1])
    rest_a = to_owners(rest_a)

    rest = cols - half
    far_b, near_b, gate_b, up_b, turned = pl.pallas_call(
        functools.partial(load_forward_kernel, shards, ((near_rows, row_total), (0, near_rows)), half, 1),
        out_shape=(
            shape(rest, row_total - near_rows, 2 * tile),
            shape(rest, near_rows, 2 * tile),
            tile_shape(rest),
            tile_shape(rest),
            pltpu.VMEM((row_blocks, tile, row_total), BF16),
        ),
        in_specs=[SMEM_SPEC] * 2 + [VMEM_SPEC] * shards + [ANY_SPEC] * 3,
        out_specs=(VMEM_SPEC,) * 5,
        scratch_shapes=[pltpu.SemaphoreType.DMA((2, rest))],
        compiler_params=limit(8),
        cost_estimate=cost(row_total, rest, 1, 1),
        name="forward_b",
    )(*lists, *xs, *from_hbm(gate_tiles, up_tiles), rest_a[0])
    weights_b = [gate_b, up_b]
    far_b, near_b = to_owners(far_b), to_owners(near_b)

    out_tiles = shape(*gate_tiles.shape)
    gate_out, up_out, hidden_out, acc_near, acc_far = pl.pallas_call(
        functools.partial(first_half_kernel, shards, owners),
        out_shape=(
            out_tiles,
            out_tiles,
            shape(*d_hidden.shape),
            shape(row_blocks, near_rows, tile, dtype=F32),
            shape(row_blocks, row_total - near_rows, tile, dtype=F32),
        ),
        in_specs=[SMEM_SPEC] * 3 + [VMEM_SPEC] * (3 + 2 * owners) + [ANY_SPEC] * (owners + 2),
        out_specs=(ANY_SPEC,) * 3 + (VMEM_SPEC,) * 2,
        scratch_shapes=[
            pltpu.VMEM((row_total, half * tile), BF16),
            pltpu.VMEM((row_total, half * tile), BF16),
            pltpu.VMEM((half, 1, slots, tile, tile), BF16),
            pltpu.VMEM((half, 1, slots, tile, tile), BF16),
            pltpu.SemaphoreType.DMA((2, half)),
            pltpu.SemaphoreType.DMA((shards,)),
            pltpu.SemaphoreType.DMA((d_hidden.shape[0] // shard_rows,)),
        ],
        compiler_params=limit(16),
        cost_estimate=cost(row_total, half, 2, 1),
        name="first_half",
    )(meta, *lists, *held(weights_a), *held([turned]), *near_a, *rest_a, *cots, far_b[0], near_b[0])

    def second_half(members, acc, parts, after):
        rows_here = len(members) * shard_rows
        return pl.pallas_call(
            functools.partial(second_half_kernel, members, owners, half),
            out_shape=(
                shape(rest, rows_here, 2 * tile),
                shape(rows_here, rest * tile),
                *[shape(shard_rows, width) for _ in members],
            ),
            in_specs=[SMEM_SPEC] * 3 + [VMEM_SPEC] * (3 + owners) + [ANY_SPEC] * (owners + 1),
            out_specs=(VMEM_SPEC,) * (2 + len(members)),
            scratch_shapes=[
                pltpu.VMEM((rows_here, rest * tile), BF16),
                pltpu.VMEM((row_blocks, rows_here, tile), F32),
                pltpu.SemaphoreType.DMA((len(members),)),
            ],
            compiler_params=limit(8),
            cost_estimate=cost(rows_here, rest, 1, 1),
            name="second_half",
        )(meta, *lists, *held(weights_b), acc, *parts, *cots, after)

    far_grads, far_hidden, *far_dxs = second_half(range(2, shards), acc_far, far_b, acc_near)
    both_cores = []
    for mine, others in zip(far_dxs[::2], far_dxs[1::2]):
        other = swap(others, "sub", 1)
        both_cores.append((mine.astype(F32) + other.astype(F32)).astype(BF16))
    back_far = [swap_far(total, base) for total, base in zip(both_cores, bases)]

    near_grads, near_hidden, own_dx, next_dx = second_half(range(2), acc_near, near_b, far_grads)
    back_next = swap(next_dx, "tok", 1)

    def last_grads(start, stop, with_hidden, outs):
        count = stop - start
        return pl.pallas_call(
            functools.partial(last_grads_kernel, shards, half, start, with_hidden),
            out_shape=(out_tiles, out_tiles, shape(*d_hidden.shape), shape(8, tile, dtype=F32)),
            in_specs=[SMEM_SPEC] * 3 + [VMEM_SPEC] * 3 + [ANY_SPEC] * 5,
            out_specs=(ANY_SPEC,) * 3 + (VMEM_SPEC,),
            scratch_shapes=[
                pltpu.VMEM((count, 1, slots, tile, tile), BF16),
                pltpu.VMEM((count, 1, slots, tile, tile), BF16),
                pltpu.SemaphoreType.DMA((2, count)),
                pltpu.SemaphoreType.DMA((d_hidden.shape[0] // shard_rows,)),
            ],
            input_output_aliases={8: 0, 9: 1, 10: 2},
            compiler_params=limit(12),
            cost_estimate=cost(row_total, count, 1, 1),
            name="last_grads",
        )(meta, *lists, *held([turned]), near_grads, far_grads, near_hidden, far_hidden, *outs)

    middle = max(1, rest // 2)
    *outs, token = last_grads(0, middle, True, (gate_out, up_out, hidden_out))
    arrived = [own_dx, back_next, *back_far]
    mine, mine_sent = pl.pallas_call(
        functools.partial(sum_kernel, len(arrived)),
        out_shape=(shape(shard_rows, width, dtype=F32), shape(shard_rows, width)),
        in_specs=[VMEM_SPEC] * len(arrived) + [ANY_SPEC],
        out_specs=(VMEM_SPEC,) * 2,
        compiler_params=limit(8),
        name="sum_shards",
    )(*arrived, token)
    if middle < rest:
        *outs, _ = last_grads(middle, rest, False, outs)
    gate_out, up_out, hidden_out = outs
    features_grad = (mine + swap(mine_sent, "sub", 1).astype(F32)).astype(BF16)
    return (hidden_out, gate_out, up_out, features_grad)


def solution(mesh):
    return jax.shard_map(
        on_device,
        mesh=mesh,
        in_specs=(
            P(("groups", "tok"), "blk"),
            P(("tok", "sub"), "blk", None, None, None),
            P(("tok", "sub"), "blk", None, None, None),
            P(("tok", "sub"), "blk", None),
            P(("tok", "sub"), "blk"),
            P(("groups", "blk"), ("tok", "sub")),
        ),
        out_specs=(
            P(("groups", "blk"), ("tok", "sub")),
            P(("groups", "tok", "sub"), "blk", None, None, None),
            P(("groups", "tok", "sub"), "blk", None, None, None),
            P(("groups", "tok"), "blk"),
        ),
        check_vma=False,
    )
```

```python
import functools

import jax
import jax.numpy as jnp
from jax import lax
from jax.experimental import pallas as pl
from jax.experimental.pallas import tpu as pltpu
from jax.sharding import PartitionSpec as P

F32 = jnp.float32
BF16 = jnp.bfloat16
MIB = 1 << 20
WINDOW = 3
VMEM_SPEC = pl.BlockSpec(memory_space=pltpu.VMEM)
SMEM_SPEC = pl.BlockSpec(memory_space=pltpu.SMEM)
ANY_SPEC = pl.BlockSpec(memory_space=pl.ANY)


def limit(mib):
    return pltpu.CompilerParams(vmem_limit_bytes=mib * MIB)


def lanes(index, width):
    return pl.ds(pl.multiple_of(index * width, width), width)


def weights_of(c, gate_ref, up_ref):
    slots, rows, cols = gate_ref.shape[2:]
    return jnp.concatenate(
        [gate_ref[c, 0].reshape(slots * rows, cols), up_ref[c, 0].reshape(slots * rows, cols)], axis=1
    )


def keep(k, count, block):
    return jnp.where(k < count, block, jnp.zeros_like(block))


def forward_column(c, first, lists, xs, gate_ref, up_ref):
    rows_ref, counts_ref = lists
    slots, tile = gate_ref.shape[2:4]
    count = counts_ref[0, first + c]
    picked = []
    for k in range(slots):
        where = lanes(rows_ref[k, 0, first + c], tile)
        picked.append(keep(k, count, jnp.concatenate([x[:, where] for x in xs], axis=0)))
    return jnp.dot(
        jnp.concatenate(picked, axis=1), weights_of(c, gate_ref, up_ref), preferred_element_type=F32
    ).astype(BF16)


def forward_kernel(members, first, rows_ref, counts_ref, *refs):
    xs = refs[:members]
    gate_ref, up_ref = refs[members : members + 2]
    part_ref = refs[-1]
    for c in range(gate_ref.shape[0]):
        part_ref[c] = forward_column(c, first, (rows_ref, counts_ref), xs, gate_ref, up_ref)


def windowed(copies, cols):
    for c in range(min(WINDOW, cols)):
        for copy in copies(c):
            copy.start()

    def arrive(c):
        for copy in copies(c):
            copy.wait()
        if c + WINDOW < cols:
            for copy in copies(c + WINDOW):
                copy.start()

    return arrive


def forward_own_kernel(x_hbm, rows_hbm, counts_hbm, gate_hbm, up_hbm, part_ref, gate_ref, up_ref, *scratch):
    x_ref, rows_ref, counts_ref, sems, small_sems = scratch
    cols = gate_ref.shape[0]

    def copies(c):
        return (
            pltpu.make_async_copy(gate_hbm.at[c], gate_ref.at[c], sems.at[0, c]),
            pltpu.make_async_copy(up_hbm.at[c], up_ref.at[c], sems.at[1, c]),
        )

    small = [
        pltpu.make_async_copy(source, target, small_sems.at[i])
        for i, (source, target) in enumerate(((rows_hbm, rows_ref), (counts_hbm, counts_ref), (x_hbm, x_ref)))
    ]
    for copy in small:
        copy.start()
    arrive = windowed(copies, cols)
    for copy in small:
        copy.wait()
    for c in range(cols):
        arrive(c)
        part_ref[c] = forward_column(c, 0, (rows_ref, counts_ref), [x_ref], gate_ref, up_ref)


def load_forward_kernel(members, groups, first, turn, rows_ref, counts_ref, *refs):
    xs = refs[:members]
    gate_hbm, up_hbm = refs[members : members + 2]
    outs = refs[-(len(groups) + 3 + turn) :]
    parts, gate_ref, up_ref, sems = outs[: len(groups)], outs[-3 - turn], outs[-2 - turn], outs[-1]
    cols, _, _, tile, _ = gate_ref.shape

    def copies(c):
        return (
            pltpu.make_async_copy(gate_hbm.at[first + c], gate_ref.at[c], sems.at[0, c]),
            pltpu.make_async_copy(up_hbm.at[first + c], up_ref.at[c], sems.at[1, c]),
        )

    arrive = windowed(copies, cols)
    if turn:
        turned_ref = outs[-2]
        for r in range(turned_ref.shape[0]):
            turned_ref[r] = jnp.concatenate([x[:, r * tile : (r + 1) * tile] for x in xs], axis=0).T
    for c in range(cols):
        arrive(c)
        part = forward_column(c, first, (rows_ref, counts_ref), xs, gate_ref, up_ref)
        for (start, stop), part_ref in zip(groups, parts):
            part_ref[c] = part[start:stop]


def shard_of(member, meta_ref):
    if member < 2:
        return meta_ref[0] ^ member
    return meta_ref[0] ^ ((member & ~1) + ((member & 1) ^ meta_ref[2]))


def start_cots(members, first, meta_ref, cots, cot_ref, sems):
    count = len(members)
    shard_rows, width = cot_ref.shape[0] // count, cot_ref.shape[1]
    shards_each = cots[0].shape[0] // shard_rows

    def copy(i, cot, first_row):
        return pltpu.make_async_copy(
            cot.at[pl.ds(first_row, shard_rows), pl.ds(first, width)],
            cot_ref.at[pl.ds(i * shard_rows, shard_rows)],
            sems.at[i],
        )

    for i, member in enumerate(members):
        shard = shard_of(member, meta_ref)
        source = (shard // shards_each) ^ meta_ref[1]
        first_row = pl.multiple_of((shard % shards_each) * shard_rows, shard_rows)
        for j, cot in enumerate(cots):

            @pl.when(source == j)
            def _(i=i, cot=cot, first_row=first_row):
                copy(i, cot, first_row).start()

    return [copy(i, cots[0], 0) for i in range(count)]


def nonlinear(total, cotangent):
    tile = total.shape[1] // 2
    gate_value, up_value = total[:, :tile], total[:, tile:]
    sig_gate = jax.nn.sigmoid(gate_value)
    act_gate = gate_value * sig_gate
    hidden = (act_gate * up_value).astype(BF16)
    gate_grad = (cotangent * up_value * sig_gate * (1.0 + gate_value * (1.0 - sig_gate))).astype(BF16)
    up_grad = (cotangent * act_gate).astype(BF16)
    return hidden, jnp.concatenate([gate_grad, up_grad], axis=1)


def total_of(c, parts):
    total = parts[0][c].astype(F32)
    for part in parts[1:]:
        total = total + part[c].astype(F32)
    return total


def back_terms(c, grads, gate_ref, up_ref):
    return lax.dot_general(
        grads, weights_of(c, gate_ref, up_ref), (((1,), (1,)), ((), ())), preferred_element_type=F32
    )


def add_back(c, lists, back, accs, slots, tile):
    rows_ref, counts_ref = lists
    rows = [rows_ref[k, 0, c] for k in range(slots)]
    start = 0
    for acc in accs:
        stop = start + acc.shape[1]
        sums = [
            acc[rows[k]] + keep(k, counts_ref[0, c], back[start:stop, k * tile : (k + 1) * tile])
            for k in range(slots)
        ]
        for k in range(slots):
            acc[rows[k]] = sums[k]
        start = stop


def tile_grads(c, first, lists, turned_ref, grads, gate_ref, up_ref):
    rows_ref, counts_ref = lists
    slots, tile = gate_ref.shape[2:4]
    picked = jnp.concatenate([turned_ref[rows_ref[k, 0, first + c]] for k in range(slots)], axis=0)
    found = jnp.dot(picked, grads, preferred_element_type=F32)
    for k in range(slots):
        term = keep(k, counts_ref[0, first + c], found[k * tile : (k + 1) * tile]).astype(BF16)
        gate_ref[c, 0, k] = term[:, :tile]
        up_ref[c, 0, k] = term[:, tile:]


def start_hidden(members, first, meta_ref, source_of, hidden_hbm, shard_rows, sems):
    width = source_of(0).shape[1]
    shards_each = hidden_hbm.shape[0] // shard_rows

    def copy(i, member):
        return pltpu.make_async_copy(
            source_of(member), hidden_hbm.at[pl.ds(i * shard_rows, shard_rows), pl.ds(first, width)], sems.at[i]
        )

    for i in range(shards_each):
        wanted = meta_ref[1] * shards_each + i
        for member in members:

            @pl.when(shard_of(member, meta_ref) == wanted)
            def _(i=i, member=member):
                copy(i, member).start()

    return [copy(i, 0) for i in range(shards_each)]


def first_half_kernel(members, owners, meta_ref, rows_ref, counts_ref, gate_in, up_in, turned_ref, *refs):
    near, rest, cots = refs[:owners], refs[owners : 2 * owners], refs[2 * owners : 3 * owners]
    gate_hbm, up_hbm, hidden_hbm, acc_near, acc_far = refs[-15:-10]
    cot_ref, hidden_ref, gate_ref, up_ref, gate_w, up_w, sems, cot_sems, hidden_sems, load_sems = refs[-10:]
    cols, _, slots, tile, _ = gate_ref.shape
    ring = gate_w.shape[0]

    def loads(c):
        return (
            pltpu.make_async_copy(gate_in.at[c], gate_w.at[c % ring], load_sems.at[0, c % ring]),
            pltpu.make_async_copy(up_in.at[c], up_w.at[c % ring], load_sems.at[1, c % ring]),
        )

    arrive = windowed(loads, cols)
    shard_rows = cot_ref.shape[0] // members
    lists = (rows_ref, counts_ref)
    waits = start_cots(range(members), 0, meta_ref, cots, cot_ref, cot_sems)
    acc_near[...] = jnp.zeros_like(acc_near)
    acc_far[...] = jnp.zeros_like(acc_far)
    for wait in waits:
        wait.wait()
    copies = []
    for c in range(cols):
        total = jnp.concatenate([total_of(c, near), total_of(c, rest)], axis=0)
        where = slice(c * tile, (c + 1) * tile)
        hidden, grads = nonlinear(total, cot_ref[:, where].astype(F32))
        hidden_ref[:, where] = hidden
        tile_grads(c, 0, lists, turned_ref, grads, gate_ref, up_ref)
        copies.append(pltpu.make_async_copy(gate_ref.at[c], gate_hbm.at[c], sems.at[0, c]))
        copies.append(pltpu.make_async_copy(up_ref.at[c], up_hbm.at[c], sems.at[1, c]))
        copies[-2].start()
        copies[-1].start()
        arrive(c)
        add_back(c, lists, back_terms(c % ring, grads, gate_w, up_w), (acc_near, acc_far), slots, tile)
    waits = start_hidden(
        range(members),
        0,
        meta_ref,
        lambda m: hidden_ref.at[pl.ds(m * shard_rows, shard_rows)],
        hidden_hbm,
        shard_rows,
        hidden_sems,
    )
    for wait in copies + waits:
        wait.wait()


def second_half_kernel(members, owners, first, meta_ref, rows_ref, counts_ref, gate_w, up_w, acc_in, *refs):
    parts, cots = refs[:owners], refs[owners : 2 * owners]
    outs = refs[-(2 + len(members) + 3) :]
    grads_ref, hidden_ref = outs[:2]
    dxs = outs[2 : 2 + len(members)]
    cot_ref, acc_ref, cot_sems = outs[-3:]
    cols, _, slots, tile, _ = gate_w.shape
    shard_rows = cot_ref.shape[0] // len(members)
    waits = start_cots(members, first * tile, meta_ref, cots, cot_ref, cot_sems)
    acc_ref[...] = acc_in[...]
    for wait in waits:
        wait.wait()
    for c in range(cols):
        where = slice(c * tile, (c + 1) * tile)
        hidden, grads = nonlinear(total_of(c, parts), cot_ref[:, where].astype(F32))
        hidden_ref[:, where] = hidden
        grads_ref[c] = grads
        add_back(first + c, (rows_ref, counts_ref), back_terms(c, grads, gate_w, up_w), (acc_ref,), slots, tile)
    for r in range(acc_ref.shape[0]):
        block = acc_ref[r].astype(BF16)
        for m, dx in enumerate(dxs):
            dx[:, r * tile : (r + 1) * tile] = block[m * shard_rows : (m + 1) * shard_rows]


def last_grads_kernel(members, first, start, with_hidden, meta_ref, rows_ref, counts_ref, turned_ref, *refs):
    near_grads, far_grads, near_hidden, far_hidden = refs[:4]
    gate_hbm, up_hbm, hidden_hbm, token_ref, gate_ref, up_ref, sems, hidden_sems = refs[-8:]
    cols, _, _, tile, _ = gate_ref.shape
    shard_rows = near_hidden.shape[0] // 2
    token_ref[...] = jnp.zeros_like(token_ref)

    def hidden_of(m):
        if m < 2:
            return near_hidden.at[pl.ds(m * shard_rows, shard_rows)]
        return far_hidden.at[pl.ds((m - 2) * shard_rows, shard_rows)]

    waits = []
    if with_hidden:
        waits = start_hidden(
            range(members), first * tile, meta_ref, hidden_of, hidden_hbm, shard_rows, hidden_sems
        )
    for c in range(cols):
        grads = jnp.concatenate([near_grads[start + c], far_grads[start + c]], axis=0)
        at = first + start + c
        tile_grads(c, first + start, (rows_ref, counts_ref), turned_ref, grads, gate_ref, up_ref)
        waits.append(pltpu.make_async_copy(gate_ref.at[c], gate_hbm.at[at], sems.at[0, c]))
        waits.append(pltpu.make_async_copy(up_ref.at[c], up_hbm.at[at], sems.at[1, c]))
        waits[-2].start()
        waits[-1].start()
    for wait in waits:
        wait.wait()


def copy_kernel(x_ref, _, out_ref):
    out_ref[...] = x_ref[...]


def add_kernel(left_ref, right_ref, out_ref):
    out_ref[...] = (left_ref[...].astype(F32) + right_ref[...].astype(F32)).astype(BF16)


def sum_kernel(count, *refs):
    total = sum(ref[...].astype(F32) for ref in refs[:count])
    refs[-2][...] = total
    refs[-1][...] = total.astype(BF16)


def swap(x, axis, step):
    return lax.ppermute(x, axis, [(i, i ^ step) for i in range(lax.axis_size(axis))])


def swap_far(x, base):
    shards, cores = lax.axis_size("tok"), lax.axis_size("sub")
    pairs = [(t * cores + s, (t ^ (base + s)) * cores + s) for t in range(shards) for s in range(cores)]
    return lax.ppermute(x, ("tok", "sub"), pairs)


def on_device(features_in, gate_tiles, up_tiles, block_rows, block_counts, d_hidden):
    shards, owners = lax.axis_size("tok"), lax.axis_size("blk")
    cols, _, slots, tile, _ = gate_tiles.shape
    shard_rows, width = features_in.shape
    row_blocks = width // tile
    row_total = shards * shard_rows
    near_rows = 2 * shard_rows
    half = cols // 2
    bases = range(2, shards, 2)
    meta = jnp.stack([lax.axis_index("tok"), lax.axis_index("blk"), lax.axis_index("sub")]).astype(jnp.int32)
    lists = (jnp.transpose(block_rows, (2, 1, 0)), jnp.transpose(block_counts, (1, 0)))

    def held(weights):
        return [pltpu.with_memory_space_constraint(w, pltpu.VMEM) for w in weights]

    def shape(*dims, dtype=BF16):
        return jax.ShapeDtypeStruct(dims, dtype)

    def cost(tokens, columns, products, tile_bytes, weight=1):
        tiles = weight * columns * slots
        return pl.CostEstimate(
            flops=4 * tokens * tiles * tile * tile * products,
            bytes_accessed=4 * tiles * tile * tile * tile_bytes,
            transcendentals=0,
        )

    def to_owners(part):
        return [part] + [swap(part, "blk", s) for s in range(1, owners)]

    fars = [swap_far(features_in, base) for base in bases]
    xs = [features_in, swap(features_in, "tok", 1)]
    cots = [d_hidden] + [swap(d_hidden, "blk", s) for s in range(1, owners)]

    def tile_shape(columns):
        return pltpu.VMEM((columns, 1, slots, tile, tile), BF16)

    def from_hbm(*arrays):
        return [pltpu.with_memory_space_constraint(array, pltpu.HBM) for array in arrays]

    near_a, *weights_a = pl.pallas_call(
        forward_own_kernel,
        out_shape=(shape(half, shard_rows, 2 * tile), tile_shape(half), tile_shape(half)),
        in_specs=[ANY_SPEC] * 5,
        out_specs=(VMEM_SPEC,) * 3,
        scratch_shapes=[
            pltpu.VMEM((shard_rows, width), BF16),
            pltpu.SMEM(lists[0].shape, jnp.int32),
            pltpu.SMEM(lists[1].shape, jnp.int32),
            pltpu.SemaphoreType.DMA((2, half)),
            pltpu.SemaphoreType.DMA((3,)),
        ],
        compiler_params=limit(8),
        cost_estimate=cost(shard_rows, half, 1, 1),
        name="forward_own_a",
    )(*from_hbm(features_in, *lists, gate_tiles, up_tiles))
    near_a = to_owners(near_a)

    for far in fars:
        ready = pl.pallas_call(
            copy_kernel,
            out_shape=shape(shard_rows, width),
            in_specs=[VMEM_SPEC, ANY_SPEC],
            out_specs=VMEM_SPEC,
            compiler_params=limit(8),
            cost_estimate=pl.CostEstimate(flops=0, bytes_accessed=0, transcendentals=0),
            name="after_own",
        )(far, near_a[0])
        xs += [far, swap(ready, "sub", 1)]

    rest_a = pl.pallas_call(
        functools.partial(forward_kernel, shards - 1, 0),
        out_shape=shape(half, row_total - shard_rows, 2 * tile),
        in_specs=[SMEM_SPEC] * 2 + [VMEM_SPEC] * (shards + 1) + [ANY_SPEC],
        out_specs=VMEM_SPEC,
        compiler_params=limit(8),
        cost_estimate=cost(row_total, half, 1, 1),
        name="forward_rest_a",
    )(*lists, *xs[1:], *held(weights_a), cots[-1])
    rest_a = to_owners(rest_a)

    rest = cols - half
    far_b, near_b, gate_b, up_b, turned = pl.pallas_call(
        functools.partial(load_forward_kernel, shards, ((near_rows, row_total), (0, near_rows)), half, 1),
        out_shape=(
            shape(rest, row_total - near_rows, 2 * tile),
            shape(rest, near_rows, 2 * tile),
            tile_shape(rest),
            tile_shape(rest),
            pltpu.VMEM((row_blocks, tile, row_total), BF16),
        ),
        in_specs=[SMEM_SPEC] * 2 + [VMEM_SPEC] * shards + [ANY_SPEC] * 4,
        out_specs=(VMEM_SPEC,) * 5,
        scratch_shapes=[pltpu.SemaphoreType.DMA((2, rest))],
        compiler_params=limit(8),
        cost_estimate=cost(row_total, rest, 1, 1, 5),
        name="forward_b",
    )(*lists, *xs, *from_hbm(gate_tiles, up_tiles), rest_a[0], near_a[-1])
    weights_b = [gate_b, up_b]
    far_b, near_b = to_owners(far_b), to_owners(near_b)

    out_tiles = shape(*gate_tiles.shape)
    gate_out, up_out, hidden_out, acc_near, acc_far = pl.pallas_call(
        functools.partial(first_half_kernel, shards, owners),
        out_shape=(
            out_tiles,
            out_tiles,
            shape(*d_hidden.shape),
            shape(row_blocks, near_rows, tile, dtype=F32),
            shape(row_blocks, row_total - near_rows, tile, dtype=F32),
        ),
        in_specs=[SMEM_SPEC] * 3
        + [ANY_SPEC] * 2
        + [VMEM_SPEC] * (1 + 2 * owners)
        + [ANY_SPEC] * (owners + 2),
        out_specs=(ANY_SPEC,) * 3 + (VMEM_SPEC,) * 2,
        scratch_shapes=[
            pltpu.VMEM((row_total, half * tile), BF16),
            pltpu.VMEM((row_total, half * tile), BF16),
            pltpu.VMEM((half, 1, slots, tile, tile), BF16),
            pltpu.VMEM((half, 1, slots, tile, tile), BF16),
            pltpu.VMEM((WINDOW + 1, 1, slots, tile, tile), BF16),
            pltpu.VMEM((WINDOW + 1, 1, slots, tile, tile), BF16),
            pltpu.SemaphoreType.DMA((2, half)),
            pltpu.SemaphoreType.DMA((shards,)),
            pltpu.SemaphoreType.DMA((d_hidden.shape[0] // shard_rows,)),
            pltpu.SemaphoreType.DMA((2, WINDOW + 1)),
        ],
        compiler_params=limit(16),
        cost_estimate=cost(row_total, half, 2, 1, 1),
        name="first_half",
    )(meta, *lists, *from_hbm(gate_tiles, up_tiles), *held([turned]), *near_a, *rest_a, *cots, far_b[0], near_b[0])

    def second_half(members, acc, parts, after):
        rows_here = len(members) * shard_rows
        return pl.pallas_call(
            functools.partial(second_half_kernel, members, owners, half),
            out_shape=(
                shape(rest, rows_here, 2 * tile),
                shape(rows_here, rest * tile),
                *[shape(shard_rows, width) for _ in members],
            ),
            in_specs=[SMEM_SPEC] * 3 + [VMEM_SPEC] * (3 + owners) + [ANY_SPEC] * (owners + 1),
            out_specs=(VMEM_SPEC,) * (2 + len(members)),
            scratch_shapes=[
                pltpu.VMEM((rows_here, rest * tile), BF16),
                pltpu.VMEM((row_blocks, rows_here, tile), F32),
                pltpu.SemaphoreType.DMA((len(members),)),
            ],
            compiler_params=limit(8),
            cost_estimate=cost(rows_here, rest, 1, 1, 1 if members[0] == 0 else 1),
            name="second_half",
        )(meta, *lists, *held(weights_b), acc, *parts, *cots, after)

    far_grads, far_hidden, *far_dxs = second_half(range(2, shards), acc_far, far_b, acc_near)
    both_cores = []
    for mine, others in zip(far_dxs[::2], far_dxs[1::2]):
        other = swap(others, "sub", 1)
        both_cores.append(
            pl.pallas_call(
                add_kernel,
                out_shape=shape(shard_rows, width),
                in_specs=[VMEM_SPEC] * 2,
                out_specs=VMEM_SPEC,
                compiler_params=limit(8),
                cost_estimate=pl.CostEstimate(flops=0, bytes_accessed=0, transcendentals=0),
                name="add_cores",
            )(mine, other)
        )
    back_far = [swap_far(total, base) for total, base in zip(both_cores, bases)]

    near_grads, near_hidden, own_dx, next_dx = second_half(range(2), acc_near, near_b, both_cores[-1])
    back_next = swap(next_dx, "tok", 1)

    def last_grads(start, stop, with_hidden, outs):
        count = stop - start
        return pl.pallas_call(
            functools.partial(last_grads_kernel, shards, half, start, with_hidden),
            out_shape=(out_tiles, out_tiles, shape(*d_hidden.shape), shape(8, tile, dtype=F32)),
            in_specs=[SMEM_SPEC] * 3 + [VMEM_SPEC] * 3 + [ANY_SPEC] * 5,
            out_specs=(ANY_SPEC,) * 3 + (VMEM_SPEC,),
            scratch_shapes=[
                pltpu.VMEM((count, 1, slots, tile, tile), BF16),
                pltpu.VMEM((count, 1, slots, tile, tile), BF16),
                pltpu.SemaphoreType.DMA((2, count)),
                pltpu.SemaphoreType.DMA((d_hidden.shape[0] // shard_rows,)),
            ],
            input_output_aliases={8: 0, 9: 1, 10: 2},
            compiler_params=limit(12),
            cost_estimate=cost(row_total, count, 1, 1, 10),
            name="last_grads",
        )(meta, *lists, *held([turned]), near_grads, far_grads, near_hidden, far_hidden, *outs)

    middle = rest
    *outs, token = last_grads(0, middle, True, (gate_out, up_out, hidden_out))
    arrived = [own_dx, back_next, *back_far]
    mine, mine_sent = pl.pallas_call(
        functools.partial(sum_kernel, len(arrived)),
        out_shape=(shape(shard_rows, width, dtype=F32), shape(shard_rows, width)),
        in_specs=[VMEM_SPEC] * len(arrived) + [ANY_SPEC],
        out_specs=(VMEM_SPEC,) * 2,
        compiler_params=limit(8),
        name="sum_shards",
    )(*arrived, token)
    if middle < rest:
        *outs, _ = last_grads(middle, rest, False, outs)
    gate_out, up_out, hidden_out = outs
    features_grad = (mine + swap(mine_sent, "sub", 1).astype(F32)).astype(BF16)
    return (hidden_out, gate_out, up_out, features_grad)


def solution(mesh):
    return jax.shard_map(
        on_device,
        mesh=mesh,
        in_specs=(
            P(("groups", "tok"), "blk"),
            P(("tok", "sub"), "blk", None, None, None),
            P(("tok", "sub"), "blk", None, None, None),
            P(("tok", "sub"), "blk", None),
            P(("tok", "sub"), "blk"),
            P(("groups", "blk"), ("tok", "sub")),
        ),
        out_specs=(
            P(("groups", "blk"), ("tok", "sub")),
            P(("groups", "tok", "sub"), "blk", None, None, None),
            P(("groups", "tok", "sub"), "blk", None, None, None),
            P(("groups", "tok"), "blk"),
        ),
        check_vma=False,
    )
```

```python
import functools

import jax
import jax.numpy as jnp
from jax import lax
from jax.experimental import pallas as pl
from jax.experimental.pallas import tpu as pltpu
from jax.sharding import PartitionSpec as P

F32 = jnp.float32
BF16 = jnp.bfloat16
MIB = 1 << 20
WINDOW = 5
VMEM_SPEC = pl.BlockSpec(memory_space=pltpu.VMEM)
SMEM_SPEC = pl.BlockSpec(memory_space=pltpu.SMEM)
ANY_SPEC = pl.BlockSpec(memory_space=pl.ANY)


def limit(mib):
    return pltpu.CompilerParams(vmem_limit_bytes=mib * MIB)


def lanes(index, width):
    return pl.ds(pl.multiple_of(index * width, width), width)


def weights_of(c, gate_ref, up_ref):
    slots, rows, cols = gate_ref.shape[2:]
    return jnp.concatenate(
        [gate_ref[c, 0].reshape(slots * rows, cols), up_ref[c, 0].reshape(slots * rows, cols)], axis=1
    )


def keep(k, count, block):
    return jnp.where(k < count, block, jnp.zeros_like(block))


def forward_column(c, first, lists, xs, gate_ref, up_ref):
    rows_ref, counts_ref = lists
    slots, tile = gate_ref.shape[2:4]
    count = counts_ref[0, first + c]
    picked = []
    for k in range(slots):
        where = lanes(rows_ref[k, 0, first + c], tile)
        picked.append(keep(k, count, jnp.concatenate([x[:, where] for x in xs], axis=0)))
    return jnp.dot(
        jnp.concatenate(picked, axis=1), weights_of(c, gate_ref, up_ref), preferred_element_type=F32
    ).astype(BF16)


def windowed(copies, cols):
    for c in range(min(WINDOW, cols)):
        for copy in copies(c):
            copy.start()

    def arrive(c):
        for copy in copies(c):
            copy.wait()
        if c + WINDOW < cols:
            for copy in copies(c + WINDOW):
                copy.start()

    return arrive


def forward_own_kernel(x_hbm, rows_hbm, counts_hbm, gate_hbm, up_hbm, part_ref, *scratch):
    x_ref, rows_ref, counts_ref, gate_ref, up_ref, sems, small_sems = scratch
    cols = gate_ref.shape[0]

    def copies(c):
        return (
            pltpu.make_async_copy(gate_hbm.at[c], gate_ref.at[c], sems.at[0, c]),
            pltpu.make_async_copy(up_hbm.at[c], up_ref.at[c], sems.at[1, c]),
        )

    small = [
        pltpu.make_async_copy(source, target, small_sems.at[i])
        for i, (source, target) in enumerate(((rows_hbm, rows_ref), (counts_hbm, counts_ref), (x_hbm, x_ref)))
    ]
    for copy in small:
        copy.start()
    arrive = windowed(copies, cols)
    for copy in small:
        copy.wait()
    for c in range(cols):
        arrive(c)
        part_ref[c] = forward_column(c, 0, (rows_ref, counts_ref), [x_ref], gate_ref, up_ref)


def forward_kernel(members, rows_ref, counts_ref, *refs):
    xs = refs[:members]
    gate_hbm, up_hbm = refs[members : members + 2]
    part_ref, gate_ref, up_ref, sems = refs[-4:]

    def copies(c):
        return (
            pltpu.make_async_copy(gate_hbm.at[c], gate_ref.at[c], sems.at[0, c]),
            pltpu.make_async_copy(up_hbm.at[c], up_ref.at[c], sems.at[1, c]),
        )

    cols = gate_ref.shape[0]
    arrive = windowed(copies, cols)
    for c in range(cols):
        arrive(c)
        part_ref[c] = forward_column(c, 0, (rows_ref, counts_ref), xs, gate_ref, up_ref)


def load_forward_kernel(members, groups, first, turn, rows_ref, counts_ref, *refs):
    xs = refs[:members]
    gate_hbm, up_hbm = refs[members : members + 2]
    outs = refs[-(len(groups) + 3 + turn) :]
    parts, gate_ref, up_ref, sems = outs[: len(groups)], outs[-3 - turn], outs[-2 - turn], outs[-1]
    cols, _, _, tile, _ = gate_ref.shape

    def copies(c):
        return (
            pltpu.make_async_copy(gate_hbm.at[first + c], gate_ref.at[c], sems.at[0, c]),
            pltpu.make_async_copy(up_hbm.at[first + c], up_ref.at[c], sems.at[1, c]),
        )

    arrive = windowed(copies, cols)
    if turn:
        turned_ref = outs[-2]
        identity = (
            lax.broadcasted_iota(jnp.int32, (tile, tile), 0) == lax.broadcasted_iota(jnp.int32, (tile, tile), 1)
        ).astype(F32).astype(BF16)
        for r in range(turned_ref.shape[0]):
            block = jnp.concatenate([x[:, r * tile : (r + 1) * tile] for x in xs], axis=0)
            turned_ref[r] = lax.dot_general(
                identity, block, (((1,), (1,)), ((), ())), preferred_element_type=F32
            ).astype(BF16)
    for c in range(cols):
        arrive(c)
        part = forward_column(c, first, (rows_ref, counts_ref), xs, gate_ref, up_ref)
        for (start, stop), part_ref in zip(groups, parts):
            part_ref[c] = part[start:stop]


def shard_of(member, meta_ref):
    if member < 2:
        return meta_ref[0] ^ member
    return meta_ref[0] ^ ((member & ~1) + ((member & 1) ^ meta_ref[2]))


def start_cots(members, first, meta_ref, cots, cot_ref, sems):
    count = len(members)
    shard_rows, width = cot_ref.shape[0] // count, cot_ref.shape[1]
    shards_each = cots[0].shape[0] // shard_rows

    def copy(i, cot, first_row):
        return pltpu.make_async_copy(
            cot.at[pl.ds(first_row, shard_rows), pl.ds(first, width)],
            cot_ref.at[pl.ds(i * shard_rows, shard_rows)],
            sems.at[i],
        )

    for i, member in enumerate(members):
        shard = shard_of(member, meta_ref)
        source = (shard // shards_each) ^ meta_ref[1]
        first_row = pl.multiple_of((shard % shards_each) * shard_rows, shard_rows)
        for j, cot in enumerate(cots):

            @pl.when(source == j)
            def _(i=i, cot=cot, first_row=first_row):
                copy(i, cot, first_row).start()

    return [copy(i, cots[0], 0) for i in range(count)]


def nonlinear(total, cotangent):
    tile = total.shape[1] // 2
    gate_value, up_value = total[:, :tile], total[:, tile:]
    sig_gate = jax.nn.sigmoid(gate_value)
    act_gate = gate_value * sig_gate
    hidden = (act_gate * up_value).astype(BF16)
    gate_grad = (cotangent * up_value * sig_gate * (1.0 + gate_value * (1.0 - sig_gate))).astype(BF16)
    up_grad = (cotangent * act_gate).astype(BF16)
    return hidden, jnp.concatenate([gate_grad, up_grad], axis=1)


def total_of(c, parts):
    total = parts[0][c].astype(F32)
    for part in parts[1:]:
        total = total + part[c].astype(F32)
    return total


def back_terms(c, grads, gate_ref, up_ref):
    return lax.dot_general(
        grads, weights_of(c, gate_ref, up_ref), (((1,), (1,)), ((), ())), preferred_element_type=F32
    )


def add_back(c, lists, back, accs, slots, tile):
    rows_ref, counts_ref = lists
    rows = [rows_ref[k, 0, c] for k in range(slots)]
    start = 0
    for acc in accs:
        stop = start + acc.shape[1]
        sums = [
            acc[rows[k]] + keep(k, counts_ref[0, c], back[start:stop, k * tile : (k + 1) * tile])
            for k in range(slots)
        ]
        for k in range(slots):
            acc[rows[k]] = sums[k]
        start = stop


def tile_grads(c, first, lists, turned_ref, grads, gate_ref, up_ref):
    rows_ref, counts_ref = lists
    slots, tile = gate_ref.shape[2:4]
    picked = jnp.concatenate([turned_ref[rows_ref[k, 0, first + c]] for k in range(slots)], axis=0)
    found = jnp.dot(picked, grads, preferred_element_type=F32)
    for k in range(slots):
        term = keep(k, counts_ref[0, first + c], found[k * tile : (k + 1) * tile]).astype(BF16)
        gate_ref[c, 0, k] = term[:, :tile]
        up_ref[c, 0, k] = term[:, tile:]


def start_hidden(members, first, meta_ref, source_of, hidden_hbm, shard_rows, sems):
    width = source_of(0).shape[1]
    shards_each = hidden_hbm.shape[0] // shard_rows

    def copy(i, member):
        return pltpu.make_async_copy(
            source_of(member), hidden_hbm.at[pl.ds(i * shard_rows, shard_rows), pl.ds(first, width)], sems.at[i]
        )

    for i in range(shards_each):
        wanted = meta_ref[1] * shards_each + i
        for member in members:

            @pl.when(shard_of(member, meta_ref) == wanted)
            def _(i=i, member=member):
                copy(i, member).start()

    return [copy(i, 0) for i in range(shards_each)]


def first_half_kernel(members, owners, meta_ref, rows_ref, counts_ref, gate_in, up_in, turned_ref, *refs):
    near, rest, cots = refs[:owners], refs[owners : 2 * owners], refs[2 * owners : 3 * owners]
    gate_hbm, up_hbm, hidden_hbm, acc_near, acc_far = refs[-15:-10]
    cot_ref, hidden_ref, gate_ref, up_ref, gate_w, up_w, sems, cot_sems, hidden_sems, load_sems = refs[-10:]
    cols, _, slots, tile, _ = gate_ref.shape
    ring = gate_w.shape[0]

    def loads(c):
        return (
            pltpu.make_async_copy(gate_in.at[c], gate_w.at[c % ring], load_sems.at[0, c % ring]),
            pltpu.make_async_copy(up_in.at[c], up_w.at[c % ring], load_sems.at[1, c % ring]),
        )

    arrive = windowed(loads, cols)
    shard_rows = cot_ref.shape[0] // members
    lists = (rows_ref, counts_ref)
    waits = start_cots(range(members), 0, meta_ref, cots, cot_ref, cot_sems)
    acc_near[...] = jnp.zeros_like(acc_near)
    acc_far[...] = jnp.zeros_like(acc_far)
    for wait in waits:
        wait.wait()
    copies = []
    for c in range(cols):
        total = jnp.concatenate([total_of(c, near), total_of(c, rest)], axis=0)
        where = slice(c * tile, (c + 1) * tile)
        hidden, grads = nonlinear(total, cot_ref[:, where].astype(F32))
        hidden_ref[:, where] = hidden
        tile_grads(c, 0, lists, turned_ref, grads, gate_ref, up_ref)
        copies.append(pltpu.make_async_copy(gate_ref.at[c], gate_hbm.at[c], sems.at[0, c]))
        copies.append(pltpu.make_async_copy(up_ref.at[c], up_hbm.at[c], sems.at[1, c]))
        copies[-2].start()
        copies[-1].start()
        arrive(c)
        add_back(c, lists, back_terms(c % ring, grads, gate_w, up_w), (acc_near, acc_far), slots, tile)
    waits = start_hidden(
        range(members),
        0,
        meta_ref,
        lambda m: hidden_ref.at[pl.ds(m * shard_rows, shard_rows)],
        hidden_hbm,
        shard_rows,
        hidden_sems,
    )
    for wait in copies + waits:
        wait.wait()


def second_half_kernel(members, owners, first, meta_ref, rows_ref, counts_ref, gate_w, up_w, acc_in, *refs):
    parts, cots = refs[:owners], refs[owners : 2 * owners]
    outs = refs[-(2 + len(members) + 3) :]
    grads_ref, hidden_ref = outs[:2]
    dxs = outs[2 : 2 + len(members)]
    cot_ref, acc_ref, cot_sems = outs[-3:]
    cols, _, slots, tile, _ = gate_w.shape
    shard_rows = cot_ref.shape[0] // len(members)
    waits = start_cots(members, first * tile, meta_ref, cots, cot_ref, cot_sems)
    acc_ref[...] = acc_in[...]
    for wait in waits:
        wait.wait()
    for c in range(cols):
        where = slice(c * tile, (c + 1) * tile)
        hidden, grads = nonlinear(total_of(c, parts), cot_ref[:, where].astype(F32))
        hidden_ref[:, where] = hidden
        grads_ref[c] = grads
        add_back(first + c, (rows_ref, counts_ref), back_terms(c, grads, gate_w, up_w), (acc_ref,), slots, tile)
    for r in range(acc_ref.shape[0]):
        block = acc_ref[r].astype(BF16)
        for m, dx in enumerate(dxs):
            dx[:, r * tile : (r + 1) * tile] = block[m * shard_rows : (m + 1) * shard_rows]


def last_grads_kernel(members, first, start, with_hidden, meta_ref, rows_ref, counts_ref, turned_ref, *refs):
    near_grads, far_grads, near_hidden, far_hidden = refs[:4]
    gate_hbm, up_hbm, hidden_hbm, token_ref, gate_ref, up_ref, sems, hidden_sems = refs[-8:]
    cols, _, _, tile, _ = gate_ref.shape
    shard_rows = near_hidden.shape[0] // 2
    token_ref[...] = jnp.zeros_like(token_ref)

    def hidden_of(m):
        if m < 2:
            return near_hidden.at[pl.ds(m * shard_rows, shard_rows)]
        return far_hidden.at[pl.ds((m - 2) * shard_rows, shard_rows)]

    waits = []
    if with_hidden:
        waits = start_hidden(
            range(members), first * tile, meta_ref, hidden_of, hidden_hbm, shard_rows, hidden_sems
        )
    for c in range(cols):
        grads = jnp.concatenate([near_grads[start + c], far_grads[start + c]], axis=0)
        at = first + start + c
        tile_grads(c, first + start, (rows_ref, counts_ref), turned_ref, grads, gate_ref, up_ref)
        waits.append(pltpu.make_async_copy(gate_ref.at[c], gate_hbm.at[at], sems.at[0, c]))
        waits.append(pltpu.make_async_copy(up_ref.at[c], up_hbm.at[at], sems.at[1, c]))
        waits[-2].start()
        waits[-1].start()
    for wait in waits:
        wait.wait()


def copy_kernel(x_ref, _, out_ref):
    out_ref[...] = x_ref[...]


def add_kernel(left_ref, right_ref, out_ref):
    out_ref[...] = (left_ref[...].astype(F32) + right_ref[...].astype(F32)).astype(BF16)


def sum_kernel(count, *refs):
    total = sum(ref[...].astype(F32) for ref in refs[:count])
    refs[-2][...] = total
    refs[-1][...] = total.astype(BF16)


def swap(x, axis, step):
    return lax.ppermute(x, axis, [(i, i ^ step) for i in range(lax.axis_size(axis))])


def swap_far(x, base):
    shards, cores = lax.axis_size("tok"), lax.axis_size("sub")
    pairs = [(t * cores + s, (t ^ (base + s)) * cores + s) for t in range(shards) for s in range(cores)]
    return lax.ppermute(x, ("tok", "sub"), pairs)


def on_device(features_in, gate_tiles, up_tiles, block_rows, block_counts, d_hidden):
    shards, owners = lax.axis_size("tok"), lax.axis_size("blk")
    cols, _, slots, tile, _ = gate_tiles.shape
    shard_rows, width = features_in.shape
    row_blocks = width // tile
    row_total = shards * shard_rows
    near_rows = 2 * shard_rows
    half = cols // 2
    bases = range(2, shards, 2)
    meta = jnp.stack([lax.axis_index("tok"), lax.axis_index("blk"), lax.axis_index("sub")]).astype(jnp.int32)
    lists = (jnp.transpose(block_rows, (2, 1, 0)), jnp.transpose(block_counts, (1, 0)))

    def held(weights):
        return [pltpu.with_memory_space_constraint(w, pltpu.VMEM) for w in weights]

    def shape(*dims, dtype=BF16):
        return jax.ShapeDtypeStruct(dims, dtype)

    def cost(tokens, columns, products, tile_bytes, weight=1):
        tiles = weight * columns * slots
        return pl.CostEstimate(
            flops=4 * tokens * tiles * tile * tile * products,
            bytes_accessed=4 * tiles * tile * tile * tile_bytes,
            transcendentals=0,
        )

    def to_owners(part):
        return [part] + [swap(part, "blk", s) for s in range(1, owners)]

    fars = [swap_far(features_in, base) for base in bases]
    xs = [features_in, swap(features_in, "tok", 1)]
    cots = [d_hidden] + [swap(d_hidden, "blk", s) for s in range(1, owners)]

    def tile_shape(columns):
        return pltpu.VMEM((columns, 1, slots, tile, tile), BF16)

    def from_hbm(*arrays):
        return [pltpu.with_memory_space_constraint(array, pltpu.HBM) for array in arrays]

    near_a = pl.pallas_call(
        forward_own_kernel,
        out_shape=shape(half, shard_rows, 2 * tile),
        in_specs=[ANY_SPEC] * 5,
        out_specs=VMEM_SPEC,
        scratch_shapes=[
            pltpu.VMEM((shard_rows, width), BF16),
            pltpu.SMEM(lists[0].shape, jnp.int32),
            pltpu.SMEM(lists[1].shape, jnp.int32),
            tile_shape(half),
            tile_shape(half),
            pltpu.SemaphoreType.DMA((2, half)),
            pltpu.SemaphoreType.DMA((3,)),
        ],
        compiler_params=limit(12),
        cost_estimate=cost(shard_rows, half, 1, 1),
        name="forward_own_a",
    )(*from_hbm(features_in, *lists, gate_tiles, up_tiles))
    near_a = to_owners(near_a)

    for far in fars:
        ready = pl.pallas_call(
            copy_kernel,
            out_shape=shape(shard_rows, width),
            in_specs=[VMEM_SPEC, ANY_SPEC],
            out_specs=VMEM_SPEC,
            compiler_params=limit(8),
            cost_estimate=pl.CostEstimate(flops=0, bytes_accessed=0, transcendentals=0),
            name="after_own",
        )(far, near_a[0])
        xs += [far, swap(ready, "sub", 1)]

    rest_a = pl.pallas_call(
        functools.partial(forward_kernel, shards - 1),
        out_shape=shape(half, row_total - shard_rows, 2 * tile),
        in_specs=[SMEM_SPEC] * 2 + [VMEM_SPEC] * (shards - 1) + [ANY_SPEC] * 3,
        out_specs=VMEM_SPEC,
        scratch_shapes=[tile_shape(half), tile_shape(half), pltpu.SemaphoreType.DMA((2, half))],
        compiler_params=limit(12),
        cost_estimate=cost(row_total, half, 1, 1),
        name="forward_rest_a",
    )(*lists, *xs[1:], *from_hbm(gate_tiles, up_tiles), cots[-1])
    rest_a = to_owners(rest_a)

    rest = cols - half
    far_b, near_b, gate_b, up_b, turned = pl.pallas_call(
        functools.partial(load_forward_kernel, shards, ((near_rows, row_total), (0, near_rows)), half, 1),
        out_shape=(
            shape(rest, row_total - near_rows, 2 * tile),
            shape(rest, near_rows, 2 * tile),
            tile_shape(rest),
            tile_shape(rest),
            pltpu.VMEM((row_blocks, tile, row_total), BF16),
        ),
        in_specs=[SMEM_SPEC] * 2 + [VMEM_SPEC] * shards + [ANY_SPEC] * 4,
        out_specs=(VMEM_SPEC,) * 5,
        scratch_shapes=[pltpu.SemaphoreType.DMA((2, rest))],
        compiler_params=limit(8),
        cost_estimate=cost(row_total, rest, 1, 1, 5),
        name="forward_b",
    )(*lists, *xs, *from_hbm(gate_tiles, up_tiles), rest_a[0], near_a[-1])
    weights_b = [gate_b, up_b]
    far_b, near_b = to_owners(far_b), to_owners(near_b)

    out_tiles = shape(*gate_tiles.shape)
    gate_out, up_out, hidden_out, acc_near, acc_far = pl.pallas_call(
        functools.partial(first_half_kernel, shards, owners),
        out_shape=(
            out_tiles,
            out_tiles,
            shape(*d_hidden.shape),
            shape(row_blocks, near_rows, tile, dtype=F32),
            shape(row_blocks, row_total - near_rows, tile, dtype=F32),
        ),
        in_specs=[SMEM_SPEC] * 3
        + [ANY_SPEC] * 2
        + [VMEM_SPEC] * (1 + 2 * owners)
        + [ANY_SPEC] * (owners + 2),
        out_specs=(ANY_SPEC,) * 3 + (VMEM_SPEC,) * 2,
        scratch_shapes=[
            pltpu.VMEM((row_total, half * tile), BF16),
            pltpu.VMEM((row_total, half * tile), BF16),
            pltpu.VMEM((half, 1, slots, tile, tile), BF16),
            pltpu.VMEM((half, 1, slots, tile, tile), BF16),
            tile_shape(min(WINDOW + 1, half)),
            tile_shape(min(WINDOW + 1, half)),
            pltpu.SemaphoreType.DMA((2, half)),
            pltpu.SemaphoreType.DMA((shards,)),
            pltpu.SemaphoreType.DMA((d_hidden.shape[0] // shard_rows,)),
            pltpu.SemaphoreType.DMA((2, min(WINDOW + 1, half))),
        ],
        compiler_params=limit(16),
        cost_estimate=cost(row_total, half, 2, 1, 1),
        name="first_half",
    )(meta, *lists, *from_hbm(gate_tiles, up_tiles), *held([turned]), *near_a, *rest_a, *cots, far_b[0], near_b[0])

    def second_half(members, acc, parts, after):
        rows_here = len(members) * shard_rows
        return pl.pallas_call(
            functools.partial(second_half_kernel, members, owners, half),
            out_shape=(
                shape(rest, rows_here, 2 * tile),
                shape(rows_here, rest * tile),
                *[shape(shard_rows, width) for _ in members],
            ),
            in_specs=[SMEM_SPEC] * 3 + [VMEM_SPEC] * (3 + owners) + [ANY_SPEC] * (owners + 1),
            out_specs=(VMEM_SPEC,) * (2 + len(members)),
            scratch_shapes=[
                pltpu.VMEM((rows_here, rest * tile), BF16),
                pltpu.VMEM((row_blocks, rows_here, tile), F32),
                pltpu.SemaphoreType.DMA((len(members),)),
            ],
            compiler_params=limit(8),
            cost_estimate=cost(rows_here, rest, 1, 1, 1 if members[0] == 0 else 1),
            name="second_half",
        )(meta, *lists, *held(weights_b), acc, *parts, *cots, after)

    far_grads, far_hidden, *far_dxs = second_half(range(2, shards), acc_far, far_b, acc_near)
    both_cores = []
    for mine, others in zip(far_dxs[::2], far_dxs[1::2]):
        other = swap(others, "sub", 1)
        both_cores.append(
            pl.pallas_call(
                add_kernel,
                out_shape=shape(shard_rows, width),
                in_specs=[VMEM_SPEC] * 2,
                out_specs=VMEM_SPEC,
                compiler_params=limit(8),
                cost_estimate=pl.CostEstimate(flops=0, bytes_accessed=0, transcendentals=0),
                name="add_cores",
            )(mine, other)
        )
    back_far = [swap_far(total, base) for total, base in zip(both_cores, bases)]

    near_grads, near_hidden, own_dx, next_dx = second_half(range(2), acc_near, near_b, both_cores[-1])
    back_next = swap(next_dx, "tok", 1)

    def last_grads(start, stop, with_hidden, outs):
        count = stop - start
        return pl.pallas_call(
            functools.partial(last_grads_kernel, shards, half, start, with_hidden),
            out_shape=(out_tiles, out_tiles, shape(*d_hidden.shape), shape(8, tile, dtype=F32)),
            in_specs=[SMEM_SPEC] * 3 + [VMEM_SPEC] * 3 + [ANY_SPEC] * 5,
            out_specs=(ANY_SPEC,) * 3 + (VMEM_SPEC,),
            scratch_shapes=[
                pltpu.VMEM((count, 1, slots, tile, tile), BF16),
                pltpu.VMEM((count, 1, slots, tile, tile), BF16),
                pltpu.SemaphoreType.DMA((2, count)),
                pltpu.SemaphoreType.DMA((d_hidden.shape[0] // shard_rows,)),
            ],
            input_output_aliases={8: 0, 9: 1, 10: 2},
            compiler_params=limit(12),
            cost_estimate=cost(row_total, count, 1, 1, 10),
            name="last_grads",
        )(meta, *lists, *held([turned]), near_grads, far_grads, near_hidden, far_hidden, *outs)

    middle = rest
    *outs, token = last_grads(0, middle, True, (gate_out, up_out, hidden_out))
    arrived = [own_dx, back_next, *back_far]
    mine, mine_sent = pl.pallas_call(
        functools.partial(sum_kernel, len(arrived)),
        out_shape=(shape(shard_rows, width, dtype=F32), shape(shard_rows, width)),
        in_specs=[VMEM_SPEC] * len(arrived) + [ANY_SPEC],
        out_specs=(VMEM_SPEC,) * 2,
        compiler_params=limit(8),
        name="sum_shards",
    )(*arrived, token)
    if middle < rest:
        *outs, _ = last_grads(middle, rest, False, outs)
    gate_out, up_out, hidden_out = outs
    features_grad = (mine + swap(mine_sent, "sub", 1).astype(F32)).astype(BF16)
    return (hidden_out, gate_out, up_out, features_grad)


def solution(mesh):
    return jax.shard_map(
        on_device,
        mesh=mesh,
        in_specs=(
            P(("groups", "tok"), "blk"),
            P(("tok", "sub"), "blk", None, None, None),
            P(("tok", "sub"), "blk", None, None, None),
            P(("tok", "sub"), "blk", None),
            P(("tok", "sub"), "blk"),
            P(("groups", "blk"), ("tok", "sub")),
        ),
        out_specs=(
            P(("groups", "blk"), ("tok", "sub")),
            P(("groups", "tok", "sub"), "blk", None, None, None),
            P(("groups", "tok", "sub"), "blk", None, None, None),
            P(("groups", "tok"), "blk"),
        ),
        check_vma=False,
    )
```

```python
import functools

import jax
import jax.numpy as jnp
from jax import lax
from jax.experimental import pallas as pl
from jax.experimental.pallas import tpu as pltpu
from jax.sharding import PartitionSpec as P

F32 = jnp.float32
BF16 = jnp.bfloat16
MIB = 1 << 20
VMEM_SPEC = pl.BlockSpec(memory_space=pltpu.VMEM)
SMEM_SPEC = pl.BlockSpec(memory_space=pltpu.SMEM)
ANY_SPEC = pl.BlockSpec(memory_space=pl.ANY)


def limit(mib):
    return pltpu.CompilerParams(vmem_limit_bytes=mib * MIB)


def lanes(index, width):
    return pl.ds(pl.multiple_of(index * width, width), width)


def weights_of(c, gate_ref, up_ref):
    slots, rows, cols = gate_ref.shape[2:]
    return jnp.concatenate(
        [gate_ref[c, 0].reshape(slots * rows, cols), up_ref[c, 0].reshape(slots * rows, cols)], axis=1
    )


def keep(k, count, block):
    return jnp.where(k < count, block, jnp.zeros_like(block))


def forward_column(c, first, lists, xs, gate_ref, up_ref):
    rows_ref, counts_ref = lists
    slots, tile = gate_ref.shape[2:4]
    count = counts_ref[0, first + c]
    picked = []
    for k in range(slots):
        where = lanes(rows_ref[k, 0, first + c], tile)
        picked.append(keep(k, count, jnp.concatenate([x[:, where] for x in xs], axis=0)))
    return jnp.dot(
        jnp.concatenate(picked, axis=1), weights_of(c, gate_ref, up_ref), preferred_element_type=F32
    ).astype(BF16)


def groups_of(cols):
    edges = [0, -(-cols * 3 // 8), -(-cols * 6 // 8), cols]
    return [(start, stop) for start, stop in zip(edges, edges[1:]) if start < stop]


def load_tiles(first, cols, gate_hbm, up_hbm, gate_ref, up_ref, sems):
    def copies(i, start, stop):
        return [
            pltpu.make_async_copy(
                source.at[pl.ds(first + start, stop - start)], target.at[pl.ds(start, stop - start)], sems.at[j, i]
            )
            for j, (source, target) in enumerate(((gate_hbm, gate_ref), (up_hbm, up_ref)))
        ]

    started = {start: copies(i, start, stop) for i, (start, stop) in enumerate(groups_of(cols))}
    for group in started.values():
        for copy in group:
            copy.start()

    def arrive(c):
        for copy in started.get(c, ()):
            copy.wait()

    return arrive


def store_tiles(first, start, stop, i, gate_ref, up_ref, gate_hbm, up_hbm, sems):
    copies = [
        pltpu.make_async_copy(
            source.at[pl.ds(start, stop - start)], target.at[pl.ds(first + start, stop - start)], sems.at[j, i]
        )
        for j, (source, target) in enumerate(((gate_ref, gate_hbm), (up_ref, up_hbm)))
    ]
    for copy in copies:
        copy.start()
    return copies


def forward_own_kernel(x_hbm, rows_hbm, counts_hbm, gate_hbm, up_hbm, part_ref, *scratch):
    x_ref, rows_ref, counts_ref, gate_ref, up_ref, sems, small_sems = scratch
    cols = gate_ref.shape[0]
    small = [
        pltpu.make_async_copy(source, target, small_sems.at[i])
        for i, (source, target) in enumerate(((rows_hbm, rows_ref), (counts_hbm, counts_ref), (x_hbm, x_ref)))
    ]
    for copy in small:
        copy.start()
    arrive = load_tiles(0, cols, gate_hbm, up_hbm, gate_ref, up_ref, sems)
    for copy in small:
        copy.wait()
    for c in range(cols):
        arrive(c)
        part_ref[c] = forward_column(c, 0, (rows_ref, counts_ref), [x_ref], gate_ref, up_ref)


def forward_kernel(members, rows_ref, counts_ref, *refs):
    xs = refs[:members]
    gate_hbm, up_hbm = refs[members : members + 2]
    part_ref, gate_ref, up_ref, sems = refs[-4:]
    cols = gate_ref.shape[0]
    arrive = load_tiles(0, cols, gate_hbm, up_hbm, gate_ref, up_ref, sems)
    for c in range(cols):
        arrive(c)
        part_ref[c] = forward_column(c, 0, (rows_ref, counts_ref), xs, gate_ref, up_ref)


def load_forward_kernel(members, groups, first, turn, rows_ref, counts_ref, *refs):
    xs = refs[:members]
    gate_hbm, up_hbm = refs[members : members + 2]
    outs = refs[-(len(groups) + 3 + turn) :]
    parts, gate_ref, up_ref, sems = outs[: len(groups)], outs[-3 - turn], outs[-2 - turn], outs[-1]
    cols, _, _, tile, _ = gate_ref.shape
    arrive = load_tiles(first, cols, gate_hbm, up_hbm, gate_ref, up_ref, sems)
    if turn:
        turned_ref = outs[-2]
        identity = (
            lax.broadcasted_iota(jnp.int32, (tile, tile), 0) == lax.broadcasted_iota(jnp.int32, (tile, tile), 1)
        ).astype(F32).astype(BF16)
        for r in range(turned_ref.shape[0]):
            block = jnp.concatenate([x[:, r * tile : (r + 1) * tile] for x in xs], axis=0)
            turned_ref[r] = lax.dot_general(
                identity, block, (((1,), (1,)), ((), ())), preferred_element_type=F32
            ).astype(BF16)
    for c in range(cols):
        arrive(c)
        part = forward_column(c, first, (rows_ref, counts_ref), xs, gate_ref, up_ref)
        for (start, stop), part_ref in zip(groups, parts):
            part_ref[c] = part[start:stop]


def shard_of(member, meta_ref):
    if member < 2:
        return meta_ref[0] ^ member
    return meta_ref[0] ^ ((member & ~1) + ((member & 1) ^ meta_ref[2]))


def start_cots(members, first, meta_ref, cots, cot_ref, sems):
    count = len(members)
    shard_rows, width = cot_ref.shape[0] // count, cot_ref.shape[1]
    shards_each = cots[0].shape[0] // shard_rows

    def copy(i, cot, first_row):
        return pltpu.make_async_copy(
            cot.at[pl.ds(first_row, shard_rows), pl.ds(first, width)],
            cot_ref.at[pl.ds(i * shard_rows, shard_rows)],
            sems.at[i],
        )

    for i, member in enumerate(members):
        shard = shard_of(member, meta_ref)
        source = (shard // shards_each) ^ meta_ref[1]
        first_row = pl.multiple_of((shard % shards_each) * shard_rows, shard_rows)
        for j, cot in enumerate(cots):

            @pl.when(source == j)
            def _(i=i, cot=cot, first_row=first_row):
                copy(i, cot, first_row).start()

    return [copy(i, cots[0], 0) for i in range(count)]


def nonlinear(total, cotangent):
    tile = total.shape[1] // 2
    gate_value, up_value = total[:, :tile], total[:, tile:]
    sig_gate = jax.nn.sigmoid(gate_value)
    act_gate = gate_value * sig_gate
    hidden = (act_gate * up_value).astype(BF16)
    gate_grad = (cotangent * up_value * sig_gate * (1.0 + gate_value * (1.0 - sig_gate))).astype(BF16)
    up_grad = (cotangent * act_gate).astype(BF16)
    return hidden, jnp.concatenate([gate_grad, up_grad], axis=1)


def total_of(c, parts):
    total = parts[0][c].astype(F32)
    for part in parts[1:]:
        total = total + part[c].astype(F32)
    return total


def back_terms(c, grads, gate_ref, up_ref):
    return lax.dot_general(
        grads, weights_of(c, gate_ref, up_ref), (((1,), (1,)), ((), ())), preferred_element_type=F32
    )


def add_back(c, lists, back, accs, slots, tile):
    rows_ref, counts_ref = lists
    rows = [rows_ref[k, 0, c] for k in range(slots)]
    start = 0
    for acc in accs:
        stop = start + acc.shape[1]
        sums = [
            acc[rows[k]] + keep(k, counts_ref[0, c], back[start:stop, k * tile : (k + 1) * tile])
            for k in range(slots)
        ]
        for k in range(slots):
            acc[rows[k]] = sums[k]
        start = stop


def tile_grads(c, first, lists, turned_ref, grads, gate_ref, up_ref):
    rows_ref, counts_ref = lists
    slots, tile = gate_ref.shape[2:4]
    picked = jnp.concatenate([turned_ref[rows_ref[k, 0, first + c]] for k in range(slots)], axis=0)
    found = jnp.dot(picked, grads, preferred_element_type=F32)
    for k in range(slots):
        term = keep(k, counts_ref[0, first + c], found[k * tile : (k + 1) * tile]).astype(BF16)
        gate_ref[c, 0, k] = term[:, :tile]
        up_ref[c, 0, k] = term[:, tile:]


def start_hidden(members, first, meta_ref, source_of, hidden_hbm, shard_rows, sems):
    width = source_of(0).shape[1]
    shards_each = hidden_hbm.shape[0] // shard_rows

    def copy(i, member):
        return pltpu.make_async_copy(
            source_of(member), hidden_hbm.at[pl.ds(i * shard_rows, shard_rows), pl.ds(first, width)], sems.at[i]
        )

    for i in range(shards_each):
        wanted = meta_ref[1] * shards_each + i
        for member in members:

            @pl.when(shard_of(member, meta_ref) == wanted)
            def _(i=i, member=member):
                copy(i, member).start()

    return [copy(i, 0) for i in range(shards_each)]


def first_half_kernel(members, owners, meta_ref, rows_ref, counts_ref, gate_in, up_in, turned_ref, *refs):
    near, rest, cots = refs[:owners], refs[owners : 2 * owners], refs[2 * owners : 3 * owners]
    gate_hbm, up_hbm, hidden_hbm, acc_near, acc_far = refs[-15:-10]
    cot_ref, hidden_ref, gate_ref, up_ref, gate_w, up_w, sems, cot_sems, hidden_sems, load_sems = refs[-10:]
    cols, _, slots, tile, _ = gate_ref.shape
    arrive = load_tiles(0, cols, gate_in, up_in, gate_w, up_w, load_sems)
    shard_rows = cot_ref.shape[0] // members
    lists = (rows_ref, counts_ref)
    waits = start_cots(range(members), 0, meta_ref, cots, cot_ref, cot_sems)
    acc_near[...] = jnp.zeros_like(acc_near)
    acc_far[...] = jnp.zeros_like(acc_far)
    for wait in waits:
        wait.wait()
    copies = []
    for i, (start, stop) in enumerate(groups_of(cols)):
        arrive(start)
        for c in range(start, stop):
            total = jnp.concatenate([total_of(c, near), total_of(c, rest)], axis=0)
            where = slice(c * tile, (c + 1) * tile)
            hidden, grads = nonlinear(total, cot_ref[:, where].astype(F32))
            hidden_ref[:, where] = hidden
            tile_grads(c, 0, lists, turned_ref, grads, gate_ref, up_ref)
            add_back(c, lists, back_terms(c, grads, gate_w, up_w), (acc_near, acc_far), slots, tile)
        copies += store_tiles(0, start, stop, i, gate_ref, up_ref, gate_hbm, up_hbm, sems)
    waits = start_hidden(
        range(members),
        0,
        meta_ref,
        lambda m: hidden_ref.at[pl.ds(m * shard_rows, shard_rows)],
        hidden_hbm,
        shard_rows,
        hidden_sems,
    )
    for wait in copies + waits:
        wait.wait()


def second_half_kernel(members, owners, first, meta_ref, rows_ref, counts_ref, gate_w, up_w, acc_in, *refs):
    parts, cots = refs[:owners], refs[owners : 2 * owners]
    outs = refs[-(2 + len(members) + 3) :]
    grads_ref, hidden_ref = outs[:2]
    dxs = outs[2 : 2 + len(members)]
    cot_ref, acc_ref, cot_sems = outs[-3:]
    cols, _, slots, tile, _ = gate_w.shape
    shard_rows = cot_ref.shape[0] // len(members)
    waits = start_cots(members, first * tile, meta_ref, cots, cot_ref, cot_sems)
    acc_ref[...] = acc_in[...]
    for wait in waits:
        wait.wait()
    for c in range(cols):
        where = slice(c * tile, (c + 1) * tile)
        hidden, grads = nonlinear(total_of(c, parts), cot_ref[:, where].astype(F32))
        hidden_ref[:, where] = hidden
        grads_ref[c] = grads
        add_back(first + c, (rows_ref, counts_ref), back_terms(c, grads, gate_w, up_w), (acc_ref,), slots, tile)
    for r in range(acc_ref.shape[0]):
        block = acc_ref[r].astype(BF16)
        for m, dx in enumerate(dxs):
            dx[:, r * tile : (r + 1) * tile] = block[m * shard_rows : (m + 1) * shard_rows]


def last_grads_kernel(members, first, start, with_hidden, meta_ref, rows_ref, counts_ref, turned_ref, *refs):
    near_grads, far_grads, near_hidden, far_hidden = refs[:4]
    gate_hbm, up_hbm, hidden_hbm, token_ref, gate_ref, up_ref, sems, hidden_sems = refs[-8:]
    cols, _, _, tile, _ = gate_ref.shape
    shard_rows = near_hidden.shape[0] // 2
    token_ref[...] = jnp.zeros_like(token_ref)

    def hidden_of(m):
        if m < 2:
            return near_hidden.at[pl.ds(m * shard_rows, shard_rows)]
        return far_hidden.at[pl.ds((m - 2) * shard_rows, shard_rows)]

    waits = []
    if with_hidden:
        waits = start_hidden(
            range(members), first * tile, meta_ref, hidden_of, hidden_hbm, shard_rows, hidden_sems
        )
    for i, (begin, end) in enumerate(groups_of(cols)):
        for c in range(begin, end):
            grads = jnp.concatenate([near_grads[start + c], far_grads[start + c]], axis=0)
            tile_grads(c, first + start, (rows_ref, counts_ref), turned_ref, grads, gate_ref, up_ref)
        waits += store_tiles(first + start, begin, end, i, gate_ref, up_ref, gate_hbm, up_hbm, sems)
    for wait in waits:
        wait.wait()


def copy_kernel(x_ref, _, out_ref):
    out_ref[...] = x_ref[...]


def add_kernel(left_ref, right_ref, out_ref):
    out_ref[...] = (left_ref[...].astype(F32) + right_ref[...].astype(F32)).astype(BF16)


def sum_kernel(count, *refs):
    total = sum(ref[...].astype(F32) for ref in refs[:count])
    refs[-2][...] = total
    refs[-1][...] = total.astype(BF16)


def swap(x, axis, step):
    return lax.ppermute(x, axis, [(i, i ^ step) for i in range(lax.axis_size(axis))])


def swap_far(x, base):
    shards, cores = lax.axis_size("tok"), lax.axis_size("sub")
    pairs = [(t * cores + s, (t ^ (base + s)) * cores + s) for t in range(shards) for s in range(cores)]
    return lax.ppermute(x, ("tok", "sub"), pairs)


def on_device(features_in, gate_tiles, up_tiles, block_rows, block_counts, d_hidden):
    shards, owners = lax.axis_size("tok"), lax.axis_size("blk")
    cols, _, slots, tile, _ = gate_tiles.shape
    shard_rows, width = features_in.shape
    row_blocks = width // tile
    row_total = shards * shard_rows
    near_rows = 2 * shard_rows
    half = cols // 2
    bases = range(2, shards, 2)
    meta = jnp.stack([lax.axis_index("tok"), lax.axis_index("blk"), lax.axis_index("sub")]).astype(jnp.int32)
    lists = (jnp.transpose(block_rows, (2, 1, 0)), jnp.transpose(block_counts, (1, 0)))

    def held(weights):
        return [pltpu.with_memory_space_constraint(w, pltpu.VMEM) for w in weights]

    def shape(*dims, dtype=BF16):
        return jax.ShapeDtypeStruct(dims, dtype)

    def cost(tokens, columns, products, tile_bytes, weight=1):
        tiles = weight * columns * slots
        return pl.CostEstimate(
            flops=4 * tokens * tiles * tile * tile * products,
            bytes_accessed=4 * tiles * tile * tile * tile_bytes,
            transcendentals=0,
        )

    def to_owners(part):
        return [part] + [swap(part, "blk", s) for s in range(1, owners)]

    fars = [swap_far(features_in, base) for base in bases]
    xs = [features_in, swap(features_in, "tok", 1)]
    cots = [d_hidden] + [swap(d_hidden, "blk", s) for s in range(1, owners)]

    def tile_shape(columns):
        return pltpu.VMEM((columns, 1, slots, tile, tile), BF16)

    def from_hbm(*arrays):
        return [pltpu.with_memory_space_constraint(array, pltpu.HBM) for array in arrays]

    near_a = pl.pallas_call(
        forward_own_kernel,
        out_shape=shape(half, shard_rows, 2 * tile),
        in_specs=[ANY_SPEC] * 5,
        out_specs=VMEM_SPEC,
        scratch_shapes=[
            pltpu.VMEM((shard_rows, width), BF16),
            pltpu.SMEM(lists[0].shape, jnp.int32),
            pltpu.SMEM(lists[1].shape, jnp.int32),
            tile_shape(half),
            tile_shape(half),
            pltpu.SemaphoreType.DMA((2, 3)),
            pltpu.SemaphoreType.DMA((3,)),
        ],
        compiler_params=limit(12),
        cost_estimate=cost(shard_rows, half, 1, 1),
        name="forward_own_a",
    )(*from_hbm(features_in, *lists, gate_tiles, up_tiles))
    near_a = to_owners(near_a)

    for far in fars:
        ready = pl.pallas_call(
            copy_kernel,
            out_shape=shape(shard_rows, width),
            in_specs=[VMEM_SPEC, ANY_SPEC],
            out_specs=VMEM_SPEC,
            compiler_params=limit(8),
            cost_estimate=pl.CostEstimate(flops=0, bytes_accessed=0, transcendentals=0),
            name="after_own",
        )(far, near_a[0])
        xs += [far, swap(ready, "sub", 1)]

    rest_a = pl.pallas_call(
        functools.partial(forward_kernel, shards - 1),
        out_shape=shape(half, row_total - shard_rows, 2 * tile),
        in_specs=[SMEM_SPEC] * 2 + [VMEM_SPEC] * (shards - 1) + [ANY_SPEC] * 3,
        out_specs=VMEM_SPEC,
        scratch_shapes=[tile_shape(half), tile_shape(half), pltpu.SemaphoreType.DMA((2, 3))],
        compiler_params=limit(12),
        cost_estimate=cost(row_total, half, 1, 1),
        name="forward_rest_a",
    )(*lists, *xs[1:], *from_hbm(gate_tiles, up_tiles), cots[-1])
    rest_a = to_owners(rest_a)

    rest = cols - half
    far_b, near_b, gate_b, up_b, turned = pl.pallas_call(
        functools.partial(load_forward_kernel, shards, ((near_rows, row_total), (0, near_rows)), half, 1),
        out_shape=(
            shape(rest, row_total - near_rows, 2 * tile),
            shape(rest, near_rows, 2 * tile),
            tile_shape(rest),
            tile_shape(rest),
            pltpu.VMEM((row_blocks, tile, row_total), BF16),
        ),
        in_specs=[SMEM_SPEC] * 2 + [VMEM_SPEC] * shards + [ANY_SPEC] * 4,
        out_specs=(VMEM_SPEC,) * 5,
        scratch_shapes=[pltpu.SemaphoreType.DMA((2, 3))],
        compiler_params=limit(8),
        cost_estimate=cost(row_total, rest, 1, 1, 5),
        name="forward_b",
    )(*lists, *xs, *from_hbm(gate_tiles, up_tiles), rest_a[0], near_a[-1])
    weights_b = [gate_b, up_b]
    far_b, near_b = to_owners(far_b), to_owners(near_b)

    out_tiles = shape(*gate_tiles.shape)
    gate_out, up_out, hidden_out, acc_near, acc_far = pl.pallas_call(
        functools.partial(first_half_kernel, shards, owners),
        out_shape=(
            out_tiles,
            out_tiles,
            shape(*d_hidden.shape),
            shape(row_blocks, near_rows, tile, dtype=F32),
            shape(row_blocks, row_total - near_rows, tile, dtype=F32),
        ),
        in_specs=[SMEM_SPEC] * 3
        + [ANY_SPEC] * 2
        + [VMEM_SPEC] * (1 + 2 * owners)
        + [ANY_SPEC] * (owners + 2),
        out_specs=(ANY_SPEC,) * 3 + (VMEM_SPEC,) * 2,
        scratch_shapes=[
            pltpu.VMEM((row_total, half * tile), BF16),
            pltpu.VMEM((row_total, half * tile), BF16),
            pltpu.VMEM((half, 1, slots, tile, tile), BF16),
            pltpu.VMEM((half, 1, slots, tile, tile), BF16),
            tile_shape(half),
            tile_shape(half),
            pltpu.SemaphoreType.DMA((2, 3)),
            pltpu.SemaphoreType.DMA((shards,)),
            pltpu.SemaphoreType.DMA((d_hidden.shape[0] // shard_rows,)),
            pltpu.SemaphoreType.DMA((2, 3)),
        ],
        compiler_params=limit(20),
        cost_estimate=cost(row_total, half, 2, 1, 1),
        name="first_half",
    )(meta, *lists, *from_hbm(gate_tiles, up_tiles), *held([turned]), *near_a, *rest_a, *cots, far_b[0], near_b[0])

    def second_half(members, acc, parts, after):
        rows_here = len(members) * shard_rows
        return pl.pallas_call(
            functools.partial(second_half_kernel, members, owners, half),
            out_shape=(
                shape(rest, rows_here, 2 * tile),
                shape(rows_here, rest * tile),
                *[shape(shard_rows, width) for _ in members],
            ),
            in_specs=[SMEM_SPEC] * 3 + [VMEM_SPEC] * (3 + owners) + [ANY_SPEC] * (owners + 1),
            out_specs=(VMEM_SPEC,) * (2 + len(members)),
            scratch_shapes=[
                pltpu.VMEM((rows_here, rest * tile), BF16),
                pltpu.VMEM((row_blocks, rows_here, tile), F32),
                pltpu.SemaphoreType.DMA((len(members),)),
            ],
            compiler_params=limit(8),
            cost_estimate=cost(rows_here, rest, 1, 1, 1 if members[0] == 0 else 1),
            name="second_half",
        )(meta, *lists, *held(weights_b), acc, *parts, *cots, after)

    far_grads, far_hidden, *far_dxs = second_half(range(2, shards), acc_far, far_b, acc_near)
    both_cores = []
    for mine, others in zip(far_dxs[::2], far_dxs[1::2]):
        other = swap(others, "sub", 1)
        both_cores.append(
            pl.pallas_call(
                add_kernel,
                out_shape=shape(shard_rows, width),
                in_specs=[VMEM_SPEC] * 2,
                out_specs=VMEM_SPEC,
                compiler_params=limit(8),
                cost_estimate=pl.CostEstimate(flops=0, bytes_accessed=0, transcendentals=0),
                name="add_cores",
            )(mine, other)
        )
    back_far = [swap_far(total, base) for total, base in zip(both_cores, bases)]

    near_grads, near_hidden, own_dx, next_dx = second_half(range(2), acc_near, near_b, both_cores[-1])
    back_next = swap(next_dx, "tok", 1)

    def last_grads(start, stop, with_hidden, outs):
        count = stop - start
        return pl.pallas_call(
            functools.partial(last_grads_kernel, shards, half, start, with_hidden),
            out_shape=(out_tiles, out_tiles, shape(*d_hidden.shape), shape(8, tile, dtype=F32)),
            in_specs=[SMEM_SPEC] * 3 + [VMEM_SPEC] * 3 + [ANY_SPEC] * 5,
            out_specs=(ANY_SPEC,) * 3 + (VMEM_SPEC,),
            scratch_shapes=[
                pltpu.VMEM((count, 1, slots, tile, tile), BF16),
                pltpu.VMEM((count, 1, slots, tile, tile), BF16),
                pltpu.SemaphoreType.DMA((2, 3)),
                pltpu.SemaphoreType.DMA((d_hidden.shape[0] // shard_rows,)),
            ],
            input_output_aliases={8: 0, 9: 1, 10: 2},
            compiler_params=limit(12),
            cost_estimate=cost(row_total, count, 1, 1, 10),
            name="last_grads",
        )(meta, *lists, *held([turned]), near_grads, far_grads, near_hidden, far_hidden, *outs)

    middle = rest
    *outs, token = last_grads(0, middle, True, (gate_out, up_out, hidden_out))
    arrived = [own_dx, back_next, *back_far]
    mine, mine_sent = pl.pallas_call(
        functools.partial(sum_kernel, len(arrived)),
        out_shape=(shape(shard_rows, width, dtype=F32), shape(shard_rows, width)),
        in_specs=[VMEM_SPEC] * len(arrived) + [ANY_SPEC],
        out_specs=(VMEM_SPEC,) * 2,
        compiler_params=limit(8),
        name="sum_shards",
    )(*arrived, token)
    if middle < rest:
        *outs, _ = last_grads(middle, rest, False, outs)
    gate_out, up_out, hidden_out = outs
    features_grad = (mine + swap(mine_sent, "sub", 1).astype(F32)).astype(BF16)
    return (hidden_out, gate_out, up_out, features_grad)


def solution(mesh):
    return jax.shard_map(
        on_device,
        mesh=mesh,
        in_specs=(
            P(("groups", "tok"), "blk"),
            P(("tok", "sub"), "blk", None, None, None),
            P(("tok", "sub"), "blk", None, None, None),
            P(("tok", "sub"), "blk", None),
            P(("tok", "sub"), "blk"),
            P(("groups", "blk"), ("tok", "sub")),
        ),
        out_specs=(
            P(("groups", "blk"), ("tok", "sub")),
            P(("groups", "tok", "sub"), "blk", None, None, None),
            P(("groups", "tok", "sub"), "blk", None, None, None),
            P(("groups", "tok"), "blk"),
        ),
        check_vma=False,
    )
```

```python
import functools

import jax
import jax.numpy as jnp
from jax import lax
from jax.experimental import pallas as pl
from jax.experimental.pallas import tpu as pltpu
from jax.sharding import PartitionSpec as P

F32 = jnp.float32
BF16 = jnp.bfloat16
MIB = 1 << 20
VMEM_SPEC = pl.BlockSpec(memory_space=pltpu.VMEM)
SMEM_SPEC = pl.BlockSpec(memory_space=pltpu.SMEM)
ANY_SPEC = pl.BlockSpec(memory_space=pl.ANY)


def limit(mib):
    return pltpu.CompilerParams(vmem_limit_bytes=mib * MIB)


def lanes(index, width):
    return pl.ds(pl.multiple_of(index * width, width), width)


def weights_of(c, gate_ref, up_ref):
    slots, rows, cols = gate_ref.shape[2:]
    return jnp.concatenate(
        [gate_ref[c, 0].reshape(slots * rows, cols), up_ref[c, 0].reshape(slots * rows, cols)], axis=1
    )


def keep(k, count, block):
    return jnp.where(k < count, block, jnp.zeros_like(block))


def forward_column(c, first, lists, xs, gate_ref, up_ref):
    rows_ref, counts_ref = lists
    slots, tile = gate_ref.shape[2:4]
    count = counts_ref[0, first + c]
    picked = []
    for k in range(slots):
        where = lanes(rows_ref[k, 0, first + c], tile)
        picked.append(keep(k, count, jnp.concatenate([x[:, where] for x in xs], axis=0)))
    return jnp.dot(
        jnp.concatenate(picked, axis=1), weights_of(c, gate_ref, up_ref), preferred_element_type=F32
    ).astype(BF16)


def groups_of(cols):
    edges = [0, -(-cols * 3 // 8), -(-cols * 6 // 8), cols]
    return [(start, stop) for start, stop in zip(edges, edges[1:]) if start < stop]


def load_tiles(first, cols, gate_hbm, up_hbm, gate_ref, up_ref, sems):
    def copies(i, start, stop):
        return [
            pltpu.make_async_copy(
                source.at[pl.ds(first + start, stop - start)], target.at[pl.ds(start, stop - start)], sems.at[j, i]
            )
            for j, (source, target) in enumerate(((gate_hbm, gate_ref), (up_hbm, up_ref)))
        ]

    started = {start: copies(i, start, stop) for i, (start, stop) in enumerate(groups_of(cols))}
    for group in started.values():
        for copy in group:
            copy.start()

    def arrive(c):
        for copy in started.get(c, ()):
            copy.wait()

    return arrive


def store_tiles(first, c, gate_ref, up_ref, gate_hbm, up_hbm, sems):
    copies = [
        pltpu.make_async_copy(gate_ref.at[c], gate_hbm.at[first + c], sems.at[0, c]),
        pltpu.make_async_copy(up_ref.at[c], up_hbm.at[first + c], sems.at[1, c]),
    ]
    for copy in copies:
        copy.start()
    return copies


def forward_own_kernel(x_hbm, rows_hbm, counts_hbm, gate_hbm, up_hbm, part_ref, gate_ref, up_ref, *scratch):
    x_ref, rows_ref, counts_ref, sems, small_sems = scratch
    cols = gate_ref.shape[0]
    small = [
        pltpu.make_async_copy(source, target, small_sems.at[i])
        for i, (source, target) in enumerate(((rows_hbm, rows_ref), (counts_hbm, counts_ref), (x_hbm, x_ref)))
    ]
    for copy in small:
        copy.start()
    arrive = load_tiles(0, cols, gate_hbm, up_hbm, gate_ref, up_ref, sems)
    for copy in small:
        copy.wait()
    for c in range(cols):
        arrive(c)
        part_ref[c] = forward_column(c, 0, (rows_ref, counts_ref), [x_ref], gate_ref, up_ref)


def forward_kernel(members, rows_ref, counts_ref, *refs):
    xs = refs[:members]
    gate_ref, up_ref = refs[members : members + 2]
    part_ref = refs[-1]
    for c in range(gate_ref.shape[0]):
        part_ref[c] = forward_column(c, 0, (rows_ref, counts_ref), xs, gate_ref, up_ref)


def load_forward_kernel(members, groups, first, turn, rows_ref, counts_ref, *refs):
    xs = refs[:members]
    gate_hbm, up_hbm = refs[members : members + 2]
    outs = refs[-(len(groups) + 3 + turn) :]
    parts, gate_ref, up_ref, sems = outs[: len(groups)], outs[-3 - turn], outs[-2 - turn], outs[-1]
    cols, _, _, tile, _ = gate_ref.shape
    arrive = load_tiles(first, cols, gate_hbm, up_hbm, gate_ref, up_ref, sems)
    if turn:
        turned_ref = outs[-2]
        identity = (
            lax.broadcasted_iota(jnp.int32, (tile, tile), 0) == lax.broadcasted_iota(jnp.int32, (tile, tile), 1)
        ).astype(F32).astype(BF16)
        for r in range(turned_ref.shape[0]):
            block = jnp.concatenate([x[:, r * tile : (r + 1) * tile] for x in xs], axis=0)
            turned_ref[r] = lax.dot_general(
                identity, block, (((1,), (1,)), ((), ())), preferred_element_type=F32
            ).astype(BF16)
    for c in range(cols):
        arrive(c)
        part = forward_column(c, first, (rows_ref, counts_ref), xs, gate_ref, up_ref)
        for (start, stop), part_ref in zip(groups, parts):
            part_ref[c] = part[start:stop]


def shard_of(member):
    if member < 2:
        return lax.axis_index("tok") ^ member
    return lax.axis_index("tok") ^ ((member & ~1) + ((member & 1) ^ lax.axis_index("sub")))


def start_cots(members, first, cots, cot_ref, sems):
    count = len(members)
    shard_rows, width = cot_ref.shape[0] // count, cot_ref.shape[1]
    shards_each = cots[0].shape[0] // shard_rows

    def copy(i, cot, first_row):
        return pltpu.make_async_copy(
            cot.at[pl.ds(first_row, shard_rows), pl.ds(first, width)],
            cot_ref.at[pl.ds(i * shard_rows, shard_rows)],
            sems.at[i],
        )

    for i, member in enumerate(members):
        shard = shard_of(member)
        source = (shard // shards_each) ^ lax.axis_index("blk")
        first_row = pl.multiple_of((shard % shards_each) * shard_rows, shard_rows)
        for j, cot in enumerate(cots):

            @pl.when(source == j)
            def _(i=i, cot=cot, first_row=first_row):
                copy(i, cot, first_row).start()

    return [copy(i, cots[0], 0) for i in range(count)]


def nonlinear(total, cotangent):
    tile = total.shape[1] // 2
    gate_value, up_value = total[:, :tile], total[:, tile:]
    sig_gate = jax.nn.sigmoid(gate_value)
    act_gate = gate_value * sig_gate
    hidden = (act_gate * up_value).astype(BF16)
    gate_grad = (cotangent * up_value * sig_gate * (1.0 + gate_value * (1.0 - sig_gate))).astype(BF16)
    up_grad = (cotangent * act_gate).astype(BF16)
    return hidden, jnp.concatenate([gate_grad, up_grad], axis=1)


def total_of(c, parts):
    total = parts[0][c].astype(F32)
    for part in parts[1:]:
        total = total + part[c].astype(F32)
    return total


def back_terms(c, grads, gate_ref, up_ref):
    return lax.dot_general(
        grads, weights_of(c, gate_ref, up_ref), (((1,), (1,)), ((), ())), preferred_element_type=F32
    )


def add_back(c, lists, back, accs, slots, tile):
    rows_ref, counts_ref = lists
    rows = [rows_ref[k, 0, c] for k in range(slots)]
    start = 0
    for acc in accs:
        stop = start + acc.shape[1]
        sums = [
            acc[rows[k]] + keep(k, counts_ref[0, c], back[start:stop, k * tile : (k + 1) * tile])
            for k in range(slots)
        ]
        for k in range(slots):
            acc[rows[k]] = sums[k]
        start = stop


def tile_grads(c, first, lists, turned_ref, grads, gate_ref, up_ref):
    rows_ref, counts_ref = lists
    slots, tile = gate_ref.shape[2:4]
    picked = jnp.concatenate([turned_ref[rows_ref[k, 0, first + c]] for k in range(slots)], axis=0)
    found = jnp.dot(picked, grads, preferred_element_type=F32)
    for k in range(slots):
        term = keep(k, counts_ref[0, first + c], found[k * tile : (k + 1) * tile]).astype(BF16)
        gate_ref[c, 0, k] = term[:, :tile]
        up_ref[c, 0, k] = term[:, tile:]


def start_hidden(members, first, source_of, hidden_hbm, shard_rows, sems):
    width = source_of(0).shape[1]
    shards_each = hidden_hbm.shape[0] // shard_rows

    def copy(i, member):
        return pltpu.make_async_copy(
            source_of(member), hidden_hbm.at[pl.ds(i * shard_rows, shard_rows), pl.ds(first, width)], sems.at[i]
        )

    for i in range(shards_each):
        wanted = lax.axis_index("blk") * shards_each + i
        for member in members:

            @pl.when(shard_of(member) == wanted)
            def _(i=i, member=member):
                copy(i, member).start()

    return [copy(i, 0) for i in range(shards_each)]


def first_half_kernel(members, owners, rows_ref, counts_ref, gate_w, up_w, turned_ref, *refs):
    near, rest, cots = refs[:owners], refs[owners : 2 * owners], refs[2 * owners : 3 * owners]
    gate_hbm, up_hbm, hidden_hbm, acc_near, acc_far = refs[-12:-7]
    cot_ref, hidden_ref, gate_ref, up_ref, sems, cot_sems, hidden_sems = refs[-7:]
    cols, _, slots, tile, _ = gate_ref.shape
    shard_rows = cot_ref.shape[0] // members
    lists = (rows_ref, counts_ref)
    waits = start_cots(range(members), 0, cots, cot_ref, cot_sems)
    acc_near[...] = jnp.zeros_like(acc_near)
    acc_far[...] = jnp.zeros_like(acc_far)
    for wait in waits:
        wait.wait()
    copies = []
    for c in range(cols):
        total = jnp.concatenate([total_of(c, near), total_of(c, rest)], axis=0)
        where = slice(c * tile, (c + 1) * tile)
        hidden, grads = nonlinear(total, cot_ref[:, where].astype(F32))
        hidden_ref[:, where] = hidden
        tile_grads(c, 0, lists, turned_ref, grads, gate_ref, up_ref)
        copies += store_tiles(0, c, gate_ref, up_ref, gate_hbm, up_hbm, sems)
        add_back(c, lists, back_terms(c, grads, gate_w, up_w), (acc_near, acc_far), slots, tile)
    waits = start_hidden(
        range(members),
        0,
        lambda m: hidden_ref.at[pl.ds(m * shard_rows, shard_rows)],
        hidden_hbm,
        shard_rows,
        hidden_sems,
    )
    for wait in copies + waits:
        wait.wait()


def second_half_kernel(members, owners, first, rows_ref, counts_ref, gate_w, up_w, acc_in, *refs):
    parts, cots = refs[:owners], refs[owners : 2 * owners]
    outs = refs[-(2 + len(members) + 3) :]
    grads_ref, hidden_ref = outs[:2]
    dxs = outs[2 : 2 + len(members)]
    cot_ref, acc_ref, cot_sems = outs[-3:]
    cols, _, slots, tile, _ = gate_w.shape
    shard_rows = cot_ref.shape[0] // len(members)
    waits = start_cots(members, first * tile, cots, cot_ref, cot_sems)
    acc_ref[...] = acc_in[...]
    for wait in waits:
        wait.wait()
    for c in range(cols):
        where = slice(c * tile, (c + 1) * tile)
        hidden, grads = nonlinear(total_of(c, parts), cot_ref[:, where].astype(F32))
        hidden_ref[:, where] = hidden
        grads_ref[c] = grads
        add_back(first + c, (rows_ref, counts_ref), back_terms(c, grads, gate_w, up_w), (acc_ref,), slots, tile)
    for r in range(acc_ref.shape[0]):
        block = acc_ref[r].astype(BF16)
        for m, dx in enumerate(dxs):
            dx[:, r * tile : (r + 1) * tile] = block[m * shard_rows : (m + 1) * shard_rows]


def last_grads_kernel(members, first, start, with_hidden, rows_ref, counts_ref, turned_ref, *refs):
    near_grads, far_grads, near_hidden, far_hidden = refs[:4]
    gate_hbm, up_hbm, hidden_hbm, token_ref, gate_ref, up_ref, sems, hidden_sems = refs[-8:]
    cols, _, _, tile, _ = gate_ref.shape
    shard_rows = near_hidden.shape[0] // 2
    token_ref[...] = jnp.zeros_like(token_ref)

    def hidden_of(m):
        if m < 2:
            return near_hidden.at[pl.ds(m * shard_rows, shard_rows)]
        return far_hidden.at[pl.ds((m - 2) * shard_rows, shard_rows)]

    waits = []
    if with_hidden:
        waits = start_hidden(
            range(members), first * tile, hidden_of, hidden_hbm, shard_rows, hidden_sems
        )
    for c in range(cols):
        grads = jnp.concatenate([near_grads[start + c], far_grads[start + c]], axis=0)
        tile_grads(c, first + start, (rows_ref, counts_ref), turned_ref, grads, gate_ref, up_ref)
        waits += store_tiles(first + start, c, gate_ref, up_ref, gate_hbm, up_hbm, sems)
    for wait in waits:
        wait.wait()


def copy_kernel(x_ref, _, out_ref):
    out_ref[...] = x_ref[...]


def add_kernel(left_ref, right_ref, out_ref):
    out_ref[...] = (left_ref[...].astype(F32) + right_ref[...].astype(F32)).astype(BF16)


def sum_kernel(count, *refs):
    total = sum(ref[...].astype(F32) for ref in refs[:count])
    refs[-2][...] = total
    refs[-1][...] = total.astype(BF16)


def swap(x, axis, step):
    return lax.ppermute(x, axis, [(i, i ^ step) for i in range(lax.axis_size(axis))])


def swap_far(x, base):
    shards, cores = lax.axis_size("tok"), lax.axis_size("sub")
    pairs = [(t * cores + s, (t ^ (base + s)) * cores + s) for t in range(shards) for s in range(cores)]
    return lax.ppermute(x, ("tok", "sub"), pairs)


def on_device(features_in, gate_tiles, up_tiles, block_rows, block_counts, d_hidden):
    shards, owners = lax.axis_size("tok"), lax.axis_size("blk")
    cols, _, slots, tile, _ = gate_tiles.shape
    shard_rows, width = features_in.shape
    row_blocks = width // tile
    row_total = shards * shard_rows
    near_rows = 2 * shard_rows
    half = max(1, cols * 3 // 8)
    bases = range(2, shards, 2)
    lists = (jnp.transpose(block_rows, (2, 1, 0)), jnp.transpose(block_counts, (1, 0)))

    def shape(*dims, dtype=BF16):
        return jax.ShapeDtypeStruct(dims, dtype)

    def cost(tokens, columns, products, tile_bytes, weight=1):
        tiles = weight * columns * slots
        return pl.CostEstimate(
            flops=4 * tokens * tiles * tile * tile * products,
            bytes_accessed=4 * tiles * tile * tile * tile_bytes,
            transcendentals=0,
        )

    def to_owners(part):
        return [part] + [swap(part, "blk", s) for s in range(1, owners)]

    fars = [swap_far(features_in, base) for base in bases]
    xs = [features_in, swap(features_in, "tok", 1)]
    cots = [d_hidden] + [swap(d_hidden, "blk", s) for s in range(1, owners)]

    def tile_shape(columns):
        return pltpu.VMEM((columns, 1, slots, tile, tile), BF16)

    def from_hbm(*arrays):
        return [pltpu.with_memory_space_constraint(array, pltpu.HBM) for array in arrays]

    near_a, *weights_a = pl.pallas_call(
        forward_own_kernel,
        out_shape=(shape(half, shard_rows, 2 * tile), tile_shape(half), tile_shape(half)),
        in_specs=[ANY_SPEC] * 5,
        out_specs=(VMEM_SPEC,) * 3,
        scratch_shapes=[
            pltpu.VMEM((shard_rows, width), BF16),
            pltpu.SMEM(lists[0].shape, jnp.int32),
            pltpu.SMEM(lists[1].shape, jnp.int32),
            pltpu.SemaphoreType.DMA((2, 3)),
            pltpu.SemaphoreType.DMA((3,)),
        ],
        compiler_params=limit(8),
        cost_estimate=cost(shard_rows, half, 1, 1),
        name="forward_own_a",
    )(*from_hbm(features_in, *lists, gate_tiles, up_tiles))
    near_a = to_owners(near_a)

    for far in fars:
        ready = pl.pallas_call(
            copy_kernel,
            out_shape=shape(shard_rows, width),
            in_specs=[VMEM_SPEC, ANY_SPEC],
            out_specs=VMEM_SPEC,
            compiler_params=limit(8),
            cost_estimate=pl.CostEstimate(flops=0, bytes_accessed=0, transcendentals=0),
            name="after_own",
        )(far, near_a[0])
        xs += [far, swap(ready, "sub", 1)]

    rest_a = pl.pallas_call(
        functools.partial(forward_kernel, shards - 1),
        out_shape=shape(half, row_total - shard_rows, 2 * tile),
        in_specs=[SMEM_SPEC] * 2 + [VMEM_SPEC] * (shards + 1) + [ANY_SPEC],
        out_specs=VMEM_SPEC,
        compiler_params=limit(8),
        cost_estimate=cost(row_total, half, 1, 1),
        name="forward_rest_a",
    )(*lists, *xs[1:], *weights_a, cots[-1])
    rest_a = to_owners(rest_a)

    rest = cols - half
    far_b, near_b, gate_b, up_b, turned = pl.pallas_call(
        functools.partial(load_forward_kernel, shards, ((near_rows, row_total), (0, near_rows)), half, 1),
        out_shape=(
            shape(rest, row_total - near_rows, 2 * tile),
            shape(rest, near_rows, 2 * tile),
            tile_shape(rest),
            tile_shape(rest),
            pltpu.VMEM((row_blocks, tile, row_total), BF16),
        ),
        in_specs=[SMEM_SPEC] * 2 + [VMEM_SPEC] * shards + [ANY_SPEC] * 4,
        out_specs=(VMEM_SPEC,) * 5,
        scratch_shapes=[pltpu.SemaphoreType.DMA((2, 3))],
        compiler_params=limit(8),
        cost_estimate=cost(row_total, rest, 1, 1, 5),
        name="forward_b",
    )(*lists, *xs, *from_hbm(gate_tiles, up_tiles), rest_a[0], near_a[-1])
    weights_b = [gate_b, up_b]
    far_b, near_b = to_owners(far_b), to_owners(near_b)

    out_tiles = shape(*gate_tiles.shape)
    gate_out, up_out, hidden_out, acc_near, acc_far = pl.pallas_call(
        functools.partial(first_half_kernel, shards, owners),
        out_shape=(
            out_tiles,
            out_tiles,
            shape(*d_hidden.shape),
            shape(row_blocks, near_rows, tile, dtype=F32),
            shape(row_blocks, row_total - near_rows, tile, dtype=F32),
        ),
        in_specs=[SMEM_SPEC] * 2 + [VMEM_SPEC] * (3 + 2 * owners) + [ANY_SPEC] * (owners + 2),
        out_specs=(ANY_SPEC,) * 3 + (VMEM_SPEC,) * 2,
        scratch_shapes=[
            pltpu.VMEM((row_total, half * tile), BF16),
            pltpu.VMEM((row_total, half * tile), BF16),
            tile_shape(half),
            tile_shape(half),
            pltpu.SemaphoreType.DMA((2, half)),
            pltpu.SemaphoreType.DMA((shards,)),
            pltpu.SemaphoreType.DMA((d_hidden.shape[0] // shard_rows,)),
        ],
        compiler_params=limit(8 + 2 * half * slots * tile * tile * 2 // MIB),
        cost_estimate=cost(row_total, half, 2, 1, 1),
        name="first_half",
    )(*lists, *weights_a, turned, *near_a, *rest_a, *cots, far_b[0], near_b[0])

    def second_half(members, acc, parts, after):
        rows_here = len(members) * shard_rows
        return pl.pallas_call(
            functools.partial(second_half_kernel, members, owners, half),
            out_shape=(
                shape(rest, rows_here, 2 * tile),
                shape(rows_here, rest * tile),
                *[shape(shard_rows, width) for _ in members],
            ),
            in_specs=[SMEM_SPEC] * 2 + [VMEM_SPEC] * (3 + owners) + [ANY_SPEC] * (owners + 1),
            out_specs=(VMEM_SPEC,) * (2 + len(members)),
            scratch_shapes=[
                pltpu.VMEM((rows_here, rest * tile), BF16),
                pltpu.VMEM((row_blocks, rows_here, tile), F32),
                pltpu.SemaphoreType.DMA((len(members),)),
            ],
            compiler_params=limit(8),
            cost_estimate=cost(rows_here, rest, 1, 1, 1 if members[0] == 0 else 1),
            name="second_half",
        )(*lists, *weights_b, acc, *parts, *cots, after)

    far_grads, far_hidden, *far_dxs = second_half(range(2, shards), acc_far, far_b, acc_near)
    both_cores = []
    for mine, others in zip(far_dxs[::2], far_dxs[1::2]):
        other = swap(others, "sub", 1)
        both_cores.append(
            pl.pallas_call(
                add_kernel,
                out_shape=shape(shard_rows, width),
                in_specs=[VMEM_SPEC] * 2,
                out_specs=VMEM_SPEC,
                compiler_params=limit(8),
                cost_estimate=pl.CostEstimate(flops=0, bytes_accessed=0, transcendentals=0),
                name="add_cores",
            )(mine, other)
        )
    back_far = [swap_far(total, base) for total, base in zip(both_cores, bases)]

    near_grads, near_hidden, own_dx, next_dx = second_half(range(2), acc_near, near_b, both_cores[-1])
    back_next = swap(next_dx, "tok", 1)

    def last_grads(start, stop, with_hidden, outs):
        count = stop - start
        return pl.pallas_call(
            functools.partial(last_grads_kernel, shards, half, start, with_hidden),
            out_shape=(out_tiles, out_tiles, shape(*d_hidden.shape), shape(8, tile, dtype=F32)),
            in_specs=[SMEM_SPEC] * 2 + [VMEM_SPEC] * 3 + [ANY_SPEC] * 5,
            out_specs=(ANY_SPEC,) * 3 + (VMEM_SPEC,),
            scratch_shapes=[
                pltpu.VMEM((count, 1, slots, tile, tile), BF16),
                pltpu.VMEM((count, 1, slots, tile, tile), BF16),
                pltpu.SemaphoreType.DMA((2, count)),
                pltpu.SemaphoreType.DMA((d_hidden.shape[0] // shard_rows,)),
            ],
            input_output_aliases={7: 0, 8: 1, 9: 2},
            compiler_params=limit(8 + 2 * count * slots * tile * tile * 2 // MIB),
            cost_estimate=cost(row_total, count, 1, 1, 10),
            name="last_grads",
        )(*lists, turned, near_grads, far_grads, near_hidden, far_hidden, *outs)

    middle = rest
    *outs, token = last_grads(0, middle, True, (gate_out, up_out, hidden_out))
    arrived = [own_dx, back_next, *back_far]
    mine, mine_sent = pl.pallas_call(
        functools.partial(sum_kernel, len(arrived)),
        out_shape=(shape(shard_rows, width, dtype=F32), shape(shard_rows, width)),
        in_specs=[VMEM_SPEC] * len(arrived) + [ANY_SPEC],
        out_specs=(VMEM_SPEC,) * 2,
        compiler_params=limit(8),
        name="sum_shards",
    )(*arrived, token)
    if middle < rest:
        *outs, _ = last_grads(middle, rest, False, outs)
    gate_out, up_out, hidden_out = outs
    features_grad = (mine + swap(mine_sent, "sub", 1).astype(F32)).astype(BF16)
    return (hidden_out, gate_out, up_out, features_grad)


def solution(mesh):
    return jax.shard_map(
        on_device,
        mesh=mesh,
        in_specs=(
            P(("groups", "tok"), "blk"),
            P(("tok", "sub"), "blk", None, None, None),
            P(("tok", "sub"), "blk", None, None, None),
            P(("tok", "sub"), "blk", None),
            P(("tok", "sub"), "blk"),
            P(("groups", "blk"), ("tok", "sub")),
        ),
        out_specs=(
            P(("groups", "blk"), ("tok", "sub")),
            P(("groups", "tok", "sub"), "blk", None, None, None),
            P(("groups", "tok", "sub"), "blk", None, None, None),
            P(("groups", "tok"), "blk"),
        ),
        check_vma=False,
    )
```

```python
import functools

import jax
import jax.numpy as jnp
from jax import lax
from jax.experimental import pallas as pl
from jax.experimental.pallas import tpu as pltpu
from jax.sharding import PartitionSpec as P

F32 = jnp.float32
BF16 = jnp.bfloat16
MIB = 1 << 20
VMEM_SPEC = pl.BlockSpec(memory_space=pltpu.VMEM)
SMEM_SPEC = pl.BlockSpec(memory_space=pltpu.SMEM)
ANY_SPEC = pl.BlockSpec(memory_space=pl.ANY)


def limit(mib):
    return pltpu.CompilerParams(vmem_limit_bytes=mib * MIB)


def lanes(index, width):
    return pl.ds(pl.multiple_of(index * width, width), width)


def weights_of(c, gate_ref, up_ref):
    slots, rows, cols = gate_ref.shape[2:]
    return jnp.concatenate(
        [gate_ref[c, 0].reshape(slots * rows, cols), up_ref[c, 0].reshape(slots * rows, cols)], axis=1
    )


def keep(k, count, block):
    return jnp.where(k < count, block, jnp.zeros_like(block))


def forward_column(c, first, lists, xs, gate_ref, up_ref):
    rows_ref, counts_ref = lists
    slots, tile = gate_ref.shape[2:4]
    count = counts_ref[0, first + c]
    picked = []
    for k in range(slots):
        where = lanes(rows_ref[k, 0, first + c], tile)
        picked.append(keep(k, count, jnp.concatenate([x[:, where] for x in xs], axis=0)))
    return jnp.dot(
        jnp.concatenate(picked, axis=1), weights_of(c, gate_ref, up_ref), preferred_element_type=F32
    ).astype(BF16)


def groups_of(cols):
    edges = [0, -(-cols * 3 // 8), -(-cols * 6 // 8), cols]
    return [(start, stop) for start, stop in zip(edges, edges[1:]) if start < stop]


def load_tiles(first, cols, gate_hbm, up_hbm, gate_ref, up_ref, sems):
    def copies(i, start, stop):
        return [
            pltpu.make_async_copy(
                source.at[pl.ds(first + start, stop - start)], target.at[pl.ds(start, stop - start)], sems.at[j, i]
            )
            for j, (source, target) in enumerate(((gate_hbm, gate_ref), (up_hbm, up_ref)))
        ]

    started = {start: copies(i, start, stop) for i, (start, stop) in enumerate(groups_of(cols))}
    for group in started.values():
        for copy in group:
            copy.start()

    def arrive(c):
        for copy in started.get(c, ()):
            copy.wait()

    return arrive


def store_tiles(first, c, gate_ref, up_ref, gate_hbm, up_hbm, sems):
    copies = [
        pltpu.make_async_copy(gate_ref.at[c], gate_hbm.at[first + c], sems.at[0, c]),
        pltpu.make_async_copy(up_ref.at[c], up_hbm.at[first + c], sems.at[1, c]),
    ]
    for copy in copies:
        copy.start()
    return copies


def forward_own_kernel(x_hbm, rows_hbm, counts_hbm, gate_hbm, up_hbm, part_ref, gate_ref, up_ref, rows_ref, counts_ref, *scratch):
    x_ref, sems, small_sems = scratch
    cols = gate_ref.shape[0]
    small = [
        pltpu.make_async_copy(source, target, small_sems.at[i])
        for i, (source, target) in enumerate(((rows_hbm, rows_ref), (counts_hbm, counts_ref), (x_hbm, x_ref)))
    ]
    for copy in small:
        copy.start()
    arrive = load_tiles(0, cols, gate_hbm, up_hbm, gate_ref, up_ref, sems)
    for copy in small:
        copy.wait()
    for c in range(cols):
        arrive(c)
        part_ref[c] = forward_column(c, 0, (rows_ref, counts_ref), [x_ref], gate_ref, up_ref)


def forward_kernel(members, rows_ref, counts_ref, *refs):
    xs = refs[:members]
    gate_ref, up_ref = refs[members : members + 2]
    part_ref = refs[-1]
    for c in range(gate_ref.shape[0]):
        part_ref[c] = forward_column(c, 0, (rows_ref, counts_ref), xs, gate_ref, up_ref)


def load_forward_kernel(members, groups, first, turn, rows_ref, counts_ref, *refs):
    xs = refs[:members]
    gate_hbm, up_hbm = refs[members : members + 2]
    outs = refs[-(len(groups) + 3 + turn) :]
    parts, gate_ref, up_ref, sems = outs[: len(groups)], outs[-3 - turn], outs[-2 - turn], outs[-1]
    cols, _, _, tile, _ = gate_ref.shape
    arrive = load_tiles(first, cols, gate_hbm, up_hbm, gate_ref, up_ref, sems)
    if turn:
        turned_ref = outs[-2]
        identity = (
            lax.broadcasted_iota(jnp.int32, (tile, tile), 0) == lax.broadcasted_iota(jnp.int32, (tile, tile), 1)
        ).astype(F32).astype(BF16)
        for r in range(turned_ref.shape[0]):
            block = jnp.concatenate([x[:, r * tile : (r + 1) * tile] for x in xs], axis=0)
            turned_ref[r] = lax.dot_general(
                identity, block, (((1,), (1,)), ((), ())), preferred_element_type=F32
            ).astype(BF16)
    for c in range(cols):
        arrive(c)
        part = forward_column(c, first, (rows_ref, counts_ref), xs, gate_ref, up_ref)
        for (start, stop), part_ref in zip(groups, parts):
            part_ref[c] = part[start:stop]


def shard_of(member):
    if member < 2:
        return lax.axis_index("tok") ^ member
    return lax.axis_index("tok") ^ ((member & ~1) + ((member & 1) ^ lax.axis_index("sub")))


def cotangent_of(members, cots, shard_rows, where):
    shards_each = cots[0].shape[0] // shard_rows
    blocks = []
    for member in members:
        shard = shard_of(member)
        source = (shard // shards_each) ^ lax.axis_index("blk")
        rows = pl.ds(pl.multiple_of((shard % shards_each) * shard_rows, shard_rows), shard_rows)
        block = cots[0][rows, where]
        for j, cot in enumerate(cots[1:], 1):
            block = jnp.where(source == j, cot[rows, where], block)
        blocks.append(block.astype(F32))
    return jnp.concatenate(blocks, axis=0)


def nonlinear(total, cotangent):
    tile = total.shape[1] // 2
    gate_value, up_value = total[:, :tile], total[:, tile:]
    sig_gate = jax.nn.sigmoid(gate_value)
    act_gate = gate_value * sig_gate
    hidden = (act_gate * up_value).astype(BF16)
    gate_grad = (cotangent * up_value * sig_gate * (1.0 + gate_value * (1.0 - sig_gate))).astype(BF16)
    up_grad = (cotangent * act_gate).astype(BF16)
    return hidden, jnp.concatenate([gate_grad, up_grad], axis=1)


def total_of(c, parts):
    total = parts[0][c].astype(F32)
    for part in parts[1:]:
        total = total + part[c].astype(F32)
    return total


def back_terms(c, grads, gate_ref, up_ref):
    return lax.dot_general(
        grads, weights_of(c, gate_ref, up_ref), (((1,), (1,)), ((), ())), preferred_element_type=F32
    )


def add_back(c, lists, back, accs, slots, tile):
    rows_ref, counts_ref = lists
    rows = [rows_ref[k, 0, c] for k in range(slots)]
    start = 0
    for acc in accs:
        stop = start + acc.shape[1]
        sums = [
            acc[rows[k]] + keep(k, counts_ref[0, c], back[start:stop, k * tile : (k + 1) * tile])
            for k in range(slots)
        ]
        for k in range(slots):
            acc[rows[k]] = sums[k]
        start = stop


def tile_grads(c, first, lists, turned_ref, grads, gate_ref, up_ref):
    rows_ref, counts_ref = lists
    slots, tile = gate_ref.shape[2:4]
    picked = jnp.concatenate([turned_ref[rows_ref[k, 0, first + c]] for k in range(slots)], axis=0)
    found = jnp.dot(picked, grads, preferred_element_type=F32)
    for k in range(slots):
        term = keep(k, counts_ref[0, first + c], found[k * tile : (k + 1) * tile]).astype(BF16)
        gate_ref[c, 0, k] = term[:, :tile]
        up_ref[c, 0, k] = term[:, tile:]


def start_hidden(members, parts, hidden_hbm, shard_rows, sems):
    shards_each = hidden_hbm.shape[0] // shard_rows

    def copies(i, member):
        rows = pl.ds(i * shard_rows, shard_rows)
        return [
            pltpu.make_async_copy(
                array.at[pl.ds(row, shard_rows)], hidden_hbm.at[rows, pl.ds(first, array.shape[1])], sems.at[j, i]
            )
            for j, (array, row, first) in enumerate(parts(member))
        ]

    for i in range(shards_each):
        wanted = lax.axis_index("blk") * shards_each + i
        for member in members:

            @pl.when(shard_of(member) == wanted)
            def _(i=i, member=member):
                for copy in copies(i, member):
                    copy.start()

    return [copy for i in range(shards_each) for copy in copies(i, 0)]


def first_half_kernel(members, owners, rows_ref, counts_ref, gate_w, up_w, turned_ref, *refs):
    near, rest, cots = refs[:owners], refs[owners : 2 * owners], refs[2 * owners : 3 * owners]
    gate_hbm, up_hbm, hidden_ref, acc_near, acc_far, grads_ref, gate_ref, up_ref, sems = refs[-9:]
    cols, _, slots, tile, _ = gate_ref.shape
    shard_rows = hidden_ref.shape[0] // members
    lists = (rows_ref, counts_ref)
    acc_near[...] = jnp.zeros_like(acc_near)
    acc_far[...] = jnp.zeros_like(acc_far)
    copies = []
    for c in range(cols):
        total = jnp.concatenate([total_of(c, near), total_of(c, rest)], axis=0)
        where = slice(c * tile, (c + 1) * tile)
        hidden, grads = nonlinear(total, cotangent_of(range(members), cots, shard_rows, where))
        hidden_ref[:, where] = hidden
        grads_ref[c] = grads
        tile_grads(c, 0, lists, turned_ref, grads, gate_ref, up_ref)
        copies += store_tiles(0, c, gate_ref, up_ref, gate_hbm, up_hbm, sems)
    for c in range(cols):
        add_back(c, lists, back_terms(c, grads_ref[c], gate_w, up_w), (acc_near, acc_far), slots, tile)
    for copy in copies:
        copy.wait()


def second_half_kernel(members, owners, first, rows_ref, counts_ref, gate_w, up_w, acc_in, *refs):
    parts, cots = refs[:owners], refs[owners : 2 * owners]
    outs = refs[-(2 + len(members) + 1) :]
    grads_ref, hidden_ref = outs[:2]
    dxs, acc_ref = outs[2:-1], outs[-1]
    cols, _, slots, tile, _ = gate_w.shape
    shard_rows = hidden_ref.shape[0] // len(members)
    acc_ref[...] = acc_in[...]
    for c in range(cols):
        where = slice((first + c) * tile, (first + c + 1) * tile)
        hidden, grads = nonlinear(total_of(c, parts), cotangent_of(members, cots, shard_rows, where))
        hidden_ref[:, c * tile : (c + 1) * tile] = hidden
        grads_ref[c] = grads
        add_back(first + c, (rows_ref, counts_ref), back_terms(c, grads, gate_w, up_w), (acc_ref,), slots, tile)
    for r in range(acc_ref.shape[0]):
        block = acc_ref[r].astype(BF16)
        for m, dx in enumerate(dxs):
            dx[:, r * tile : (r + 1) * tile] = block[m * shard_rows : (m + 1) * shard_rows]


def last_grads_kernel(members, first, rows_ref, counts_ref, turned_ref, *refs):
    near_grads, far_grads, hidden_a, near_hidden, far_hidden = refs[:5]
    gate_hbm, up_hbm, hidden_hbm, token_ref, gate_ref, up_ref, sems, hidden_sems = refs[-8:]
    cols, _, _, tile, _ = gate_ref.shape
    shard_rows = near_hidden.shape[0] // 2
    token_ref[...] = jnp.zeros_like(token_ref)

    def parts(m):
        mine = (near_hidden, m * shard_rows) if m < 2 else (far_hidden, (m - 2) * shard_rows)
        return (hidden_a, m * shard_rows, 0), (*mine, first * tile)

    copies = start_hidden(range(members), parts, hidden_hbm, shard_rows, hidden_sems)
    for c in range(cols):
        grads = jnp.concatenate([near_grads[c], far_grads[c]], axis=0)
        tile_grads(c, first, (rows_ref, counts_ref), turned_ref, grads, gate_ref, up_ref)
        copies += store_tiles(first, c, gate_ref, up_ref, gate_hbm, up_hbm, sems)
    for copy in copies:
        copy.wait()


def copy_kernel(x_ref, _, out_ref):
    out_ref[...] = x_ref[...]


def add_kernel(left_ref, right_ref, out_ref):
    out_ref[...] = (left_ref[...].astype(F32) + right_ref[...].astype(F32)).astype(BF16)


def sum_kernel(count, *refs):
    total = sum(ref[...].astype(F32) for ref in refs[:count])
    refs[-2][...] = total
    refs[-1][...] = total.astype(BF16)


def swap(x, axis, step):
    return lax.ppermute(x, axis, [(i, i ^ step) for i in range(lax.axis_size(axis))])


def swap_far(x, base):
    shards, cores = lax.axis_size("tok"), lax.axis_size("sub")
    pairs = [(t * cores + s, (t ^ (base + s)) * cores + s) for t in range(shards) for s in range(cores)]
    return lax.ppermute(x, ("tok", "sub"), pairs)


def on_device(features_in, gate_tiles, up_tiles, block_rows, block_counts, d_hidden):
    shards, owners = lax.axis_size("tok"), lax.axis_size("blk")
    cols, _, slots, tile, _ = gate_tiles.shape
    shard_rows, width = features_in.shape
    row_blocks = width // tile
    row_total = shards * shard_rows
    near_rows = 2 * shard_rows
    half = max(1, cols // 2)
    bases = range(2, shards, 2)
    lists = (jnp.transpose(block_rows, (2, 1, 0)), jnp.transpose(block_counts, (1, 0)))

    def shape(*dims, dtype=BF16):
        return jax.ShapeDtypeStruct(dims, dtype)

    def cost(tokens, columns, products, tile_bytes, weight=1):
        tiles = weight * columns * slots
        return pl.CostEstimate(
            flops=4 * tokens * tiles * tile * tile * products,
            bytes_accessed=4 * tiles * tile * tile * tile_bytes,
            transcendentals=0,
        )

    def to_owners(part):
        return [part] + [swap(part, "blk", s) for s in range(1, owners)]

    fars = [swap_far(features_in, base) for base in bases]
    xs = [features_in, swap(features_in, "tok", 1)]
    cots = [d_hidden] + [swap(d_hidden, "blk", s) for s in range(1, owners)]

    def tile_shape(columns):
        return pltpu.VMEM((columns, 1, slots, tile, tile), BF16)

    def from_hbm(*arrays):
        return [pltpu.with_memory_space_constraint(array, pltpu.HBM) for array in arrays]

    near_a, *weights_a, rows_held, counts_held = pl.pallas_call(
        forward_own_kernel,
        out_shape=(
            shape(half, shard_rows, 2 * tile),
            tile_shape(half),
            tile_shape(half),
            pltpu.SMEM(lists[0].shape, jnp.int32),
            pltpu.SMEM(lists[1].shape, jnp.int32),
        ),
        in_specs=[ANY_SPEC] * 5,
        out_specs=(VMEM_SPEC,) * 3 + (SMEM_SPEC,) * 2,
        scratch_shapes=[
            pltpu.VMEM((shard_rows, width), BF16),
            pltpu.SemaphoreType.DMA((2, 3)),
            pltpu.SemaphoreType.DMA((3,)),
        ],
        compiler_params=limit(8),
        cost_estimate=cost(shard_rows, half, 1, 1),
        name="forward_own_a",
    )(*from_hbm(features_in, *lists, gate_tiles, up_tiles))
    near_a = to_owners(near_a)
    lists = (rows_held, counts_held)

    for far in fars:
        ready = pl.pallas_call(
            copy_kernel,
            out_shape=shape(shard_rows, width),
            in_specs=[VMEM_SPEC, ANY_SPEC],
            out_specs=VMEM_SPEC,
            compiler_params=limit(8),
            cost_estimate=pl.CostEstimate(flops=0, bytes_accessed=0, transcendentals=0),
            name="after_own",
        )(far, near_a[0])
        xs += [far, swap(ready, "sub", 1)]

    rest_a = pl.pallas_call(
        functools.partial(forward_kernel, shards - 1),
        out_shape=shape(half, row_total - shard_rows, 2 * tile),
        in_specs=[SMEM_SPEC] * 2 + [VMEM_SPEC] * (shards + 1) + [ANY_SPEC],
        out_specs=VMEM_SPEC,
        compiler_params=limit(8),
        cost_estimate=cost(row_total, half, 1, 1),
        name="forward_rest_a",
    )(*lists, *xs[1:], *weights_a, cots[-1])
    rest_a = to_owners(rest_a)

    rest = cols - half
    far_b, near_b, gate_b, up_b, turned = pl.pallas_call(
        functools.partial(load_forward_kernel, shards, ((near_rows, row_total), (0, near_rows)), half, 1),
        out_shape=(
            shape(rest, row_total - near_rows, 2 * tile),
            shape(rest, near_rows, 2 * tile),
            tile_shape(rest),
            tile_shape(rest),
            pltpu.VMEM((row_blocks, tile, row_total), BF16),
        ),
        in_specs=[SMEM_SPEC] * 2 + [VMEM_SPEC] * shards + [ANY_SPEC] * 4,
        out_specs=(VMEM_SPEC,) * 5,
        scratch_shapes=[pltpu.SemaphoreType.DMA((2, 3))],
        compiler_params=limit(8),
        cost_estimate=cost(row_total, rest, 1, 1, 5),
        name="forward_b",
    )(*lists, *xs, *from_hbm(gate_tiles, up_tiles), rest_a[0], near_a[-1])
    weights_b = [gate_b, up_b]
    far_b, near_b = to_owners(far_b), to_owners(near_b)

    out_tiles = shape(*gate_tiles.shape)
    tile_bytes = slots * tile * tile * 2
    gate_out, up_out, hidden_a, acc_near, acc_far = pl.pallas_call(
        functools.partial(first_half_kernel, shards, owners),
        out_shape=(
            out_tiles,
            out_tiles,
            shape(row_total, half * tile),
            shape(row_blocks, near_rows, tile, dtype=F32),
            shape(row_blocks, row_total - near_rows, tile, dtype=F32),
        ),
        in_specs=[SMEM_SPEC] * 2 + [VMEM_SPEC] * (3 + 3 * owners) + [ANY_SPEC] * 2,
        out_specs=(ANY_SPEC,) * 2 + (VMEM_SPEC,) * 3,
        scratch_shapes=[
            pltpu.VMEM((half, row_total, 2 * tile), BF16),
            tile_shape(half),
            tile_shape(half),
            pltpu.SemaphoreType.DMA((2, half)),
        ],
        compiler_params=limit(8 + 2 * half * tile_bytes // MIB),
        cost_estimate=cost(row_total, half, 2, 1, 1),
        name="first_half",
    )(*lists, *weights_a, turned, *near_a, *rest_a, *cots, far_b[0], near_b[0])

    def second_half(members, acc, parts, after, weight):
        rows_here = len(members) * shard_rows
        return pl.pallas_call(
            functools.partial(second_half_kernel, members, owners, half),
            out_shape=(
                shape(rest, rows_here, 2 * tile),
                shape(rows_here, rest * tile),
                *[shape(shard_rows, width) for _ in members],
            ),
            in_specs=[SMEM_SPEC] * 2 + [VMEM_SPEC] * (3 + 2 * owners) + [ANY_SPEC],
            out_specs=(VMEM_SPEC,) * (2 + len(members)),
            scratch_shapes=[pltpu.VMEM((row_blocks, rows_here, tile), F32)],
            compiler_params=limit(8),
            cost_estimate=cost(rows_here, rest, 1, 1, weight),
            name="second_half",
        )(*lists, *weights_b, acc, *parts, *cots, after)

    far_grads, far_hidden, *far_dxs = second_half(range(2, shards), acc_far, far_b, acc_near, 1)
    both_cores = []
    for mine, others in zip(far_dxs[::2], far_dxs[1::2]):
        other = swap(others, "sub", 1)
        both_cores.append(
            pl.pallas_call(
                add_kernel,
                out_shape=shape(shard_rows, width),
                in_specs=[VMEM_SPEC] * 2,
                out_specs=VMEM_SPEC,
                compiler_params=limit(8),
                cost_estimate=pl.CostEstimate(flops=0, bytes_accessed=0, transcendentals=0),
                name="add_cores",
            )(mine, other)
        )
    back_far = [swap_far(total, base) for total, base in zip(both_cores, bases)]

    near_grads, near_hidden, own_dx, next_dx = second_half(range(2), acc_near, near_b, both_cores[-1], 1)
    back_next = swap(next_dx, "tok", 1)

    gate_out, up_out, hidden_out, token = pl.pallas_call(
        functools.partial(last_grads_kernel, shards, half),
        out_shape=(out_tiles, out_tiles, shape(*d_hidden.shape), shape(8, tile, dtype=F32)),
        in_specs=[SMEM_SPEC] * 2 + [VMEM_SPEC] * 6 + [ANY_SPEC] * 2,
        out_specs=(ANY_SPEC,) * 3 + (VMEM_SPEC,),
        scratch_shapes=[
            tile_shape(rest),
            tile_shape(rest),
            pltpu.SemaphoreType.DMA((2, rest)),
            pltpu.SemaphoreType.DMA((2, d_hidden.shape[0] // shard_rows)),
        ],
        input_output_aliases={8: 0, 9: 1},
        compiler_params=limit(8 + 2 * rest * tile_bytes // MIB),
        cost_estimate=cost(row_total, rest, 1, 1, 10),
        name="last_grads",
    )(*lists, turned, near_grads, far_grads, hidden_a, near_hidden, far_hidden, gate_out, up_out)
    arrived = [own_dx, back_next, *back_far]
    mine, mine_sent = pl.pallas_call(
        functools.partial(sum_kernel, len(arrived)),
        out_shape=(shape(shard_rows, width, dtype=F32), shape(shard_rows, width)),
        in_specs=[VMEM_SPEC] * len(arrived) + [ANY_SPEC],
        out_specs=(VMEM_SPEC,) * 2,
        compiler_params=limit(8),
        name="sum_shards",
    )(*arrived, token)
    features_grad = (mine + swap(mine_sent, "sub", 1).astype(F32)).astype(BF16)
    return (hidden_out, gate_out, up_out, features_grad)


def solution(mesh):
    return jax.shard_map(
        on_device,
        mesh=mesh,
        in_specs=(
            P(("groups", "tok"), "blk"),
            P(("tok", "sub"), "blk", None, None, None),
            P(("tok", "sub"), "blk", None, None, None),
            P(("tok", "sub"), "blk", None),
            P(("tok", "sub"), "blk"),
            P(("groups", "blk"), ("tok", "sub")),
        ),
        out_specs=(
            P(("groups", "blk"), ("tok", "sub")),
            P(("groups", "tok", "sub"), "blk", None, None, None),
            P(("groups", "tok", "sub"), "blk", None, None, None),
            P(("groups", "tok"), "blk"),
        ),
        check_vma=False,
    )
```

```python
import functools

import jax
import jax.numpy as jnp
from jax import lax
from jax.experimental import pallas as pl
from jax.experimental.pallas import tpu as pltpu
from jax.sharding import PartitionSpec as P

F32 = jnp.float32
BF16 = jnp.bfloat16
MIB = 1 << 20
VMEM_SPEC = pl.BlockSpec(memory_space=pltpu.VMEM)
SMEM_SPEC = pl.BlockSpec(memory_space=pltpu.SMEM)
ANY_SPEC = pl.BlockSpec(memory_space=pl.ANY)


def limit(mib):
    return pltpu.CompilerParams(vmem_limit_bytes=mib * MIB)


def lanes(index, width):
    return pl.ds(pl.multiple_of(index * width, width), width)


def weights_of(c, gate_ref, up_ref):
    slots, rows, cols = gate_ref.shape[2:]
    return jnp.concatenate(
        [gate_ref[c, 0].reshape(slots * rows, cols), up_ref[c, 0].reshape(slots * rows, cols)], axis=1
    )


def keep(k, count, block):
    return jnp.where(k < count, block, jnp.zeros_like(block))


def forward_column(c, first, lists, xs, gate_ref, up_ref):
    rows_ref, counts_ref = lists
    slots, tile = gate_ref.shape[2:4]
    count = counts_ref[0, first + c]
    picked = []
    for k in range(slots):
        where = lanes(rows_ref[k, 0, first + c], tile)
        picked.append(keep(k, count, jnp.concatenate([x[:, where] for x in xs], axis=0)))
    return jnp.dot(
        jnp.concatenate(picked, axis=1), weights_of(c, gate_ref, up_ref), preferred_element_type=F32
    ).astype(BF16)


def groups_of(cols):
    edges = [0, -(-cols * 3 // 8), -(-cols * 6 // 8), cols]
    return [(start, stop) for start, stop in zip(edges, edges[1:]) if start < stop]


def load_tiles(first, cols, gate_hbm, up_hbm, gate_ref, up_ref, sems):
    def copies(i, start, stop):
        return [
            pltpu.make_async_copy(
                source.at[pl.ds(first + start, stop - start)], target.at[pl.ds(start, stop - start)], sems.at[j, i]
            )
            for j, (source, target) in enumerate(((gate_hbm, gate_ref), (up_hbm, up_ref)))
        ]

    started = {start: copies(i, start, stop) for i, (start, stop) in enumerate(groups_of(cols))}
    for group in started.values():
        for copy in group:
            copy.start()

    def arrive(c):
        for copy in started.get(c, ()):
            copy.wait()

    return arrive


def store_tiles(first, c, gate_ref, up_ref, gate_hbm, up_hbm, sems):
    copies = [
        pltpu.make_async_copy(gate_ref.at[c], gate_hbm.at[first + c], sems.at[0, c]),
        pltpu.make_async_copy(up_ref.at[c], up_hbm.at[first + c], sems.at[1, c]),
    ]
    for copy in copies:
        copy.start()
    return copies


def forward_own_kernel(x_hbm, rows_hbm, counts_hbm, gate_hbm, up_hbm, part_ref, gate_ref, up_ref, rows_ref, counts_ref, *scratch):
    x_ref, sems, small_sems = scratch
    cols = gate_ref.shape[0]
    small = [
        pltpu.make_async_copy(source, target, small_sems.at[i])
        for i, (source, target) in enumerate(((rows_hbm, rows_ref), (counts_hbm, counts_ref), (x_hbm, x_ref)))
    ]
    for copy in small:
        copy.start()
    arrive = load_tiles(0, cols, gate_hbm, up_hbm, gate_ref, up_ref, sems)
    for copy in small:
        copy.wait()
    for c in range(cols):
        arrive(c)
        part_ref[c] = forward_column(c, 0, (rows_ref, counts_ref), [x_ref], gate_ref, up_ref)


def forward_kernel(members, rows_ref, counts_ref, *refs):
    xs = refs[:members]
    gate_ref, up_ref = refs[members : members + 2]
    part_ref = refs[-1]
    for c in range(gate_ref.shape[0]):
        part_ref[c] = forward_column(c, 0, (rows_ref, counts_ref), xs, gate_ref, up_ref)


def load_forward_kernel(members, groups, first, turn, rows_ref, counts_ref, *refs):
    xs = refs[:members]
    gate_hbm, up_hbm = refs[members : members + 2]
    outs = refs[-(len(groups) + 3 + turn) :]
    parts, gate_ref, up_ref, sems = outs[: len(groups)], outs[-3 - turn], outs[-2 - turn], outs[-1]
    cols, _, _, tile, _ = gate_ref.shape
    arrive = load_tiles(first, cols, gate_hbm, up_hbm, gate_ref, up_ref, sems)
    if turn:
        turned_ref = outs[-2]
        identity = (
            lax.broadcasted_iota(jnp.int32, (tile, tile), 0) == lax.broadcasted_iota(jnp.int32, (tile, tile), 1)
        ).astype(F32).astype(BF16)
        for r in range(turned_ref.shape[0]):
            block = jnp.concatenate([x[:, r * tile : (r + 1) * tile] for x in xs], axis=0)
            turned_ref[r] = lax.dot_general(
                identity, block, (((1,), (1,)), ((), ())), preferred_element_type=F32
            ).astype(BF16)
    for c in range(cols):
        arrive(c)
        part = forward_column(c, first, (rows_ref, counts_ref), xs, gate_ref, up_ref)
        for (start, stop), part_ref in zip(groups, parts):
            part_ref[c] = part[start:stop]


def shard_of(member):
    if member < 2:
        return lax.axis_index("tok") ^ member
    return lax.axis_index("tok") ^ ((member & ~1) + ((member & 1) ^ lax.axis_index("sub")))


def cotangent_of(members, cots, shard_rows, where):
    shards_each = cots[0].shape[0] // shard_rows
    blocks = []
    for member in members:
        shard = shard_of(member)
        source = (shard // shards_each) ^ lax.axis_index("blk")
        rows = pl.ds(pl.multiple_of((shard % shards_each) * shard_rows, shard_rows), shard_rows)
        block = cots[0][rows, where]
        for j, cot in enumerate(cots[1:], 1):
            block = jnp.where(source == j, cot[rows, where], block)
        blocks.append(block.astype(F32))
    return jnp.concatenate(blocks, axis=0)


def nonlinear(total, cotangent):
    tile = total.shape[1] // 2
    gate_value, up_value = total[:, :tile], total[:, tile:]
    sig_gate = jax.nn.sigmoid(gate_value)
    act_gate = gate_value * sig_gate
    hidden = (act_gate * up_value).astype(BF16)
    gate_grad = (cotangent * up_value * sig_gate * (1.0 + gate_value * (1.0 - sig_gate))).astype(BF16)
    up_grad = (cotangent * act_gate).astype(BF16)
    return hidden, jnp.concatenate([gate_grad, up_grad], axis=1)


def total_of(c, parts):
    total = parts[0][c].astype(F32)
    for part in parts[1:]:
        total = total + part[c].astype(F32)
    return total


def back_terms(c, grads, gate_ref, up_ref):
    return lax.dot_general(
        grads, weights_of(c, gate_ref, up_ref), (((1,), (1,)), ((), ())), preferred_element_type=F32
    )


def add_back(c, lists, back, accs, slots, tile):
    rows_ref, counts_ref = lists
    rows = [rows_ref[k, 0, c] for k in range(slots)]
    start = 0
    for acc in accs:
        stop = start + acc.shape[1]
        sums = [
            acc[rows[k]] + keep(k, counts_ref[0, c], back[start:stop, k * tile : (k + 1) * tile])
            for k in range(slots)
        ]
        for k in range(slots):
            acc[rows[k]] = sums[k]
        start = stop


def tile_grads(c, first, lists, turned_ref, grads, gate_ref, up_ref):
    rows_ref, counts_ref = lists
    slots, tile = gate_ref.shape[2:4]
    picked = jnp.concatenate([turned_ref[rows_ref[k, 0, first + c]] for k in range(slots)], axis=0)
    found = jnp.dot(picked, grads, preferred_element_type=F32)
    for k in range(slots):
        term = keep(k, counts_ref[0, first + c], found[k * tile : (k + 1) * tile]).astype(BF16)
        gate_ref[c, 0, k] = term[:, :tile]
        up_ref[c, 0, k] = term[:, tile:]


def start_hidden(members, parts, hidden_hbm, shard_rows, sems):
    shards_each = hidden_hbm.shape[0] // shard_rows

    def copies(i, member):
        rows = pl.ds(i * shard_rows, shard_rows)
        return [
            pltpu.make_async_copy(
                array.at[pl.ds(row, shard_rows)], hidden_hbm.at[rows, pl.ds(first, array.shape[1])], sems.at[j, i]
            )
            for j, (array, row, first) in enumerate(parts(member))
        ]

    for i in range(shards_each):
        wanted = lax.axis_index("blk") * shards_each + i
        for member in members:

            @pl.when(shard_of(member) == wanted)
            def _(i=i, member=member):
                for copy in copies(i, member):
                    copy.start()

    return [copy for i in range(shards_each) for copy in copies(i, 0)]


def first_half_kernel(members, owners, rows_ref, counts_ref, gate_w, up_w, turned_ref, *refs):
    groups = [refs[start : start + owners] for start in range(0, 3 * owners, owners)]
    cots = refs[3 * owners : 4 * owners]
    gate_hbm, up_hbm, hidden_ref = refs[-10:-7]
    accs = refs[-7:-4]
    grads_ref, gate_ref, up_ref, sems = refs[-4:]
    cols, _, slots, tile, _ = gate_ref.shape
    shard_rows = hidden_ref.shape[0] // len(members)
    lists = (rows_ref, counts_ref)
    for acc in accs:
        acc[...] = jnp.zeros_like(acc)
    copies = []
    for c in range(cols):
        total = jnp.concatenate([total_of(c, parts) for parts in groups], axis=0)
        where = slice(c * tile, (c + 1) * tile)
        hidden, grads = nonlinear(total, cotangent_of(members, cots, shard_rows, where))
        hidden_ref[:, where] = hidden
        grads_ref[c] = grads
        tile_grads(c, 0, lists, turned_ref, grads, gate_ref, up_ref)
        copies += store_tiles(0, c, gate_ref, up_ref, gate_hbm, up_hbm, sems)
    for c in range(cols):
        add_back(c, lists, back_terms(c, grads_ref[c], gate_w, up_w), accs, slots, tile)
    for copy in copies:
        copy.wait()


def second_half_kernel(members, owners, first, rows_ref, counts_ref, gate_w, up_w, acc_in, *refs):
    parts, cots = refs[:owners], refs[owners : 2 * owners]
    outs = refs[-(2 + len(members) + 1) :]
    grads_ref, hidden_ref = outs[:2]
    dxs, acc_ref = outs[2:-1], outs[-1]
    cols, _, slots, tile, _ = gate_w.shape
    shard_rows = hidden_ref.shape[0] // len(members)
    acc_ref[...] = acc_in[...]
    for c in range(cols):
        where = slice((first + c) * tile, (first + c + 1) * tile)
        hidden, grads = nonlinear(total_of(c, parts), cotangent_of(members, cots, shard_rows, where))
        hidden_ref[:, c * tile : (c + 1) * tile] = hidden
        grads_ref[c] = grads
        add_back(first + c, (rows_ref, counts_ref), back_terms(c, grads, gate_w, up_w), (acc_ref,), slots, tile)
    for r in range(acc_ref.shape[0]):
        block = acc_ref[r].astype(BF16)
        for m, dx in enumerate(dxs):
            dx[:, r * tile : (r + 1) * tile] = block[m * shard_rows : (m + 1) * shard_rows]


def last_grads_kernel(members, first, rows_ref, counts_ref, turned_ref, *refs):
    all_grads, hidden_a, hiddens = refs[:3], refs[3], refs[4:7]
    gate_hbm, up_hbm, hidden_hbm, token_ref, gate_ref, up_ref, sems, hidden_sems = refs[-8:]
    cols, _, _, tile, _ = gate_ref.shape
    shard_rows = hiddens[0].shape[0]
    token_ref[...] = jnp.zeros_like(token_ref)

    def parts(member):
        at = members.index(member)
        mine = (hiddens[at], 0) if at < 2 else (hiddens[2], (at - 2) * shard_rows)
        return (hidden_a, at * shard_rows, 0), (*mine, first * tile)

    copies = start_hidden(members, parts, hidden_hbm, shard_rows, hidden_sems)
    for c in range(cols):
        grads = jnp.concatenate([part[c] for part in all_grads], axis=0)
        tile_grads(c, first, (rows_ref, counts_ref), turned_ref, grads, gate_ref, up_ref)
        copies += store_tiles(first, c, gate_ref, up_ref, gate_hbm, up_hbm, sems)
    for copy in copies:
        copy.wait()


def copy_kernel(x_ref, _, out_ref):
    out_ref[...] = x_ref[...]


def add_kernel(left_ref, right_ref, *refs):
    out_ref = refs[-1]
    out_ref[...] = (left_ref[...].astype(F32) + right_ref[...].astype(F32)).astype(BF16)


def sum_kernel(count, *refs):
    total = sum(ref[...].astype(F32) for ref in refs[:count])
    refs[-2][...] = total
    refs[-1][...] = total.astype(BF16)


def swap(x, axis, step):
    return lax.ppermute(x, axis, [(i, i ^ step) for i in range(lax.axis_size(axis))])


def swap_far(x, base):
    shards, cores = lax.axis_size("tok"), lax.axis_size("sub")
    pairs = [(t * cores + s, (t ^ (base + s)) * cores + s) for t in range(shards) for s in range(cores)]
    return lax.ppermute(x, ("tok", "sub"), pairs)


def on_device(features_in, gate_tiles, up_tiles, block_rows, block_counts, d_hidden):
    shards, owners = lax.axis_size("tok"), lax.axis_size("blk")
    cols, _, slots, tile, _ = gate_tiles.shape
    shard_rows, width = features_in.shape
    row_blocks = width // tile
    row_total = shards * shard_rows
    near_rows = 2 * shard_rows
    half = max(1, cols // 2)
    bases = range(2, shards, 2)
    lists = (jnp.transpose(block_rows, (2, 1, 0)), jnp.transpose(block_counts, (1, 0)))

    def shape(*dims, dtype=BF16):
        return jax.ShapeDtypeStruct(dims, dtype)

    def cost(tokens, columns, products, tile_bytes, weight=1):
        tiles = weight * columns * slots
        return pl.CostEstimate(
            flops=4 * tokens * tiles * tile * tile * products,
            bytes_accessed=4 * tiles * tile * tile * tile_bytes,
            transcendentals=0,
        )

    def to_owners(part):
        return [part] + [swap(part, "blk", s) for s in range(1, owners)]

    fars = [swap_far(features_in, base) for base in bases]
    features_next = swap(features_in, "tok", 1)
    cots = [d_hidden] + [swap(d_hidden, "blk", s) for s in range(1, owners)]

    def tile_shape(columns):
        return pltpu.VMEM((columns, 1, slots, tile, tile), BF16)

    def from_hbm(*arrays):
        return [pltpu.with_memory_space_constraint(array, pltpu.HBM) for array in arrays]

    near_a, *weights_a, rows_held, counts_held = pl.pallas_call(
        forward_own_kernel,
        out_shape=(
            shape(half, shard_rows, 2 * tile),
            tile_shape(half),
            tile_shape(half),
            pltpu.SMEM(lists[0].shape, jnp.int32),
            pltpu.SMEM(lists[1].shape, jnp.int32),
        ),
        in_specs=[ANY_SPEC] * 5,
        out_specs=(VMEM_SPEC,) * 3 + (SMEM_SPEC,) * 2,
        scratch_shapes=[
            pltpu.VMEM((shard_rows, width), BF16),
            pltpu.SemaphoreType.DMA((2, 3)),
            pltpu.SemaphoreType.DMA((3,)),
        ],
        compiler_params=limit(8),
        cost_estimate=cost(shard_rows, half, 1, 1),
        name="forward_own_a",
    )(*from_hbm(features_in, *lists, gate_tiles, up_tiles))
    near_a = to_owners(near_a)
    lists = (rows_held, counts_held)

    members = [0, 1, *range(2, shards, 2), *range(3, shards, 2)]
    far_members = members[2:]
    own_rows, far_rows = shard_rows, row_total - near_rows
    before_swap = [
        pl.pallas_call(
            copy_kernel,
            out_shape=shape(shard_rows, width),
            in_specs=[VMEM_SPEC, ANY_SPEC],
            out_specs=VMEM_SPEC,
            compiler_params=limit(8),
            cost_estimate=pl.CostEstimate(flops=0, bytes_accessed=0, transcendentals=0),
            name="after_own",
        )(far, near_a[0])
        for far in fars
    ]
    fetched = [features_next, *fars]
    swapped = [swap(far, "sub", 1) for far in before_swap]
    xs = [features_in, *fetched, *swapped]

    def forward_a(name, shard_xs, after):
        tokens = len(shard_xs) * shard_rows
        return to_owners(
            pl.pallas_call(
                functools.partial(forward_kernel, len(shard_xs)),
                out_shape=shape(half, tokens, 2 * tile),
                in_specs=[SMEM_SPEC] * 2 + [VMEM_SPEC] * (len(shard_xs) + 2) + [ANY_SPEC] * len(after),
                out_specs=VMEM_SPEC,
                compiler_params=limit(8),
                cost_estimate=cost(tokens, half, 1, 1),
                name=name,
            )(*lists, *shard_xs, *weights_a, *after)
        )

    fetched_a = forward_a("forward_fetched_a", fetched, [cots[-1], before_swap[-1]])
    swapped_a = forward_a("forward_swapped_a", swapped, [fetched_a[0]])

    rest = cols - half
    groups = ((near_rows, row_total), (own_rows, near_rows), (0, own_rows))
    far_b, next_b, own_b, gate_b, up_b, turned = pl.pallas_call(
        functools.partial(load_forward_kernel, shards, groups, half, 1),
        out_shape=(
            *[shape(rest, stop - start, 2 * tile) for start, stop in groups],
            tile_shape(rest),
            tile_shape(rest),
            pltpu.VMEM((row_blocks, tile, row_total), BF16),
        ),
        in_specs=[SMEM_SPEC] * 2 + [VMEM_SPEC] * shards + [ANY_SPEC] * 4,
        out_specs=(VMEM_SPEC,) * 6,
        scratch_shapes=[pltpu.SemaphoreType.DMA((2, 3))],
        compiler_params=limit(8),
        cost_estimate=cost(row_total, rest, 1, 1, 5),
        name="forward_b",
    )(*lists, *xs, *from_hbm(gate_tiles, up_tiles), swapped_a[0], near_a[-1])
    weights_b = [gate_b, up_b]
    far_b, next_b, own_b = to_owners(far_b), to_owners(next_b), to_owners(own_b)

    out_tiles = shape(*gate_tiles.shape)
    tile_bytes = slots * tile * tile * 2
    gate_out, up_out, hidden_a, acc_own, acc_next, acc_far = pl.pallas_call(
        functools.partial(first_half_kernel, members, owners),
        out_shape=(
            out_tiles,
            out_tiles,
            shape(row_total, half * tile),
            *[shape(row_blocks, rows, tile, dtype=F32) for rows in (own_rows, own_rows, far_rows)],
        ),
        in_specs=[SMEM_SPEC] * 2 + [VMEM_SPEC] * (3 + 4 * owners) + [ANY_SPEC] * 3,
        out_specs=(ANY_SPEC,) * 2 + (VMEM_SPEC,) * 4,
        scratch_shapes=[
            pltpu.VMEM((half, row_total, 2 * tile), BF16),
            tile_shape(half),
            tile_shape(half),
            pltpu.SemaphoreType.DMA((2, half)),
        ],
        compiler_params=limit(8 + 2 * half * tile_bytes // MIB),
        cost_estimate=cost(row_total, half, 2, 1, 1),
        name="first_half",
    )(
        *lists, *weights_a, turned, *near_a, *fetched_a, *swapped_a, *cots, far_b[0], next_b[0], own_b[0]
    )

    def second_half(name, chunk, acc, parts, after, weight):
        rows_here = len(chunk) * shard_rows
        return pl.pallas_call(
            functools.partial(second_half_kernel, chunk, owners, half),
            out_shape=(
                shape(rest, rows_here, 2 * tile),
                shape(rows_here, rest * tile),
                *[shape(shard_rows, width) for _ in chunk],
            ),
            in_specs=[SMEM_SPEC] * 2 + [VMEM_SPEC] * (3 + 2 * owners) + [ANY_SPEC],
            out_specs=(VMEM_SPEC,) * (2 + len(chunk)),
            scratch_shapes=[pltpu.VMEM((row_blocks, rows_here, tile), F32)],
            compiler_params=limit(8),
            cost_estimate=cost(rows_here, rest, 1, 1, weight),
            name=name,
        )(*lists, *weights_b, acc, *parts, *cots, after)

    far_grads, far_hidden, *far_dxs = second_half("far_b", far_members, acc_far, far_b, acc_own, 1)
    next_grads, next_hidden, next_dx = second_half("next_b", [1], acc_next, next_b, far_grads, 1)
    both_cores = []
    for mine, others in zip(far_dxs[: len(bases)], far_dxs[len(bases) :]):
        both_cores.append(
            pl.pallas_call(
                add_kernel,
                out_shape=shape(shard_rows, width),
                in_specs=[VMEM_SPEC] * 2 + [ANY_SPEC] * 2,
                out_specs=VMEM_SPEC,
                compiler_params=limit(8),
                cost_estimate=pl.CostEstimate(flops=0, bytes_accessed=0, transcendentals=0),
                name="add_cores",
            )(mine, swap(others, "sub", 1), next_grads, own_b[-1])
        )
    back_far = [swap_far(total, base) for total, base in zip(both_cores, bases)]
    back_next = swap(next_dx, "tok", 1)
    own_grads, own_hidden, own_dx = second_half("own_b", [0], acc_own, own_b, both_cores[-1], 1)

    gate_out, up_out, hidden_out, token = pl.pallas_call(
        functools.partial(last_grads_kernel, members, half),
        out_shape=(out_tiles, out_tiles, shape(*d_hidden.shape), shape(8, tile, dtype=F32)),
        in_specs=[SMEM_SPEC] * 2 + [VMEM_SPEC] * 8 + [ANY_SPEC] * 2,
        out_specs=(ANY_SPEC,) * 3 + (VMEM_SPEC,),
        scratch_shapes=[
            tile_shape(rest),
            tile_shape(rest),
            pltpu.SemaphoreType.DMA((2, rest)),
            pltpu.SemaphoreType.DMA((2, d_hidden.shape[0] // shard_rows)),
        ],
        input_output_aliases={10: 0, 11: 1},
        compiler_params=limit(8 + 2 * rest * tile_bytes // MIB),
        cost_estimate=cost(row_total, rest, 1, 1, 10),
        name="last_grads",
    )(
        *lists,
        turned,
        own_grads,
        next_grads,
        far_grads,
        hidden_a,
        own_hidden,
        next_hidden,
        far_hidden,
        gate_out,
        up_out,
    )
    arrived = [own_dx, back_next, *back_far]
    mine, mine_sent = pl.pallas_call(
        functools.partial(sum_kernel, len(arrived)),
        out_shape=(shape(shard_rows, width, dtype=F32), shape(shard_rows, width)),
        in_specs=[VMEM_SPEC] * len(arrived) + [ANY_SPEC],
        out_specs=(VMEM_SPEC,) * 2,
        compiler_params=limit(8),
        name="sum_shards",
    )(*arrived, token)
    features_grad = (mine + swap(mine_sent, "sub", 1).astype(F32)).astype(BF16)
    return (hidden_out, gate_out, up_out, features_grad)


def solution(mesh):
    return jax.shard_map(
        on_device,
        mesh=mesh,
        in_specs=(
            P(("groups", "tok"), "blk"),
            P(("tok", "sub"), "blk", None, None, None),
            P(("tok", "sub"), "blk", None, None, None),
            P(("tok", "sub"), "blk", None),
            P(("tok", "sub"), "blk"),
            P(("groups", "blk"), ("tok", "sub")),
        ),
        out_specs=(
            P(("groups", "blk"), ("tok", "sub")),
            P(("groups", "tok", "sub"), "blk", None, None, None),
            P(("groups", "tok", "sub"), "blk", None, None, None),
            P(("groups", "tok"), "blk"),
        ),
        check_vma=False,
    )
```

```python
import functools

import jax
import jax.numpy as jnp
from jax import lax
from jax.experimental import pallas as pl
from jax.experimental.pallas import tpu as pltpu
from jax.sharding import PartitionSpec as P

F32 = jnp.float32
BF16 = jnp.bfloat16
MIB = 1 << 20
VMEM_SPEC = pl.BlockSpec(memory_space=pltpu.VMEM)
SMEM_SPEC = pl.BlockSpec(memory_space=pltpu.SMEM)
ANY_SPEC = pl.BlockSpec(memory_space=pl.ANY)


def limit(mib):
    return pltpu.CompilerParams(vmem_limit_bytes=mib * MIB)


def lanes(index, width):
    return pl.ds(pl.multiple_of(index * width, width), width)


def weights_of(c, gate_ref, up_ref):
    slots, rows, cols = gate_ref.shape[2:]
    return jnp.concatenate(
        [gate_ref[c, 0].reshape(slots * rows, cols), up_ref[c, 0].reshape(slots * rows, cols)], axis=1
    )


def keep(k, count, block):
    return jnp.where(k < count, block, jnp.zeros_like(block))


def forward_column(c, first, lists, xs, gate_ref, up_ref):
    rows_ref, counts_ref = lists
    slots, tile = gate_ref.shape[2:4]
    count = counts_ref[0, first + c]
    picked = []
    for k in range(slots):
        where = lanes(rows_ref[k, 0, first + c], tile)
        picked.append(keep(k, count, jnp.concatenate([x[:, where] for x in xs], axis=0)))
    return jnp.dot(
        jnp.concatenate(picked, axis=1), weights_of(c, gate_ref, up_ref), preferred_element_type=F32
    ).astype(BF16)


def groups_of(cols):
    edges = [0, -(-cols * 3 // 8), -(-cols * 6 // 8), cols]
    return [(start, stop) for start, stop in zip(edges, edges[1:]) if start < stop]


def load_tiles(first, cols, gate_hbm, up_hbm, gate_ref, up_ref, sems):
    def copies(i, start, stop):
        return [
            pltpu.make_async_copy(
                source.at[pl.ds(first + start, stop - start)], target.at[pl.ds(start, stop - start)], sems.at[j, i]
            )
            for j, (source, target) in enumerate(((gate_hbm, gate_ref), (up_hbm, up_ref)))
        ]

    started = {start: copies(i, start, stop) for i, (start, stop) in enumerate(groups_of(cols))}
    for group in started.values():
        for copy in group:
            copy.start()

    def arrive(c):
        for copy in started.get(c, ()):
            copy.wait()

    return arrive


def store_tiles(first, c, gate_ref, up_ref, gate_hbm, up_hbm, sems):
    copies = [
        pltpu.make_async_copy(gate_ref.at[c], gate_hbm.at[first + c], sems.at[0, c]),
        pltpu.make_async_copy(up_ref.at[c], up_hbm.at[first + c], sems.at[1, c]),
    ]
    for copy in copies:
        copy.start()
    return copies


def forward_own_kernel(x_hbm, rows_hbm, counts_hbm, gate_hbm, up_hbm, part_ref, gate_ref, up_ref, rows_ref, counts_ref, *scratch):
    x_ref, sems, small_sems = scratch
    cols = gate_ref.shape[0]
    small = [
        pltpu.make_async_copy(source, target, small_sems.at[i])
        for i, (source, target) in enumerate(((rows_hbm, rows_ref), (counts_hbm, counts_ref), (x_hbm, x_ref)))
    ]
    for copy in small:
        copy.start()
    arrive = load_tiles(0, cols, gate_hbm, up_hbm, gate_ref, up_ref, sems)
    for copy in small:
        copy.wait()
    for c in range(cols):
        arrive(c)
        part_ref[c] = forward_column(c, 0, (rows_ref, counts_ref), [x_ref], gate_ref, up_ref)


def forward_kernel(members, rows_ref, counts_ref, *refs):
    xs = refs[:members]
    gate_ref, up_ref = refs[members : members + 2]
    part_ref = refs[-1]
    for c in range(gate_ref.shape[0]):
        part_ref[c] = forward_column(c, 0, (rows_ref, counts_ref), xs, gate_ref, up_ref)


def load_forward_kernel(members, groups, first, turn, rows_ref, counts_ref, *refs):
    xs = refs[:members]
    gate_hbm, up_hbm = refs[members : members + 2]
    outs = refs[-(len(groups) + 3 + turn) :]
    parts, gate_ref, up_ref, sems = outs[: len(groups)], outs[-3 - turn], outs[-2 - turn], outs[-1]
    cols, _, _, tile, _ = gate_ref.shape
    arrive = load_tiles(first, cols, gate_hbm, up_hbm, gate_ref, up_ref, sems)
    if turn:
        turned_ref = outs[-2]
        identity = (
            lax.broadcasted_iota(jnp.int32, (tile, tile), 0) == lax.broadcasted_iota(jnp.int32, (tile, tile), 1)
        ).astype(F32).astype(BF16)
        for r in range(turned_ref.shape[0]):
            block = jnp.concatenate([x[:, r * tile : (r + 1) * tile] for x in xs], axis=0)
            turned_ref[r] = lax.dot_general(
                identity, block, (((1,), (1,)), ((), ())), preferred_element_type=F32
            ).astype(BF16)
    for c in range(cols):
        arrive(c)
        part = forward_column(c, first, (rows_ref, counts_ref), xs, gate_ref, up_ref)
        for (start, stop), part_ref in zip(groups, parts):
            part_ref[c] = part[start:stop]


def shard_of(member):
    if member < 2:
        return lax.axis_index("tok") ^ member
    return lax.axis_index("tok") ^ ((member & ~1) + ((member & 1) ^ lax.axis_index("sub")))


def cotangent_of(members, cots, shard_rows, where):
    shards_each = cots[0].shape[0] // shard_rows
    blocks = []
    for member in members:
        shard = shard_of(member)
        source = (shard // shards_each) ^ lax.axis_index("blk")
        rows = pl.ds(pl.multiple_of((shard % shards_each) * shard_rows, shard_rows), shard_rows)
        block = cots[0][rows, where]
        for j, cot in enumerate(cots[1:], 1):
            block = jnp.where(source == j, cot[rows, where], block)
        blocks.append(block.astype(F32))
    return jnp.concatenate(blocks, axis=0)


def nonlinear(total, cotangent):
    tile = total.shape[1] // 2
    gate_value, up_value = total[:, :tile], total[:, tile:]
    sig_gate = jax.nn.sigmoid(gate_value)
    act_gate = gate_value * sig_gate
    hidden = (act_gate * up_value).astype(BF16)
    gate_grad = (cotangent * up_value * sig_gate * (1.0 + gate_value * (1.0 - sig_gate))).astype(BF16)
    up_grad = (cotangent * act_gate).astype(BF16)
    return hidden, jnp.concatenate([gate_grad, up_grad], axis=1)


def total_of(c, parts):
    total = parts[0][c].astype(F32)
    for part in parts[1:]:
        total = total + part[c].astype(F32)
    return total


def back_terms(c, grads, gate_ref, up_ref):
    return lax.dot_general(
        grads, weights_of(c, gate_ref, up_ref), (((1,), (1,)), ((), ())), preferred_element_type=F32
    )


def add_back(c, lists, back, accs, slots, tile):
    rows_ref, counts_ref = lists
    rows = [rows_ref[k, 0, c] for k in range(slots)]
    start = 0
    for acc in accs:
        stop = start + acc.shape[1]
        sums = [
            acc[rows[k]] + keep(k, counts_ref[0, c], back[start:stop, k * tile : (k + 1) * tile])
            for k in range(slots)
        ]
        for k in range(slots):
            acc[rows[k]] = sums[k]
        start = stop


def tile_grads(c, first, lists, turned_ref, grads, gate_ref, up_ref):
    rows_ref, counts_ref = lists
    slots, tile = gate_ref.shape[2:4]
    picked = jnp.concatenate([turned_ref[rows_ref[k, 0, first + c]] for k in range(slots)], axis=0)
    found = jnp.dot(picked, grads, preferred_element_type=F32)
    for k in range(slots):
        term = keep(k, counts_ref[0, first + c], found[k * tile : (k + 1) * tile]).astype(BF16)
        gate_ref[c, 0, k] = term[:, :tile]
        up_ref[c, 0, k] = term[:, tile:]


def start_hidden(members, parts, hidden_hbm, shard_rows, sems):
    shards_each = hidden_hbm.shape[0] // shard_rows

    def copies(i, member):
        rows = pl.ds(i * shard_rows, shard_rows)
        return [
            pltpu.make_async_copy(
                array.at[pl.ds(row, shard_rows)], hidden_hbm.at[rows, pl.ds(first, array.shape[1])], sems.at[j, i]
            )
            for j, (array, row, first) in enumerate(parts(member))
        ]

    for i in range(shards_each):
        wanted = lax.axis_index("blk") * shards_each + i
        for member in members:

            @pl.when(shard_of(member) == wanted)
            def _(i=i, member=member):
                for copy in copies(i, member):
                    copy.start()

    return [copy for i in range(shards_each) for copy in copies(i, 0)]


def first_half_kernel(members, owners, rows_ref, counts_ref, gate_w, up_w, turned_ref, *refs):
    groups = [refs[start : start + owners] for start in range(0, 2 * owners, owners)]
    cots = refs[2 * owners : 3 * owners]
    gate_hbm, up_hbm, hidden_ref = refs[-10:-7]
    accs = refs[-7:-4]
    grads_ref, gate_ref, up_ref, sems = refs[-4:]
    cols, _, slots, tile, _ = gate_ref.shape
    shard_rows = hidden_ref.shape[0] // len(members)
    lists = (rows_ref, counts_ref)
    for acc in accs:
        acc[...] = jnp.zeros_like(acc)
    copies = []
    for c in range(cols):
        total = jnp.concatenate([total_of(c, parts) for parts in groups], axis=0)
        where = slice(c * tile, (c + 1) * tile)
        hidden, grads = nonlinear(total, cotangent_of(members, cots, shard_rows, where))
        hidden_ref[:, where] = hidden
        grads_ref[c] = grads
        tile_grads(c, 0, lists, turned_ref, grads, gate_ref, up_ref)
        copies += store_tiles(0, c, gate_ref, up_ref, gate_hbm, up_hbm, sems)
    for c in range(cols):
        add_back(c, lists, back_terms(c, grads_ref[c], gate_w, up_w), accs, slots, tile)
    for copy in copies:
        copy.wait()


def second_half_kernel(members, owners, first, rows_ref, counts_ref, gate_w, up_w, acc_in, *refs):
    parts, cots = refs[:owners], refs[owners : 2 * owners]
    outs = refs[-(2 + len(members) + 1) :]
    grads_ref, hidden_ref = outs[:2]
    dxs, acc_ref = outs[2:-1], outs[-1]
    cols, _, slots, tile, _ = gate_w.shape
    shard_rows = hidden_ref.shape[0] // len(members)
    acc_ref[...] = acc_in[...]
    for c in range(cols):
        where = slice((first + c) * tile, (first + c + 1) * tile)
        hidden, grads = nonlinear(total_of(c, parts), cotangent_of(members, cots, shard_rows, where))
        hidden_ref[:, c * tile : (c + 1) * tile] = hidden
        grads_ref[c] = grads
        add_back(first + c, (rows_ref, counts_ref), back_terms(c, grads, gate_w, up_w), (acc_ref,), slots, tile)
    for r in range(acc_ref.shape[0]):
        block = acc_ref[r].astype(BF16)
        for m, dx in enumerate(dxs):
            dx[:, r * tile : (r + 1) * tile] = block[m * shard_rows : (m + 1) * shard_rows]


def last_half_kernel(members, owners, first, rows_ref, counts_ref, gate_w, up_w, turned_ref, acc_in, *refs):
    parts, cots = refs[:owners], refs[owners : 2 * owners]
    next_grads, far_grads, hidden_a, next_hidden, far_hidden = refs[2 * owners : 2 * owners + 5]
    gate_hbm, up_hbm, hidden_hbm, dx_ref = refs[-11:-7]
    acc_ref, grads_ref, hidden_ref, gate_ref, up_ref, sems, hidden_sems = refs[-7:]
    cols, _, slots, tile, _ = gate_ref.shape
    shard_rows = hidden_ref.shape[0]
    lists = (rows_ref, counts_ref)

    def hidden_of(member):
        at = members.index(member)
        mine = ((hidden_ref, 0), (next_hidden, 0))[at] if at < 2 else (far_hidden, (at - 2) * shard_rows)
        return (hidden_a, at * shard_rows, 0), (*mine, first * tile)

    acc_ref[...] = acc_in[...]
    copies = []
    for c in range(cols):
        where = slice((first + c) * tile, (first + c + 1) * tile)
        hidden, grads = nonlinear(total_of(c, parts), cotangent_of(members[:1], cots, shard_rows, where))
        hidden_ref[:, c * tile : (c + 1) * tile] = hidden
        grads_ref[c] = grads
        grads = jnp.concatenate([grads, next_grads[c], far_grads[c]], axis=0)
        tile_grads(c, first, lists, turned_ref, grads, gate_ref, up_ref)
        copies += store_tiles(first, c, gate_ref, up_ref, gate_hbm, up_hbm, sems)
    copies += start_hidden(members, hidden_of, hidden_hbm, shard_rows, hidden_sems)
    for c in range(cols):
        add_back(first + c, lists, back_terms(c, grads_ref[c], gate_w, up_w), (acc_ref,), slots, tile)
    for r in range(acc_ref.shape[0]):
        dx_ref[:, r * tile : (r + 1) * tile] = acc_ref[r].astype(BF16)
    for copy in copies:
        copy.wait()


def copy_kernel(x_ref, _, out_ref):
    out_ref[...] = x_ref[...]


def add_kernel(left_ref, right_ref, *refs):
    out_ref = refs[-1]
    out_ref[...] = (left_ref[...].astype(F32) + right_ref[...].astype(F32)).astype(BF16)


def sum_kernel(count, *refs):
    total = sum(ref[...].astype(F32) for ref in refs[:count])
    refs[-2][...] = total
    refs[-1][...] = total.astype(BF16)


def swap(x, axis, step):
    return lax.ppermute(x, axis, [(i, i ^ step) for i in range(lax.axis_size(axis))])


def swap_far(x, base):
    shards, cores = lax.axis_size("tok"), lax.axis_size("sub")
    pairs = [(t * cores + s, (t ^ (base + s)) * cores + s) for t in range(shards) for s in range(cores)]
    return lax.ppermute(x, ("tok", "sub"), pairs)


def on_device(features_in, gate_tiles, up_tiles, block_rows, block_counts, d_hidden):
    shards, owners = lax.axis_size("tok"), lax.axis_size("blk")
    cols, _, slots, tile, _ = gate_tiles.shape
    shard_rows, width = features_in.shape
    row_blocks = width // tile
    row_total = shards * shard_rows
    near_rows = 2 * shard_rows
    half = max(1, cols // 2)
    bases = range(2, shards, 2)
    lists = (jnp.transpose(block_rows, (2, 1, 0)), jnp.transpose(block_counts, (1, 0)))

    def shape(*dims, dtype=BF16):
        return jax.ShapeDtypeStruct(dims, dtype)

    def cost(tokens, columns, products, tile_bytes, weight=1):
        tiles = weight * columns * slots
        return pl.CostEstimate(
            flops=4 * tokens * tiles * tile * tile * products,
            bytes_accessed=4 * tiles * tile * tile * tile_bytes,
            transcendentals=0,
        )

    def to_owners(part):
        return [part] + [swap(part, "blk", s) for s in range(1, owners)]

    fars = [swap_far(features_in, base) for base in bases]
    features_next = swap(features_in, "tok", 1)
    cots = [d_hidden] + [swap(d_hidden, "blk", s) for s in range(1, owners)]

    def tile_shape(columns):
        return pltpu.VMEM((columns, 1, slots, tile, tile), BF16)

    def from_hbm(*arrays):
        return [pltpu.with_memory_space_constraint(array, pltpu.HBM) for array in arrays]

    near_a, *weights_a, rows_held, counts_held = pl.pallas_call(
        forward_own_kernel,
        out_shape=(
            shape(half, shard_rows, 2 * tile),
            tile_shape(half),
            tile_shape(half),
            pltpu.SMEM(lists[0].shape, jnp.int32),
            pltpu.SMEM(lists[1].shape, jnp.int32),
        ),
        in_specs=[ANY_SPEC] * 5,
        out_specs=(VMEM_SPEC,) * 3 + (SMEM_SPEC,) * 2,
        scratch_shapes=[
            pltpu.VMEM((shard_rows, width), BF16),
            pltpu.SemaphoreType.DMA((2, 3)),
            pltpu.SemaphoreType.DMA((3,)),
        ],
        compiler_params=limit(8),
        cost_estimate=cost(shard_rows, half, 1, 1),
        name="forward_own_a",
    )(*from_hbm(features_in, *lists, gate_tiles, up_tiles))
    near_a = to_owners(near_a)
    lists = (rows_held, counts_held)

    members = [0, 1, *range(2, shards, 2), *range(3, shards, 2)]
    far_members = members[2:]
    own_rows, far_rows = shard_rows, row_total - near_rows
    before_swap = [
        pl.pallas_call(
            copy_kernel,
            out_shape=shape(shard_rows, width),
            in_specs=[VMEM_SPEC, ANY_SPEC],
            out_specs=VMEM_SPEC,
            compiler_params=limit(8),
            cost_estimate=pl.CostEstimate(flops=0, bytes_accessed=0, transcendentals=0),
            name="after_own",
        )(far, near_a[0])
        for far in fars
    ]
    fetched = [features_next, *fars]
    swapped = [swap(far, "sub", 1) for far in before_swap]
    xs = [features_in, *fetched, *swapped]

    def forward_a(name, shard_xs, after):
        tokens = len(shard_xs) * shard_rows
        return to_owners(
            pl.pallas_call(
                functools.partial(forward_kernel, len(shard_xs)),
                out_shape=shape(half, tokens, 2 * tile),
                in_specs=[SMEM_SPEC] * 2 + [VMEM_SPEC] * (len(shard_xs) + 2) + [ANY_SPEC] * len(after),
                out_specs=VMEM_SPEC,
                compiler_params=limit(8),
                cost_estimate=cost(tokens, half, 1, 1),
                name=name,
            )(*lists, *shard_xs, *weights_a, *after)
        )

    rest_a = forward_a("forward_rest_a", [*fetched, *swapped], [cots[-1]])

    rest = cols - half
    groups = ((near_rows, row_total), (own_rows, near_rows), (0, own_rows))
    far_b, next_b, own_b, gate_b, up_b, turned = pl.pallas_call(
        functools.partial(load_forward_kernel, shards, groups, half, 1),
        out_shape=(
            *[shape(rest, stop - start, 2 * tile) for start, stop in groups],
            tile_shape(rest),
            tile_shape(rest),
            pltpu.VMEM((row_blocks, tile, row_total), BF16),
        ),
        in_specs=[SMEM_SPEC] * 2 + [VMEM_SPEC] * shards + [ANY_SPEC] * 4,
        out_specs=(VMEM_SPEC,) * 6,
        scratch_shapes=[pltpu.SemaphoreType.DMA((2, 3))],
        compiler_params=limit(8),
        cost_estimate=cost(row_total, rest, 1, 1, 5),
        name="forward_b",
    )(*lists, *xs, *from_hbm(gate_tiles, up_tiles), rest_a[0], near_a[-1])
    weights_b = [gate_b, up_b]
    own_b, next_b, far_b = to_owners(own_b), to_owners(next_b), to_owners(far_b)

    out_tiles = shape(*gate_tiles.shape)
    tile_bytes = slots * tile * tile * 2
    gate_out, up_out, hidden_a, acc_own, acc_next, acc_far = pl.pallas_call(
        functools.partial(first_half_kernel, members, owners),
        out_shape=(
            out_tiles,
            out_tiles,
            shape(row_total, half * tile),
            *[shape(row_blocks, rows, tile, dtype=F32) for rows in (own_rows, own_rows, far_rows)],
        ),
        in_specs=[SMEM_SPEC] * 2 + [VMEM_SPEC] * (3 + 3 * owners) + [ANY_SPEC] * 3,
        out_specs=(ANY_SPEC,) * 2 + (VMEM_SPEC,) * 4,
        scratch_shapes=[
            pltpu.VMEM((half, row_total, 2 * tile), BF16),
            tile_shape(half),
            tile_shape(half),
            pltpu.SemaphoreType.DMA((2, half)),
        ],
        compiler_params=limit(8 + 2 * half * tile_bytes // MIB),
        cost_estimate=cost(row_total, half, 2, 1, 1),
        name="first_half",
    )(
        *lists, *weights_a, turned, *near_a, *rest_a, *cots, far_b[0], next_b[0], own_b[0]
    )

    def second_half(name, chunk, acc, parts, after, weight):
        rows_here = len(chunk) * shard_rows
        return pl.pallas_call(
            functools.partial(second_half_kernel, chunk, owners, half),
            out_shape=(
                shape(rest, rows_here, 2 * tile),
                shape(rows_here, rest * tile),
                *[shape(shard_rows, width) for _ in chunk],
            ),
            in_specs=[SMEM_SPEC] * 2 + [VMEM_SPEC] * (3 + 2 * owners) + [ANY_SPEC],
            out_specs=(VMEM_SPEC,) * (2 + len(chunk)),
            scratch_shapes=[pltpu.VMEM((row_blocks, rows_here, tile), F32)],
            compiler_params=limit(8),
            cost_estimate=cost(rows_here, rest, 1, 1, weight),
            name=name,
        )(*lists, *weights_b, acc, *parts, *cots, after)

    far_grads, far_hidden, *far_dxs = second_half("far_b", far_members, acc_far, far_b, acc_own, 1)
    next_grads, next_hidden, next_dx = second_half("next_b", [1], acc_next, next_b, far_grads, 1)
    both_cores = []
    for mine, others in zip(far_dxs[: len(bases)], far_dxs[len(bases) :]):
        both_cores.append(
            pl.pallas_call(
                add_kernel,
                out_shape=shape(shard_rows, width),
                in_specs=[VMEM_SPEC] * 2 + [ANY_SPEC] * 2,
                out_specs=VMEM_SPEC,
                compiler_params=limit(8),
                cost_estimate=pl.CostEstimate(flops=0, bytes_accessed=0, transcendentals=0),
                name="add_cores",
            )(mine, swap(others, "sub", 1), next_grads, own_b[-1])
        )
    back_far = [swap_far(total, base) for total, base in zip(both_cores, bases)]
    back_next = swap(next_dx, "tok", 1)
    gate_out, up_out, hidden_out, own_dx = pl.pallas_call(
        functools.partial(last_half_kernel, members, owners, half),
        out_shape=(out_tiles, out_tiles, shape(*d_hidden.shape), shape(shard_rows, width)),
        in_specs=[SMEM_SPEC] * 2 + [VMEM_SPEC] * (9 + 2 * owners) + [ANY_SPEC] * 3,
        out_specs=(ANY_SPEC,) * 3 + (VMEM_SPEC,),
        scratch_shapes=[
            pltpu.VMEM((row_blocks, shard_rows, tile), F32),
            pltpu.VMEM((rest, shard_rows, 2 * tile), BF16),
            pltpu.VMEM((shard_rows, rest * tile), BF16),
            tile_shape(rest),
            tile_shape(rest),
            pltpu.SemaphoreType.DMA((2, rest)),
            pltpu.SemaphoreType.DMA((2, d_hidden.shape[0] // shard_rows)),
        ],
        input_output_aliases={11 + 2 * owners: 0, 12 + 2 * owners: 1},
        compiler_params=limit(8 + 2 * rest * tile_bytes // MIB),
        cost_estimate=cost(row_total, rest, 1, 1, 10),
        name="last_half",
    )(
        *lists,
        *weights_b,
        turned,
        acc_own,
        *own_b,
        *cots,
        next_grads,
        far_grads,
        hidden_a,
        next_hidden,
        far_hidden,
        gate_out,
        up_out,
        both_cores[-1],
    )
    arrived = [own_dx, back_next, *back_far]
    mine, mine_sent = pl.pallas_call(
        functools.partial(sum_kernel, len(arrived)),
        out_shape=(shape(shard_rows, width, dtype=F32), shape(shard_rows, width)),
        in_specs=[VMEM_SPEC] * len(arrived),
        out_specs=(VMEM_SPEC,) * 2,
        compiler_params=limit(8),
        name="sum_shards",
    )(*arrived)
    features_grad = (mine + swap(mine_sent, "sub", 1).astype(F32)).astype(BF16)
    return (hidden_out, gate_out, up_out, features_grad)


def solution(mesh):
    return jax.shard_map(
        on_device,
        mesh=mesh,
        in_specs=(
            P(("groups", "tok"), "blk"),
            P(("tok", "sub"), "blk", None, None, None),
            P(("tok", "sub"), "blk", None, None, None),
            P(("tok", "sub"), "blk", None),
            P(("tok", "sub"), "blk"),
            P(("groups", "blk"), ("tok", "sub")),
        ),
        out_specs=(
            P(("groups", "blk"), ("tok", "sub")),
            P(("groups", "tok", "sub"), "blk", None, None, None),
            P(("groups", "tok", "sub"), "blk", None, None, None),
            P(("groups", "tok"), "blk"),
        ),
        check_vma=False,
    )
```

```python
import functools

import jax
import jax.numpy as jnp
from jax import lax
from jax.experimental import pallas as pl
from jax.experimental.pallas import tpu as pltpu
from jax.sharding import PartitionSpec as P

F32 = jnp.float32
BF16 = jnp.bfloat16
MIB = 1 << 20
VMEM_SPEC = pl.BlockSpec(memory_space=pltpu.VMEM)
SMEM_SPEC = pl.BlockSpec(memory_space=pltpu.SMEM)
ANY_SPEC = pl.BlockSpec(memory_space=pl.ANY)


def limit(mib):
    return pltpu.CompilerParams(vmem_limit_bytes=mib * MIB)


def lanes(index, width):
    return pl.ds(pl.multiple_of(index * width, width), width)


def weights_of(c, gate_ref, up_ref):
    slots, rows, cols = gate_ref.shape[2:]
    return jnp.concatenate(
        [gate_ref[c, 0].reshape(slots * rows, cols), up_ref[c, 0].reshape(slots * rows, cols)], axis=1
    )


def keep(k, count, block):
    return jnp.where(k < count, block, jnp.zeros_like(block))


def forward_column(c, first, lists, xs, gate_ref, up_ref):
    rows_ref, counts_ref = lists
    slots, tile = gate_ref.shape[2:4]
    count = counts_ref[0, first + c]
    picked = []
    for k in range(slots):
        where = lanes(rows_ref[k, 0, first + c], tile)
        picked.append(keep(k, count, jnp.concatenate([x[:, where] for x in xs], axis=0)))
    return jnp.dot(
        jnp.concatenate(picked, axis=1), weights_of(c, gate_ref, up_ref), preferred_element_type=F32
    ).astype(BF16)


def groups_of(cols):
    edges = [0, -(-cols * 3 // 8), -(-cols * 6 // 8), cols]
    return [(start, stop) for start, stop in zip(edges, edges[1:]) if start < stop]


def load_tiles(first, cols, gate_hbm, up_hbm, gate_ref, up_ref, sems):
    def copies(i, start, stop):
        return [
            pltpu.make_async_copy(
                source.at[pl.ds(first + start, stop - start)], target.at[pl.ds(start, stop - start)], sems.at[j, i]
            )
            for j, (source, target) in enumerate(((gate_hbm, gate_ref), (up_hbm, up_ref)))
        ]

    started = {start: copies(i, start, stop) for i, (start, stop) in enumerate(groups_of(cols))}
    for group in started.values():
        for copy in group:
            copy.start()

    def arrive(c):
        for copy in started.get(c, ()):
            copy.wait()

    return arrive


def store_tiles(first, c, gate_ref, up_ref, gate_hbm, up_hbm, sems):
    copies = [
        pltpu.make_async_copy(gate_ref.at[c], gate_hbm.at[first + c], sems.at[0, c]),
        pltpu.make_async_copy(up_ref.at[c], up_hbm.at[first + c], sems.at[1, c]),
    ]
    for copy in copies:
        copy.start()
    return copies


def forward_own_kernel(x_hbm, rows_hbm, counts_hbm, gate_hbm, up_hbm, part_ref, gate_ref, up_ref, rows_ref, counts_ref, *scratch):
    x_ref, sems, small_sems = scratch
    cols = gate_ref.shape[0]
    small = [
        pltpu.make_async_copy(source, target, small_sems.at[i])
        for i, (source, target) in enumerate(((rows_hbm, rows_ref), (counts_hbm, counts_ref), (x_hbm, x_ref)))
    ]
    for copy in small:
        copy.start()
    arrive = load_tiles(0, cols, gate_hbm, up_hbm, gate_ref, up_ref, sems)
    for copy in small:
        copy.wait()
    for start, stop in groups_of(cols):
        arrive(start)
        found = [
            forward_column(c, 0, (rows_ref, counts_ref), [x_ref], gate_ref, up_ref) for c in range(start, stop)
        ]
        for c in range(start, stop):
            part_ref[c] = found[c - start]


def forward_kernel(members, rows_ref, counts_ref, *refs):
    xs = refs[:members]
    gate_ref, up_ref = refs[members : members + 2]
    part_ref = refs[-1]
    for start, stop in groups_of(gate_ref.shape[0]):
        found = [
            forward_column(c, 0, (rows_ref, counts_ref), xs, gate_ref, up_ref) for c in range(start, stop)
        ]
        for c in range(start, stop):
            part_ref[c] = found[c - start]


def load_forward_kernel(members, groups, first, turn, rows_ref, counts_ref, *refs):
    xs = refs[:members]
    gate_hbm, up_hbm = refs[members : members + 2]
    outs = refs[-(len(groups) + 3 + turn) :]
    parts, gate_ref, up_ref, sems = outs[: len(groups)], outs[-3 - turn], outs[-2 - turn], outs[-1]
    cols, _, _, tile, _ = gate_ref.shape
    arrive = load_tiles(first, cols, gate_hbm, up_hbm, gate_ref, up_ref, sems)
    if turn:
        turned_ref = outs[-2]
        identity = (
            lax.broadcasted_iota(jnp.int32, (tile, tile), 0) == lax.broadcasted_iota(jnp.int32, (tile, tile), 1)
        ).astype(F32).astype(BF16)
        for r in range(turned_ref.shape[0]):
            block = jnp.concatenate([x[:, r * tile : (r + 1) * tile] for x in xs], axis=0)
            turned_ref[r] = lax.dot_general(
                identity, block, (((1,), (1,)), ((), ())), preferred_element_type=F32
            ).astype(BF16)
    for begin, end in groups_of(cols):
        arrive(begin)
        found = [
            forward_column(c, first, (rows_ref, counts_ref), xs, gate_ref, up_ref) for c in range(begin, end)
        ]
        for c in range(begin, end):
            for (start, stop), part_ref in zip(groups, parts):
                part_ref[c] = found[c - begin][start:stop]


def shard_of(member):
    if member < 2:
        return lax.axis_index("tok") ^ member
    return lax.axis_index("tok") ^ ((member & ~1) + ((member & 1) ^ lax.axis_index("sub")))


def cotangent_of(members, cots, shard_rows, where):
    shards_each = cots[0].shape[0] // shard_rows
    blocks = []
    for member in members:
        shard = shard_of(member)
        source = (shard // shards_each) ^ lax.axis_index("blk")
        rows = pl.ds(pl.multiple_of((shard % shards_each) * shard_rows, shard_rows), shard_rows)
        block = cots[0][rows, where]
        for j, cot in enumerate(cots[1:], 1):
            block = jnp.where(source == j, cot[rows, where], block)
        blocks.append(block.astype(F32))
    return jnp.concatenate(blocks, axis=0)


def nonlinear(total, cotangent):
    tile = total.shape[1] // 2
    gate_value, up_value = total[:, :tile], total[:, tile:]
    sig_gate = jax.nn.sigmoid(gate_value)
    act_gate = gate_value * sig_gate
    hidden = (act_gate * up_value).astype(BF16)
    gate_grad = (cotangent * up_value * sig_gate * (1.0 + gate_value * (1.0 - sig_gate))).astype(BF16)
    up_grad = (cotangent * act_gate).astype(BF16)
    return hidden, jnp.concatenate([gate_grad, up_grad], axis=1)


def total_of(c, parts):
    total = parts[0][c].astype(F32)
    for part in parts[1:]:
        total = total + part[c].astype(F32)
    return total


def elementwise(members, parts_of, cots, first, shard_rows, hidden_ref, grads_ref):
    cols, _, width = grads_ref.shape
    tile = width // 2
    for start in range(0, cols, 2):
        found = []
        for c in range(start, min(start + 2, cols)):
            where = slice((first + c) * tile, (first + c + 1) * tile)
            found.append(nonlinear(parts_of(c), cotangent_of(members, cots, shard_rows, where)))
        for c, (hidden, grads) in enumerate(found, start):
            hidden_ref[:, c * tile : (c + 1) * tile] = hidden
            grads_ref[c] = grads


def add_back(first, lists, grads_ref, gate_ref, up_ref, accs):
    rows_ref, counts_ref = lists
    cols, _, slots, tile, _ = gate_ref.shape
    step = slots // 3 if grads_ref.shape[1] > 64 else slots // 2

    def product(c, k):
        tiles = [w[c, 0, k : k + step].reshape(step * tile, tile) for w in (gate_ref, up_ref)]
        return lax.dot_general(
            grads_ref[c], jnp.concatenate(tiles, axis=1), (((1,), (1,)), ((), ())), preferred_element_type=F32
        )

    def add(c, k, back):
        count = counts_ref[0, first + c]
        rows = [rows_ref[k + i, 0, first + c] for i in range(step)]
        start = 0
        for acc in accs:
            stop = start + acc.shape[1]
            sums = [
                acc[row] + keep(k + i, count, back[start:stop, i * tile : (i + 1) * tile])
                for i, row in enumerate(rows)
            ]
            for row, value in zip(rows, sums):
                acc[row] = value
            start = stop

    waiting = None
    for c in range(cols):
        for k in range(0, slots, step):
            back = product(c, k)
            if waiting is not None:
                add(*waiting)
            waiting = (c, k, back)
    add(*waiting)


def tile_grads(c, first, lists, turned_ref, grads, gate_ref, up_ref):
    rows_ref, counts_ref = lists
    slots, tile = gate_ref.shape[2:4]
    picked = jnp.concatenate([turned_ref[rows_ref[k, 0, first + c]] for k in range(slots)], axis=0)
    found = jnp.dot(picked, grads, preferred_element_type=F32)
    for k in range(slots):
        term = keep(k, counts_ref[0, first + c], found[k * tile : (k + 1) * tile]).astype(BF16)
        gate_ref[c, 0, k] = term[:, :tile]
        up_ref[c, 0, k] = term[:, tile:]


def start_hidden(members, parts, hidden_hbm, shard_rows, sems):
    shards_each = hidden_hbm.shape[0] // shard_rows

    def copies(i, member):
        rows = pl.ds(i * shard_rows, shard_rows)
        return [
            pltpu.make_async_copy(
                array.at[pl.ds(row, shard_rows)], hidden_hbm.at[rows, pl.ds(first, array.shape[1])], sems.at[j, i]
            )
            for j, (array, row, first) in enumerate(parts(member))
        ]

    for i in range(shards_each):
        wanted = lax.axis_index("blk") * shards_each + i
        for member in members:

            @pl.when(shard_of(member) == wanted)
            def _(i=i, member=member):
                for copy in copies(i, member):
                    copy.start()

    return [copy for i in range(shards_each) for copy in copies(i, 0)]


def first_half_kernel(members, owners, rows_ref, counts_ref, gate_w, up_w, turned_ref, *refs):
    near, rest, cots = refs[:owners], refs[owners : 2 * owners], refs[2 * owners : 3 * owners]
    gate_hbm, up_hbm, hidden_ref, acc_near, acc_far, grads_ref, gate_ref, up_ref, sems = refs[-9:]
    cols = gate_ref.shape[0]
    shard_rows = hidden_ref.shape[0] // members
    lists = (rows_ref, counts_ref)
    acc_near[...] = jnp.zeros_like(acc_near)
    acc_far[...] = jnp.zeros_like(acc_far)
    elementwise(
        range(members),
        lambda c: jnp.concatenate([total_of(c, near), total_of(c, rest)], axis=0),
        cots,
        0,
        shard_rows,
        hidden_ref,
        grads_ref,
    )
    copies = []
    for c in range(cols):
        tile_grads(c, 0, lists, turned_ref, grads_ref[c], gate_ref, up_ref)
        copies += store_tiles(0, c, gate_ref, up_ref, gate_hbm, up_hbm, sems)
    add_back(0, lists, grads_ref, gate_w, up_w, (acc_near, acc_far))
    for copy in copies:
        copy.wait()


def second_half_kernel(members, owners, first, rows_ref, counts_ref, gate_w, up_w, acc_in, *refs):
    parts, cots = refs[:owners], refs[owners : 2 * owners]
    outs = refs[-(2 + len(members) + 1) :]
    grads_ref, hidden_ref = outs[:2]
    dxs, acc_ref = outs[2:-1], outs[-1]
    tile = gate_w.shape[3]
    shard_rows = hidden_ref.shape[0] // len(members)
    acc_ref[...] = acc_in[...]
    elementwise(members, lambda c: total_of(c, parts), cots, first, shard_rows, hidden_ref, grads_ref)
    add_back(first, (rows_ref, counts_ref), grads_ref, gate_w, up_w, (acc_ref,))
    for r in range(acc_ref.shape[0]):
        block = acc_ref[r].astype(BF16)
        for m, dx in enumerate(dxs):
            dx[:, r * tile : (r + 1) * tile] = block[m * shard_rows : (m + 1) * shard_rows]


def last_grads_kernel(members, first, rows_ref, counts_ref, turned_ref, *refs):
    near_grads, far_grads, hidden_a, near_hidden, far_hidden = refs[:5]
    gate_hbm, up_hbm, hidden_hbm, token_ref, gate_ref, up_ref, sems, hidden_sems = refs[-8:]
    cols, _, _, tile, _ = gate_ref.shape
    shard_rows = near_hidden.shape[0] // 2
    token_ref[...] = jnp.zeros_like(token_ref)

    def parts(m):
        mine = (near_hidden, m * shard_rows) if m < 2 else (far_hidden, (m - 2) * shard_rows)
        return (hidden_a, m * shard_rows, 0), (*mine, first * tile)

    copies = start_hidden(range(members), parts, hidden_hbm, shard_rows, hidden_sems)
    for c in range(cols):
        grads = jnp.concatenate([near_grads[c], far_grads[c]], axis=0)
        tile_grads(c, first, (rows_ref, counts_ref), turned_ref, grads, gate_ref, up_ref)
        copies += store_tiles(first, c, gate_ref, up_ref, gate_hbm, up_hbm, sems)
    for copy in copies:
        copy.wait()


def copy_kernel(x_ref, _, out_ref):
    out_ref[...] = x_ref[...]


def add_kernel(left_ref, right_ref, out_ref):
    out_ref[...] = (left_ref[...].astype(F32) + right_ref[...].astype(F32)).astype(BF16)


def sum_kernel(count, *refs):
    total = sum(ref[...].astype(F32) for ref in refs[:count])
    refs[-2][...] = total
    refs[-1][...] = total.astype(BF16)


def swap(x, axis, step):
    return lax.ppermute(x, axis, [(i, i ^ step) for i in range(lax.axis_size(axis))])


def swap_far(x, base):
    shards, cores = lax.axis_size("tok"), lax.axis_size("sub")
    pairs = [(t * cores + s, (t ^ (base + s)) * cores + s) for t in range(shards) for s in range(cores)]
    return lax.ppermute(x, ("tok", "sub"), pairs)


def on_device(features_in, gate_tiles, up_tiles, block_rows, block_counts, d_hidden):
    shards, owners = lax.axis_size("tok"), lax.axis_size("blk")
    cols, _, slots, tile, _ = gate_tiles.shape
    shard_rows, width = features_in.shape
    row_blocks = width // tile
    row_total = shards * shard_rows
    near_rows = 2 * shard_rows
    half = max(1, cols // 2)
    bases = range(2, shards, 2)
    lists = (jnp.transpose(block_rows, (2, 1, 0)), jnp.transpose(block_counts, (1, 0)))

    def shape(*dims, dtype=BF16):
        return jax.ShapeDtypeStruct(dims, dtype)

    def cost(tokens, columns, products, tile_bytes, weight=1):
        tiles = weight * columns * slots
        return pl.CostEstimate(
            flops=4 * tokens * tiles * tile * tile * products,
            bytes_accessed=4 * tiles * tile * tile * tile_bytes,
            transcendentals=0,
        )

    def to_owners(part):
        return [part] + [swap(part, "blk", s) for s in range(1, owners)]

    fars = [swap_far(features_in, base) for base in bases]
    xs = [features_in, swap(features_in, "tok", 1)]
    cots = [d_hidden] + [swap(d_hidden, "blk", s) for s in range(1, owners)]

    def tile_shape(columns):
        return pltpu.VMEM((columns, 1, slots, tile, tile), BF16)

    def from_hbm(*arrays):
        return [pltpu.with_memory_space_constraint(array, pltpu.HBM) for array in arrays]

    near_a, *weights_a, rows_held, counts_held = pl.pallas_call(
        forward_own_kernel,
        out_shape=(
            shape(half, shard_rows, 2 * tile),
            tile_shape(half),
            tile_shape(half),
            pltpu.SMEM(lists[0].shape, jnp.int32),
            pltpu.SMEM(lists[1].shape, jnp.int32),
        ),
        in_specs=[ANY_SPEC] * 5,
        out_specs=(VMEM_SPEC,) * 3 + (SMEM_SPEC,) * 2,
        scratch_shapes=[
            pltpu.VMEM((shard_rows, width), BF16),
            pltpu.SemaphoreType.DMA((2, 3)),
            pltpu.SemaphoreType.DMA((3,)),
        ],
        compiler_params=limit(8),
        cost_estimate=cost(shard_rows, half, 1, 1),
        name="forward_own_a",
    )(*from_hbm(features_in, *lists, gate_tiles, up_tiles))
    near_a = to_owners(near_a)
    lists = (rows_held, counts_held)

    for far in fars:
        ready = pl.pallas_call(
            copy_kernel,
            out_shape=shape(shard_rows, width),
            in_specs=[VMEM_SPEC, ANY_SPEC],
            out_specs=VMEM_SPEC,
            compiler_params=limit(8),
            cost_estimate=pl.CostEstimate(flops=0, bytes_accessed=0, transcendentals=0),
            name="after_own",
        )(far, near_a[0])
        xs += [far, swap(ready, "sub", 1)]

    rest_a = pl.pallas_call(
        functools.partial(forward_kernel, shards - 1),
        out_shape=shape(half, row_total - shard_rows, 2 * tile),
        in_specs=[SMEM_SPEC] * 2 + [VMEM_SPEC] * (shards + 1) + [ANY_SPEC],
        out_specs=VMEM_SPEC,
        compiler_params=limit(8),
        cost_estimate=cost(row_total, half, 1, 1),
        name="forward_rest_a",
    )(*lists, *xs[1:], *weights_a, cots[-1])
    rest_a = to_owners(rest_a)

    rest = cols - half
    far_b, near_b, gate_b, up_b, turned = pl.pallas_call(
        functools.partial(load_forward_kernel, shards, ((near_rows, row_total), (0, near_rows)), half, 1),
        out_shape=(
            shape(rest, row_total - near_rows, 2 * tile),
            shape(rest, near_rows, 2 * tile),
            tile_shape(rest),
            tile_shape(rest),
            pltpu.VMEM((row_blocks, tile, row_total), BF16),
        ),
        in_specs=[SMEM_SPEC] * 2 + [VMEM_SPEC] * shards + [ANY_SPEC] * 4,
        out_specs=(VMEM_SPEC,) * 5,
        scratch_shapes=[pltpu.SemaphoreType.DMA((2, 3))],
        compiler_params=limit(8),
        cost_estimate=cost(row_total, rest, 1, 1, 5),
        name="forward_b",
    )(*lists, *xs, *from_hbm(gate_tiles, up_tiles), rest_a[0], near_a[-1])
    weights_b = [gate_b, up_b]
    far_b, near_b = to_owners(far_b), to_owners(near_b)

    out_tiles = shape(*gate_tiles.shape)
    tile_bytes = slots * tile * tile * 2
    gate_out, up_out, hidden_a, acc_near, acc_far = pl.pallas_call(
        functools.partial(first_half_kernel, shards, owners),
        out_shape=(
            out_tiles,
            out_tiles,
            shape(row_total, half * tile),
            shape(row_blocks, near_rows, tile, dtype=F32),
            shape(row_blocks, row_total - near_rows, tile, dtype=F32),
        ),
        in_specs=[SMEM_SPEC] * 2 + [VMEM_SPEC] * (3 + 3 * owners) + [ANY_SPEC] * 2,
        out_specs=(ANY_SPEC,) * 2 + (VMEM_SPEC,) * 3,
        scratch_shapes=[
            pltpu.VMEM((half, row_total, 2 * tile), BF16),
            tile_shape(half),
            tile_shape(half),
            pltpu.SemaphoreType.DMA((2, half)),
        ],
        compiler_params=limit(8 + 2 * half * tile_bytes // MIB),
        cost_estimate=cost(row_total, half, 2, 1, 1),
        name="first_half",
    )(*lists, *weights_a, turned, *near_a, *rest_a, *cots, far_b[0], near_b[0])

    def second_half(members, acc, parts, after, weight):
        rows_here = len(members) * shard_rows
        return pl.pallas_call(
            functools.partial(second_half_kernel, members, owners, half),
            out_shape=(
                shape(rest, rows_here, 2 * tile),
                shape(rows_here, rest * tile),
                *[shape(shard_rows, width) for _ in members],
            ),
            in_specs=[SMEM_SPEC] * 2 + [VMEM_SPEC] * (3 + 2 * owners) + [ANY_SPEC],
            out_specs=(VMEM_SPEC,) * (2 + len(members)),
            scratch_shapes=[pltpu.VMEM((row_blocks, rows_here, tile), F32)],
            compiler_params=limit(8),
            cost_estimate=cost(rows_here, rest, 1, 1, weight),
            name="second_half",
        )(*lists, *weights_b, acc, *parts, *cots, after)

    far_grads, far_hidden, *far_dxs = second_half(range(2, shards), acc_far, far_b, acc_near, 1)
    both_cores = []
    for mine, others in zip(far_dxs[::2], far_dxs[1::2]):
        other = swap(others, "sub", 1)
        both_cores.append(
            pl.pallas_call(
                add_kernel,
                out_shape=shape(shard_rows, width),
                in_specs=[VMEM_SPEC] * 2,
                out_specs=VMEM_SPEC,
                compiler_params=limit(8),
                cost_estimate=pl.CostEstimate(flops=0, bytes_accessed=0, transcendentals=0),
                name="add_cores",
            )(mine, other)
        )
    back_far = [swap_far(total, base) for total, base in zip(both_cores, bases)]

    near_grads, near_hidden, own_dx, next_dx = second_half(range(2), acc_near, near_b, both_cores[-1], 1)
    back_next = swap(next_dx, "tok", 1)

    gate_out, up_out, hidden_out, token = pl.pallas_call(
        functools.partial(last_grads_kernel, shards, half),
        out_shape=(out_tiles, out_tiles, shape(*d_hidden.shape), shape(8, tile, dtype=F32)),
        in_specs=[SMEM_SPEC] * 2 + [VMEM_SPEC] * 6 + [ANY_SPEC] * 2,
        out_specs=(ANY_SPEC,) * 3 + (VMEM_SPEC,),
        scratch_shapes=[
            tile_shape(rest),
            tile_shape(rest),
            pltpu.SemaphoreType.DMA((2, rest)),
            pltpu.SemaphoreType.DMA((2, d_hidden.shape[0] // shard_rows)),
        ],
        input_output_aliases={8: 0, 9: 1},
        compiler_params=limit(8 + 2 * rest * tile_bytes // MIB),
        cost_estimate=cost(row_total, rest, 1, 1, 10),
        name="last_grads",
    )(*lists, turned, near_grads, far_grads, hidden_a, near_hidden, far_hidden, gate_out, up_out)
    arrived = [own_dx, back_next, *back_far]
    mine, mine_sent = pl.pallas_call(
        functools.partial(sum_kernel, len(arrived)),
        out_shape=(shape(shard_rows, width, dtype=F32), shape(shard_rows, width)),
        in_specs=[VMEM_SPEC] * len(arrived) + [ANY_SPEC],
        out_specs=(VMEM_SPEC,) * 2,
        compiler_params=limit(8),
        name="sum_shards",
    )(*arrived, token)
    features_grad = (mine + swap(mine_sent, "sub", 1).astype(F32)).astype(BF16)
    return (hidden_out, gate_out, up_out, features_grad)


def solution(mesh):
    return jax.shard_map(
        on_device,
        mesh=mesh,
        in_specs=(
            P(("groups", "tok"), "blk"),
            P(("tok", "sub"), "blk", None, None, None),
            P(("tok", "sub"), "blk", None, None, None),
            P(("tok", "sub"), "blk", None),
            P(("tok", "sub"), "blk"),
            P(("groups", "blk"), ("tok", "sub")),
        ),
        out_specs=(
            P(("groups", "blk"), ("tok", "sub")),
            P(("groups", "tok", "sub"), "blk", None, None, None),
            P(("groups", "tok", "sub"), "blk", None, None, None),
            P(("groups", "tok"), "blk"),
        ),
        check_vma=False,
    )
```

```python
import functools

import jax
import jax.numpy as jnp
from jax import lax
from jax.experimental import pallas as pl
from jax.experimental.pallas import tpu as pltpu
from jax.sharding import PartitionSpec as P

F32 = jnp.float32
BF16 = jnp.bfloat16
MIB = 1 << 20
VMEM_SPEC = pl.BlockSpec(memory_space=pltpu.VMEM)
SMEM_SPEC = pl.BlockSpec(memory_space=pltpu.SMEM)
ANY_SPEC = pl.BlockSpec(memory_space=pl.ANY)


def limit(mib):
    return pltpu.CompilerParams(vmem_limit_bytes=mib * MIB)


def lanes(index, width):
    return pl.ds(pl.multiple_of(index * width, width), width)


def weights_of(c, gate_ref, up_ref):
    slots, rows, cols = gate_ref.shape[2:]
    return jnp.concatenate(
        [gate_ref[c, 0].reshape(slots * rows, cols), up_ref[c, 0].reshape(slots * rows, cols)], axis=1
    )


def keep(k, count, block):
    return jnp.where(k < count, block, jnp.zeros_like(block))


def forward_column(c, first, lists, xs, gate_ref, up_ref):
    rows_ref, counts_ref = lists
    slots, tile = gate_ref.shape[2:4]
    count = counts_ref[0, first + c]
    picked = []
    for k in range(slots):
        where = lanes(rows_ref[k, 0, first + c], tile)
        picked.append(keep(k, count, jnp.concatenate([x[:, where] for x in xs], axis=0)))
    return jnp.dot(
        jnp.concatenate(picked, axis=1), weights_of(c, gate_ref, up_ref), preferred_element_type=F32
    ).astype(BF16)


def groups_of(cols):
    edges = [0, -(-cols * 3 // 8), -(-cols * 6 // 8), cols]
    return [(start, stop) for start, stop in zip(edges, edges[1:]) if start < stop]


def load_tiles(first, cols, gate_hbm, up_hbm, gate_ref, up_ref, sems):
    def copies(i, start, stop):
        return [
            pltpu.make_async_copy(
                source.at[pl.ds(first + start, stop - start)], target.at[pl.ds(start, stop - start)], sems.at[j, i]
            )
            for j, (source, target) in enumerate(((gate_hbm, gate_ref), (up_hbm, up_ref)))
        ]

    started = {start: copies(i, start, stop) for i, (start, stop) in enumerate(groups_of(cols))}
    for group in started.values():
        for copy in group:
            copy.start()

    def arrive(c):
        for copy in started.get(c, ()):
            copy.wait()

    return arrive


def store_tiles(first, c, gate_ref, up_ref, gate_hbm, up_hbm, sems):
    copies = [
        pltpu.make_async_copy(gate_ref.at[c], gate_hbm.at[first + c], sems.at[0, c]),
        pltpu.make_async_copy(up_ref.at[c], up_hbm.at[first + c], sems.at[1, c]),
    ]
    for copy in copies:
        copy.start()
    return copies


def forward_own_kernel(x_hbm, rows_hbm, counts_hbm, gate_hbm, up_hbm, part_ref, gate_ref, up_ref, rows_ref, counts_ref, *scratch):
    x_ref, sems, small_sems = scratch
    cols = gate_ref.shape[0]
    small = [
        pltpu.make_async_copy(source, target, small_sems.at[i])
        for i, (source, target) in enumerate(((rows_hbm, rows_ref), (counts_hbm, counts_ref), (x_hbm, x_ref)))
    ]
    for copy in small:
        copy.start()
    arrive = load_tiles(0, cols, gate_hbm, up_hbm, gate_ref, up_ref, sems)
    for copy in small:
        copy.wait()
    for c in range(cols):
        arrive(c)
        part_ref[c] = forward_column(c, 0, (rows_ref, counts_ref), [x_ref], gate_ref, up_ref)


def forward_kernel(members, rows_ref, counts_ref, *refs):
    xs = refs[:members]
    gate_ref, up_ref = refs[members : members + 2]
    part_ref = refs[-1]
    for c in range(gate_ref.shape[0]):
        part_ref[c] = forward_column(c, 0, (rows_ref, counts_ref), xs, gate_ref, up_ref)


def unit(size):
    row, column = (lax.broadcasted_iota(jnp.int32, (size, size), axis) for axis in (0, 1))
    return (row == column).astype(F32).astype(BF16)


def load_forward_kernel(members, groups, first, turn, rows_ref, counts_ref, *refs):
    xs = refs[:members]
    gate_hbm, up_hbm = refs[members : members + 2]
    outs = refs[-(len(groups) + 3 + turn) :]
    parts, gate_ref, up_ref, sems = outs[: len(groups)], outs[-3 - turn], outs[-2 - turn], outs[-1]
    cols, _, _, tile, _ = gate_ref.shape
    arrive = load_tiles(first, cols, gate_hbm, up_hbm, gate_ref, up_ref, sems)
    if turn:
        turned_ref = outs[-2]
        identity = unit(tile)
        for r in range(turned_ref.shape[0]):
            block = jnp.concatenate([x[:, r * tile : (r + 1) * tile] for x in xs], axis=0)
            turned_ref[r] = lax.dot_general(
                identity, block, (((1,), (1,)), ((), ())), preferred_element_type=F32
            ).astype(BF16)
    for c in range(cols):
        arrive(c)
        part = forward_column(c, first, (rows_ref, counts_ref), xs, gate_ref, up_ref)
        for (start, stop), part_ref in zip(groups, parts):
            part_ref[c] = part[start:stop]


def shard_of(member):
    if member < 2:
        return lax.axis_index("tok") ^ member
    return lax.axis_index("tok") ^ ((member & ~1) + ((member & 1) ^ lax.axis_index("sub")))


def cotangent_of(members, cots, shard_rows, where):
    shards_each = cots[0].shape[0] // shard_rows
    blocks = []
    for member in members:
        shard = shard_of(member)
        source = (shard // shards_each) ^ lax.axis_index("blk")
        rows = pl.ds(pl.multiple_of((shard % shards_each) * shard_rows, shard_rows), shard_rows)
        block = cots[0][rows, where]
        for j, cot in enumerate(cots[1:], 1):
            block = jnp.where(source == j, cot[rows, where], block)
        blocks.append(block.astype(F32))
    return jnp.concatenate(blocks, axis=0)


def nonlinear(total, cotangent):
    tile = total.shape[1] // 2
    gate_value, up_value = total[:, :tile], total[:, tile:]
    sig_gate = jax.nn.sigmoid(gate_value)
    act_gate = gate_value * sig_gate
    hidden = (act_gate * up_value).astype(BF16)
    gate_grad = (cotangent * up_value * sig_gate * (1.0 + gate_value * (1.0 - sig_gate))).astype(BF16)
    up_grad = (cotangent * act_gate).astype(BF16)
    return hidden, jnp.concatenate([gate_grad, up_grad], axis=1)


def total_of(c, parts):
    total = parts[0][c].astype(F32)
    for part in parts[1:]:
        total = total + part[c].astype(F32)
    return total


def back_terms(c, grads, gate_ref, up_ref):
    return lax.dot_general(
        grads, weights_of(c, gate_ref, up_ref), (((1,), (1,)), ((), ())), preferred_element_type=F32
    )


def turn_kernel(gate_ref, up_ref, _, turned_ref):
    cols, _, slots, rows, tile = gate_ref.shape
    identity = unit(tile)
    for c in range(cols):
        for i, tiles in enumerate((gate_ref, up_ref)):
            turned_ref[c, i * tile : (i + 1) * tile] = lax.dot_general(
                identity,
                tiles[c, 0].reshape(slots * rows, tile),
                (((1,), (1,)), ((), ())),
                preferred_element_type=F32,
            ).astype(BF16)


def add_back(c, lists, back, accs, slots, tile):
    rows_ref, counts_ref = lists
    rows = [rows_ref[k, 0, c] for k in range(slots)]
    start = 0
    for acc in accs:
        stop = start + acc.shape[1]
        sums = [
            acc[rows[k]] + keep(k, counts_ref[0, c], back[start:stop, k * tile : (k + 1) * tile])
            for k in range(slots)
        ]
        for k in range(slots):
            acc[rows[k]] = sums[k]
        start = stop


def tile_grads(c, first, lists, turned_ref, grads, gate_ref, up_ref):
    rows_ref, counts_ref = lists
    slots, tile = gate_ref.shape[2:4]
    picked = jnp.concatenate([turned_ref[rows_ref[k, 0, first + c]] for k in range(slots)], axis=0)
    found = jnp.dot(picked, grads, preferred_element_type=F32)
    for k in range(slots):
        term = keep(k, counts_ref[0, first + c], found[k * tile : (k + 1) * tile]).astype(BF16)
        gate_ref[c, 0, k] = term[:, :tile]
        up_ref[c, 0, k] = term[:, tile:]


def start_hidden(members, parts, hidden_hbm, shard_rows, sems):
    shards_each = hidden_hbm.shape[0] // shard_rows

    def copies(i, member):
        rows = pl.ds(i * shard_rows, shard_rows)
        return [
            pltpu.make_async_copy(
                array.at[pl.ds(row, shard_rows)], hidden_hbm.at[rows, pl.ds(first, array.shape[1])], sems.at[j, i]
            )
            for j, (array, row, first) in enumerate(parts(member))
        ]

    for i in range(shards_each):
        wanted = lax.axis_index("blk") * shards_each + i
        for member in members:

            @pl.when(shard_of(member) == wanted)
            def _(i=i, member=member):
                for copy in copies(i, member):
                    copy.start()

    return [copy for i in range(shards_each) for copy in copies(i, 0)]


def first_half_kernel(members, owners, rows_ref, counts_ref, gate_w, up_w, turned_ref, *refs):
    groups = [refs[start : start + owners] for start in range(0, 2 * owners, owners)]
    cots = refs[2 * owners : 3 * owners]
    gate_hbm, up_hbm, hidden_ref = refs[-10:-7]
    accs = refs[-7:-4]
    grads_ref, gate_ref, up_ref, sems = refs[-4:]
    cols, _, slots, tile, _ = gate_ref.shape
    shard_rows = hidden_ref.shape[0] // len(members)
    lists = (rows_ref, counts_ref)
    for acc in accs:
        acc[...] = jnp.zeros_like(acc)
    copies = []
    for c in range(cols):
        total = jnp.concatenate([total_of(c, parts) for parts in groups], axis=0)
        where = slice(c * tile, (c + 1) * tile)
        hidden, grads = nonlinear(total, cotangent_of(members, cots, shard_rows, where))
        hidden_ref[:, where] = hidden
        grads_ref[c] = grads
        tile_grads(c, 0, lists, turned_ref, grads, gate_ref, up_ref)
        copies += store_tiles(0, c, gate_ref, up_ref, gate_hbm, up_hbm, sems)
    for c in range(cols):
        add_back(c, lists, back_terms(c, grads_ref[c], gate_w, up_w), accs, slots, tile)
    for copy in copies:
        copy.wait()


def second_half_kernel(members, owners, first, slots, rows_ref, counts_ref, turned_w, acc_in, *refs):
    parts, cots = refs[:owners], refs[owners : 2 * owners]
    outs = refs[-(2 + len(members) + 1) :]
    grads_ref, hidden_ref = outs[:2]
    dxs, acc_ref = outs[2:-1], outs[-1]
    cols, tile = turned_w.shape[0], turned_w.shape[1] // 2
    shard_rows = hidden_ref.shape[0] // len(members)
    acc_ref[...] = acc_in[...]
    for c in range(cols):
        where = slice((first + c) * tile, (first + c + 1) * tile)
        hidden, grads = nonlinear(total_of(c, parts), cotangent_of(members, cots, shard_rows, where))
        hidden_ref[:, c * tile : (c + 1) * tile] = hidden
        grads_ref[c] = grads
        back = jnp.dot(grads, turned_w[c], preferred_element_type=F32)
        add_back(first + c, (rows_ref, counts_ref), back, (acc_ref,), slots, tile)
    for r in range(acc_ref.shape[0]):
        block = acc_ref[r].astype(BF16)
        for m, dx in enumerate(dxs):
            dx[:, r * tile : (r + 1) * tile] = block[m * shard_rows : (m + 1) * shard_rows]


def last_half_kernel(members, owners, first, rows_ref, counts_ref, turned_w, turned_ref, acc_in, *refs):
    parts, cots = refs[:owners], refs[owners : 2 * owners]
    next_grads, far_grads, hidden_a, next_hidden, far_hidden = refs[2 * owners : 2 * owners + 5]
    gate_hbm, up_hbm, hidden_hbm, dx_ref = refs[-11:-7]
    acc_ref, grads_ref, hidden_ref, gate_ref, up_ref, sems, hidden_sems = refs[-7:]
    cols, _, slots, tile, _ = gate_ref.shape
    shard_rows = hidden_ref.shape[0]
    lists = (rows_ref, counts_ref)

    def hidden_of(member):
        at = members.index(member)
        mine = ((hidden_ref, 0), (next_hidden, 0))[at] if at < 2 else (far_hidden, (at - 2) * shard_rows)
        return (hidden_a, at * shard_rows, 0), (*mine, first * tile)

    acc_ref[...] = acc_in[...]
    copies = []
    for c in range(cols):
        where = slice((first + c) * tile, (first + c + 1) * tile)
        hidden, grads = nonlinear(total_of(c, parts), cotangent_of(members[:1], cots, shard_rows, where))
        hidden_ref[:, c * tile : (c + 1) * tile] = hidden
        grads_ref[c] = grads
        grads = jnp.concatenate([grads, next_grads[c], far_grads[c]], axis=0)
        tile_grads(c, first, lists, turned_ref, grads, gate_ref, up_ref)
        copies += store_tiles(first, c, gate_ref, up_ref, gate_hbm, up_hbm, sems)
    copies += start_hidden(members, hidden_of, hidden_hbm, shard_rows, hidden_sems)
    for c in range(cols):
        back = jnp.dot(grads_ref[c], turned_w[c], preferred_element_type=F32)
        add_back(first + c, lists, back, (acc_ref,), slots, tile)
    for r in range(acc_ref.shape[0]):
        dx_ref[:, r * tile : (r + 1) * tile] = acc_ref[r].astype(BF16)
    for copy in copies:
        copy.wait()


def copy_kernel(x_ref, _, out_ref):
    out_ref[...] = x_ref[...]


def add_kernel(left_ref, right_ref, _, out_ref):
    out_ref[...] = (left_ref[...].astype(F32) + right_ref[...].astype(F32)).astype(BF16)


def sum_kernel(count, *refs):
    total = sum(ref[...].astype(F32) for ref in refs[:count])
    refs[-2][...] = total
    refs[-1][...] = total.astype(BF16)


def swap(x, axis, step):
    return lax.ppermute(x, axis, [(i, i ^ step) for i in range(lax.axis_size(axis))])


def swap_far(x, base):
    shards, cores = lax.axis_size("tok"), lax.axis_size("sub")
    pairs = [(t * cores + s, (t ^ (base + s)) * cores + s) for t in range(shards) for s in range(cores)]
    return lax.ppermute(x, ("tok", "sub"), pairs)


def on_device(features_in, gate_tiles, up_tiles, block_rows, block_counts, d_hidden):
    shards, owners = lax.axis_size("tok"), lax.axis_size("blk")
    cols, _, slots, tile, _ = gate_tiles.shape
    shard_rows, width = features_in.shape
    row_blocks = width // tile
    row_total = shards * shard_rows
    near_rows = 2 * shard_rows
    half = max(1, cols // 2)
    bases = range(2, shards, 2)
    lists = (jnp.transpose(block_rows, (2, 1, 0)), jnp.transpose(block_counts, (1, 0)))

    def shape(*dims, dtype=BF16):
        return jax.ShapeDtypeStruct(dims, dtype)

    def cost(tokens, columns, products, tile_bytes, weight=1):
        tiles = weight * columns * slots
        return pl.CostEstimate(
            flops=4 * tokens * tiles * tile * tile * products,
            bytes_accessed=4 * tiles * tile * tile * tile_bytes,
            transcendentals=0,
        )

    def to_owners(part):
        return [part] + [swap(part, "blk", s) for s in range(1, owners)]

    fars = [swap_far(features_in, base) for base in bases]
    features_next = swap(features_in, "tok", 1)
    cots = [d_hidden] + [swap(d_hidden, "blk", s) for s in range(1, owners)]

    def tile_shape(columns):
        return pltpu.VMEM((columns, 1, slots, tile, tile), BF16)

    def from_hbm(*arrays):
        return [pltpu.with_memory_space_constraint(array, pltpu.HBM) for array in arrays]

    near_a, *weights_a, rows_held, counts_held = pl.pallas_call(
        forward_own_kernel,
        out_shape=(
            shape(half, shard_rows, 2 * tile),
            tile_shape(half),
            tile_shape(half),
            pltpu.SMEM(lists[0].shape, jnp.int32),
            pltpu.SMEM(lists[1].shape, jnp.int32),
        ),
        in_specs=[ANY_SPEC] * 5,
        out_specs=(VMEM_SPEC,) * 3 + (SMEM_SPEC,) * 2,
        scratch_shapes=[
            pltpu.VMEM((shard_rows, width), BF16),
            pltpu.SemaphoreType.DMA((2, 3)),
            pltpu.SemaphoreType.DMA((3,)),
        ],
        compiler_params=limit(8),
        cost_estimate=cost(shard_rows, half, 1, 1),
        name="forward_own_a",
    )(*from_hbm(features_in, *lists, gate_tiles, up_tiles))
    near_a = to_owners(near_a)
    lists = (rows_held, counts_held)

    members = [0, 1, *range(2, shards, 2), *range(3, shards, 2)]
    far_members = members[2:]
    own_rows, far_rows = shard_rows, row_total - near_rows
    before_swap = [
        pl.pallas_call(
            copy_kernel,
            out_shape=shape(shard_rows, width),
            in_specs=[VMEM_SPEC, ANY_SPEC],
            out_specs=VMEM_SPEC,
            compiler_params=limit(8),
            cost_estimate=pl.CostEstimate(flops=0, bytes_accessed=0, transcendentals=0),
            name="after_own",
        )(far, near_a[0])
        for far in fars
    ]
    fetched = [features_next, *fars]
    swapped = [swap(far, "sub", 1) for far in before_swap]
    xs = [features_in, *fetched, *swapped]

    def forward_a(name, shard_xs, after):
        tokens = len(shard_xs) * shard_rows
        return to_owners(
            pl.pallas_call(
                functools.partial(forward_kernel, len(shard_xs)),
                out_shape=shape(half, tokens, 2 * tile),
                in_specs=[SMEM_SPEC] * 2 + [VMEM_SPEC] * (len(shard_xs) + 2) + [ANY_SPEC] * len(after),
                out_specs=VMEM_SPEC,
                compiler_params=limit(8),
                cost_estimate=cost(tokens, half, 1, 1),
                name=name,
            )(*lists, *shard_xs, *weights_a, *after)
        )

    rest_a = forward_a("forward_rest_a", [*fetched, *swapped], [cots[-1]])

    rest = cols - half
    groups = ((near_rows, row_total), (own_rows, near_rows), (0, own_rows))
    far_b, next_b, own_b, gate_b, up_b, turned = pl.pallas_call(
        functools.partial(load_forward_kernel, shards, groups, half, 1),
        out_shape=(
            *[shape(rest, stop - start, 2 * tile) for start, stop in groups],
            tile_shape(rest),
            tile_shape(rest),
            pltpu.VMEM((row_blocks, tile, row_total), BF16),
        ),
        in_specs=[SMEM_SPEC] * 2 + [VMEM_SPEC] * shards + [ANY_SPEC] * 4,
        out_specs=(VMEM_SPEC,) * 6,
        scratch_shapes=[pltpu.SemaphoreType.DMA((2, 3))],
        compiler_params=limit(8),
        cost_estimate=cost(row_total, rest, 1, 1, 5),
        name="forward_b",
    )(*lists, *xs, *from_hbm(gate_tiles, up_tiles), rest_a[0], near_a[-1])
    own_b, next_b, far_b = to_owners(own_b), to_owners(next_b), to_owners(far_b)

    turned_b = pl.pallas_call(
        turn_kernel,
        out_shape=shape(rest, 2 * tile, slots * tile),
        in_specs=[VMEM_SPEC] * 2 + [ANY_SPEC],
        out_specs=VMEM_SPEC,
        compiler_params=limit(8),
        cost_estimate=cost(2 * tile, rest, 1, 1, 0),
        name="turn_b",
    )(gate_b, up_b, far_b[0])

    out_tiles = shape(*gate_tiles.shape)
    tile_bytes = slots * tile * tile * 2
    gate_out, up_out, hidden_a, acc_own, acc_next, acc_far = pl.pallas_call(
        functools.partial(first_half_kernel, members, owners),
        out_shape=(
            out_tiles,
            out_tiles,
            shape(row_total, half * tile),
            *[shape(row_blocks, rows, tile, dtype=F32) for rows in (own_rows, own_rows, far_rows)],
        ),
        in_specs=[SMEM_SPEC] * 2 + [VMEM_SPEC] * (3 + 3 * owners) + [ANY_SPEC] * 3,
        out_specs=(ANY_SPEC,) * 2 + (VMEM_SPEC,) * 4,
        scratch_shapes=[
            pltpu.VMEM((half, row_total, 2 * tile), BF16),
            tile_shape(half),
            tile_shape(half),
            pltpu.SemaphoreType.DMA((2, half)),
        ],
        compiler_params=limit(8 + 2 * half * tile_bytes // MIB),
        cost_estimate=cost(row_total, half, 2, 1, 1),
        name="first_half",
    )(
        *lists, *weights_a, turned, *near_a, *rest_a, *cots, far_b[0], next_b[0], turned_b
    )

    def second_half(name, chunk, acc, parts, after, weight):
        rows_here = len(chunk) * shard_rows
        return pl.pallas_call(
            functools.partial(second_half_kernel, chunk, owners, half, slots),
            out_shape=(
                shape(rest, rows_here, 2 * tile),
                shape(rows_here, rest * tile),
                *[shape(shard_rows, width) for _ in chunk],
            ),
            in_specs=[SMEM_SPEC] * 2 + [VMEM_SPEC] * (2 + 2 * owners) + [ANY_SPEC],
            out_specs=(VMEM_SPEC,) * (2 + len(chunk)),
            scratch_shapes=[pltpu.VMEM((row_blocks, rows_here, tile), F32)],
            compiler_params=limit(8),
            cost_estimate=cost(rows_here, rest, 1, 1, weight),
            name=name,
        )(*lists, turned_b, acc, *parts, *cots, after)

    far_grads, far_hidden, *far_dxs = second_half("far_b", far_members, acc_far, far_b, acc_own, 1)
    both_cores = []
    for mine, others in zip(far_dxs[: len(bases)], far_dxs[len(bases) :]):
        both_cores.append(
            pl.pallas_call(
                add_kernel,
                out_shape=shape(shard_rows, width),
                in_specs=[VMEM_SPEC] * 2 + [ANY_SPEC],
                out_specs=VMEM_SPEC,
                compiler_params=limit(8),
                cost_estimate=pl.CostEstimate(flops=0, bytes_accessed=0, transcendentals=0),
                name="add_cores",
            )(mine, swap(others, "sub", 1), next_b[-1])
        )
    back_far = [swap_far(total, base) for total, base in zip(both_cores, bases)]
    next_grads, next_hidden, next_dx = second_half("next_b", [1], acc_next, next_b, both_cores[-1], 1)
    back_next = swap(next_dx, "tok", 1)
    gate_out, up_out, hidden_out, own_dx = pl.pallas_call(
        functools.partial(last_half_kernel, members, owners, half),
        out_shape=(out_tiles, out_tiles, shape(*d_hidden.shape), shape(shard_rows, width)),
        in_specs=[SMEM_SPEC] * 2 + [VMEM_SPEC] * (8 + 2 * owners) + [ANY_SPEC] * 3,
        out_specs=(ANY_SPEC,) * 3 + (VMEM_SPEC,),
        scratch_shapes=[
            pltpu.VMEM((row_blocks, shard_rows, tile), F32),
            pltpu.VMEM((rest, shard_rows, 2 * tile), BF16),
            pltpu.VMEM((shard_rows, rest * tile), BF16),
            tile_shape(rest),
            tile_shape(rest),
            pltpu.SemaphoreType.DMA((2, rest)),
            pltpu.SemaphoreType.DMA((2, d_hidden.shape[0] // shard_rows)),
        ],
        input_output_aliases={10 + 2 * owners: 0, 11 + 2 * owners: 1},
        compiler_params=limit(8 + 2 * rest * tile_bytes // MIB),
        cost_estimate=cost(row_total, rest, 1, 1, 10),
        name="last_half",
    )(
        *lists,
        turned_b,
        turned,
        acc_own,
        *own_b,
        *cots,
        next_grads,
        far_grads,
        hidden_a,
        next_hidden,
        far_hidden,
        gate_out,
        up_out,
        both_cores[-1],
    )
    arrived = [own_dx, back_next, *back_far]
    mine, mine_sent = pl.pallas_call(
        functools.partial(sum_kernel, len(arrived)),
        out_shape=(shape(shard_rows, width, dtype=F32), shape(shard_rows, width)),
        in_specs=[VMEM_SPEC] * len(arrived),
        out_specs=(VMEM_SPEC,) * 2,
        compiler_params=limit(8),
        name="sum_shards",
    )(*arrived)
    features_grad = (mine + swap(mine_sent, "sub", 1).astype(F32)).astype(BF16)
    return (hidden_out, gate_out, up_out, features_grad)


def solution(mesh):
    return jax.shard_map(
        on_device,
        mesh=mesh,
        in_specs=(
            P(("groups", "tok"), "blk"),
            P(("tok", "sub"), "blk", None, None, None),
            P(("tok", "sub"), "blk", None, None, None),
            P(("tok", "sub"), "blk", None),
            P(("tok", "sub"), "blk"),
            P(("groups", "blk"), ("tok", "sub")),
        ),
        out_specs=(
            P(("groups", "blk"), ("tok", "sub")),
            P(("groups", "tok", "sub"), "blk", None, None, None),
            P(("groups", "tok", "sub"), "blk", None, None, None),
            P(("groups", "tok"), "blk"),
        ),
        check_vma=False,
    )
```

```python
import functools

import jax
import jax.numpy as jnp
from jax import lax
from jax.experimental import pallas as pl
from jax.experimental.pallas import tpu as pltpu
from jax.sharding import PartitionSpec as P

F32 = jnp.float32
BF16 = jnp.bfloat16
MIB = 1 << 20
VMEM_SPEC = pl.BlockSpec(memory_space=pltpu.VMEM)
SMEM_SPEC = pl.BlockSpec(memory_space=pltpu.SMEM)
ANY_SPEC = pl.BlockSpec(memory_space=pl.ANY)


def limit(mib):
    return pltpu.CompilerParams(vmem_limit_bytes=mib * MIB)


def lanes(index, width):
    return pl.ds(pl.multiple_of(index * width, width), width)


def weights_of(c, gate_ref, up_ref):
    slots, rows, cols = gate_ref.shape[2:]
    return jnp.concatenate(
        [gate_ref[c, 0].reshape(slots * rows, cols), up_ref[c, 0].reshape(slots * rows, cols)], axis=1
    )


def keep(k, count, block):
    return jnp.where(k < count, block, jnp.zeros_like(block))


def forward_column(c, first, lists, xs, gate_ref, up_ref):
    rows_ref, counts_ref = lists
    slots, tile = gate_ref.shape[2:4]
    count = counts_ref[0, first + c]
    picked = []
    for k in range(slots):
        where = lanes(rows_ref[k, 0, first + c], tile)
        picked.append(keep(k, count, jnp.concatenate([x[:, where] for x in xs], axis=0)))
    return jnp.dot(
        jnp.concatenate(picked, axis=1), weights_of(c, gate_ref, up_ref), preferred_element_type=F32
    ).astype(BF16)


def groups_of(cols):
    edges = [0, -(-cols * 3 // 8), -(-cols * 6 // 8), cols]
    return [(start, stop) for start, stop in zip(edges, edges[1:]) if start < stop]


def load_tiles(first, cols, gate_hbm, up_hbm, gate_ref, up_ref, sems):
    def copies(i, start, stop):
        return [
            pltpu.make_async_copy(
                source.at[pl.ds(first + start, stop - start)], target.at[pl.ds(start, stop - start)], sems.at[j, i]
            )
            for j, (source, target) in enumerate(((gate_hbm, gate_ref), (up_hbm, up_ref)))
        ]

    started = {start: copies(i, start, stop) for i, (start, stop) in enumerate(groups_of(cols))}
    for group in started.values():
        for copy in group:
            copy.start()

    def arrive(c):
        for copy in started.get(c, ()):
            copy.wait()

    return arrive


def store_tiles(first, c, gate_ref, up_ref, gate_hbm, up_hbm, sems):
    copies = [
        pltpu.make_async_copy(gate_ref.at[c], gate_hbm.at[first + c], sems.at[0, c]),
        pltpu.make_async_copy(up_ref.at[c], up_hbm.at[first + c], sems.at[1, c]),
    ]
    for copy in copies:
        copy.start()
    return copies


def forward_own_kernel(x_hbm, rows_hbm, counts_hbm, gate_hbm, up_hbm, part_ref, gate_ref, up_ref, rows_ref, counts_ref, *scratch):
    x_ref, sems, small_sems = scratch
    cols = gate_ref.shape[0]
    small = [
        pltpu.make_async_copy(source, target, small_sems.at[i])
        for i, (source, target) in enumerate(((rows_hbm, rows_ref), (counts_hbm, counts_ref), (x_hbm, x_ref)))
    ]
    for copy in small:
        copy.start()
    arrive = load_tiles(0, cols, gate_hbm, up_hbm, gate_ref, up_ref, sems)
    for copy in small:
        copy.wait()
    for c in range(cols):
        arrive(c)
        part_ref[c] = forward_column(c, 0, (rows_ref, counts_ref), [x_ref], gate_ref, up_ref)


def forward_kernel(members, rows_ref, counts_ref, *refs):
    xs = refs[:members]
    gate_ref, up_ref = refs[members : members + 2]
    part_ref = refs[-1]
    for c in range(gate_ref.shape[0]):
        part_ref[c] = forward_column(c, 0, (rows_ref, counts_ref), xs, gate_ref, up_ref)


def unit(size):
    row, column = (lax.broadcasted_iota(jnp.int32, (size, size), axis) for axis in (0, 1))
    return (row == column).astype(F32).astype(BF16)


def load_forward_kernel(members, groups, first, turn, rows_ref, counts_ref, *refs):
    xs = refs[:members]
    gate_hbm, up_hbm = refs[members : members + 2]
    outs = refs[-(len(groups) + 3 + turn) :]
    parts, gate_ref, up_ref, sems = outs[: len(groups)], outs[-3 - turn], outs[-2 - turn], outs[-1]
    cols, _, _, tile, _ = gate_ref.shape
    arrive = load_tiles(first, cols, gate_hbm, up_hbm, gate_ref, up_ref, sems)
    if turn:
        turned_ref = outs[-2]
        identity = unit(tile)
        for r in range(turned_ref.shape[0]):
            block = jnp.concatenate([x[:, r * tile : (r + 1) * tile] for x in xs], axis=0)
            turned_ref[r] = lax.dot_general(
                identity, block, (((1,), (1,)), ((), ())), preferred_element_type=F32
            ).astype(BF16)
    for c in range(cols):
        arrive(c)
        part = forward_column(c, first, (rows_ref, counts_ref), xs, gate_ref, up_ref)
        for (start, stop), part_ref in zip(groups, parts):
            part_ref[c] = part[start:stop]


def shard_of(member):
    if member < 2:
        return lax.axis_index("tok") ^ member
    return lax.axis_index("tok") ^ ((member & ~1) + ((member & 1) ^ lax.axis_index("sub")))


def cotangent_of(members, cots, shard_rows, where):
    shards_each = cots[0].shape[0] // shard_rows
    blocks = []
    for member in members:
        shard = shard_of(member)
        source = (shard // shards_each) ^ lax.axis_index("blk")
        rows = pl.ds(pl.multiple_of((shard % shards_each) * shard_rows, shard_rows), shard_rows)
        block = cots[0][rows, where]
        for j, cot in enumerate(cots[1:], 1):
            block = jnp.where(source == j, cot[rows, where], block)
        blocks.append(block.astype(F32))
    return jnp.concatenate(blocks, axis=0)


def nonlinear(total, cotangent):
    tile = total.shape[1] // 2
    gate_value, up_value = total[:, :tile], total[:, tile:]
    sig_gate = jax.nn.sigmoid(gate_value)
    act_gate = gate_value * sig_gate
    hidden = (act_gate * up_value).astype(BF16)
    gate_grad = (cotangent * up_value * sig_gate * (1.0 + gate_value * (1.0 - sig_gate))).astype(BF16)
    up_grad = (cotangent * act_gate).astype(BF16)
    return hidden, jnp.concatenate([gate_grad, up_grad], axis=1)


def total_of(c, parts):
    total = parts[0][c].astype(F32)
    for part in parts[1:]:
        total = total + part[c].astype(F32)
    return total


def back_terms(c, grads, gate_ref, up_ref):
    return lax.dot_general(
        grads, weights_of(c, gate_ref, up_ref), (((1,), (1,)), ((), ())), preferred_element_type=F32
    )


def turn_kernel(gate_ref, up_ref, _, turned_ref):
    cols, _, slots, rows, tile = gate_ref.shape
    identity = unit(tile)
    for c in range(cols):
        for i, tiles in enumerate((gate_ref, up_ref)):
            turned_ref[c, i * tile : (i + 1) * tile] = lax.dot_general(
                identity,
                tiles[c, 0].reshape(slots * rows, tile),
                (((1,), (1,)), ((), ())),
                preferred_element_type=F32,
            ).astype(BF16)


def add_back(c, lists, back, accs, slots, tile):
    rows_ref, counts_ref = lists
    rows = [rows_ref[k, 0, c] for k in range(slots)]
    start = 0
    for acc in accs:
        stop = start + acc.shape[1]
        sums = [
            acc[rows[k]] + keep(k, counts_ref[0, c], back[start:stop, k * tile : (k + 1) * tile])
            for k in range(slots)
        ]
        for k in range(slots):
            acc[rows[k]] = sums[k]
        start = stop


def tile_grads(c, first, lists, turned_ref, grads, gate_ref, up_ref):
    rows_ref, counts_ref = lists
    slots, tile = gate_ref.shape[2:4]
    picked = jnp.concatenate([turned_ref[rows_ref[k, 0, first + c]] for k in range(slots)], axis=0)
    found = jnp.dot(picked, grads, preferred_element_type=F32)
    for k in range(slots):
        term = keep(k, counts_ref[0, first + c], found[k * tile : (k + 1) * tile]).astype(BF16)
        gate_ref[c, 0, k] = term[:, :tile]
        up_ref[c, 0, k] = term[:, tile:]


def start_hidden(members, parts, hidden_hbm, shard_rows, sems):
    shards_each = hidden_hbm.shape[0] // shard_rows

    def copies(i, member):
        rows = pl.ds(i * shard_rows, shard_rows)
        return [
            pltpu.make_async_copy(
                array.at[pl.ds(row, shard_rows)], hidden_hbm.at[rows, pl.ds(first, array.shape[1])], sems.at[j, i]
            )
            for j, (array, row, first) in enumerate(parts(member))
        ]

    for i in range(shards_each):
        wanted = lax.axis_index("blk") * shards_each + i
        for member in members:

            @pl.when(shard_of(member) == wanted)
            def _(i=i, member=member):
                for copy in copies(i, member):
                    copy.start()

    return [copy for i in range(shards_each) for copy in copies(i, 0)]


def first_half_kernel(members, owners, rows_ref, counts_ref, gate_w, up_w, turned_ref, *refs):
    groups = [refs[start : start + owners] for start in range(0, 2 * owners, owners)]
    cots = refs[2 * owners : 3 * owners]
    gate_hbm, up_hbm, hidden_ref = refs[-10:-7]
    accs = refs[-7:-4]
    grads_ref, gate_ref, up_ref, sems = refs[-4:]
    cols, _, slots, tile, _ = gate_ref.shape
    shard_rows = hidden_ref.shape[0] // len(members)
    lists = (rows_ref, counts_ref)
    for acc in accs:
        acc[...] = jnp.zeros_like(acc)
    copies = []
    for c in range(cols):
        total = jnp.concatenate([total_of(c, parts) for parts in groups], axis=0)
        where = slice(c * tile, (c + 1) * tile)
        hidden, grads = nonlinear(total, cotangent_of(members, cots, shard_rows, where))
        hidden_ref[:, where] = hidden
        grads_ref[c] = grads
        tile_grads(c, 0, lists, turned_ref, grads, gate_ref, up_ref)
        copies += store_tiles(0, c, gate_ref, up_ref, gate_hbm, up_hbm, sems)
    for c in range(cols):
        add_back(c, lists, back_terms(c, grads_ref[c], gate_w, up_w), accs, slots, tile)
    for copy in copies:
        copy.wait()


def second_half_kernel(members, owners, first, slots, rows_ref, counts_ref, turned_w, acc_in, *refs):
    parts, cots = refs[:owners], refs[owners : 2 * owners]
    outs = refs[-(2 + len(members) + 1) :]
    grads_ref, hidden_ref = outs[:2]
    dxs, acc_ref = outs[2:-1], outs[-1]
    cols, tile = turned_w.shape[0], turned_w.shape[1] // 2
    shard_rows = hidden_ref.shape[0] // len(members)
    acc_ref[...] = acc_in[...]
    for c in range(cols):
        where = slice((first + c) * tile, (first + c + 1) * tile)
        hidden, grads = nonlinear(total_of(c, parts), cotangent_of(members, cots, shard_rows, where))
        hidden_ref[:, c * tile : (c + 1) * tile] = hidden
        grads_ref[c] = grads
        back = jnp.dot(grads, turned_w[c], preferred_element_type=F32)
        add_back(first + c, (rows_ref, counts_ref), back, (acc_ref,), slots, tile)
    for r in range(acc_ref.shape[0]):
        block = acc_ref[r].astype(BF16)
        for m, dx in enumerate(dxs):
            dx[:, r * tile : (r + 1) * tile] = block[m * shard_rows : (m + 1) * shard_rows]
    width = acc_ref.shape[0] * tile
    for dx in dxs:
        if dx.shape[1] > width:
            dx[:, width:] = jnp.zeros_like(dx[:, width:])


def last_half_kernel(members, owners, first, rows_ref, counts_ref, turned_w, turned_ref, acc_in, *refs):
    parts, cots = refs[:owners], refs[owners : 2 * owners]
    next_grads, far_grads, hidden_a, next_hidden, far_hidden = refs[2 * owners : 2 * owners + 5]
    gate_hbm, up_hbm, hidden_hbm, dx_ref = refs[-11:-7]
    acc_ref, grads_ref, hidden_ref, gate_ref, up_ref, sems, hidden_sems = refs[-7:]
    cols, _, slots, tile, _ = gate_ref.shape
    shard_rows = hidden_ref.shape[0]
    lists = (rows_ref, counts_ref)

    def hidden_of(member):
        at = members.index(member)
        mine = ((hidden_ref, 0), (next_hidden, 0))[at] if at < 2 else (far_hidden, (at - 2) * shard_rows)
        return (hidden_a, at * shard_rows, 0), (*mine, first * tile)

    acc_ref[...] = acc_in[...]
    copies = []
    for c in range(cols):
        where = slice((first + c) * tile, (first + c + 1) * tile)
        hidden, grads = nonlinear(total_of(c, parts), cotangent_of(members[:1], cots, shard_rows, where))
        hidden_ref[:, c * tile : (c + 1) * tile] = hidden
        grads_ref[c] = grads
        grads = jnp.concatenate([grads, next_grads[c], far_grads[c]], axis=0)
        tile_grads(c, first, lists, turned_ref, grads, gate_ref, up_ref)
        copies += store_tiles(first, c, gate_ref, up_ref, gate_hbm, up_hbm, sems)
    copies += start_hidden(members, hidden_of, hidden_hbm, shard_rows, hidden_sems)
    for c in range(cols):
        back = jnp.dot(grads_ref[c], turned_w[c], preferred_element_type=F32)
        add_back(first + c, lists, back, (acc_ref,), slots, tile)
    for r in range(acc_ref.shape[0]):
        dx_ref[:, r * tile : (r + 1) * tile] = acc_ref[r].astype(BF16)
    for copy in copies:
        copy.wait()


def copy_kernel(x_ref, _, out_ref):
    out_ref[...] = x_ref[...]


def add_kernel(left_ref, right_ref, _, out_ref):
    right = right_ref[:, : left_ref.shape[1]]
    out_ref[...] = (left_ref[...].astype(F32) + right.astype(F32)).astype(BF16)


def sum_kernel(count, *refs):
    total = sum(ref[...].astype(F32) for ref in refs[:count])
    refs[-2][...] = total
    refs[-1][...] = total.astype(BF16)


def swap(x, axis, step):
    return lax.ppermute(x, axis, [(i, i ^ step) for i in range(lax.axis_size(axis))])


def swap_far(x, base):
    shards, cores = lax.axis_size("tok"), lax.axis_size("sub")
    pairs = [(t * cores + s, (t ^ (base + s)) * cores + s) for t in range(shards) for s in range(cores)]
    return lax.ppermute(x, ("tok", "sub"), pairs)


def on_device(features_in, gate_tiles, up_tiles, block_rows, block_counts, d_hidden):
    shards, owners = lax.axis_size("tok"), lax.axis_size("blk")
    cols, _, slots, tile, _ = gate_tiles.shape
    shard_rows, width = features_in.shape
    row_blocks = width // tile
    row_total = shards * shard_rows
    near_rows = 2 * shard_rows
    half = max(1, cols * 6 // 16)
    bases = range(2, shards, 2)
    lists = (jnp.transpose(block_rows, (2, 1, 0)), jnp.transpose(block_counts, (1, 0)))

    def shape(*dims, dtype=BF16):
        return jax.ShapeDtypeStruct(dims, dtype)

    def cost(tokens, columns, products, tile_bytes, weight=1):
        tiles = weight * columns * slots
        return pl.CostEstimate(
            flops=4 * tokens * tiles * tile * tile * products,
            bytes_accessed=4 * tiles * tile * tile * tile_bytes,
            transcendentals=0,
        )

    def to_owners(part):
        return [part] + [swap(part, "blk", s) for s in range(1, owners)]

    fars = [swap_far(features_in, base) for base in bases]
    features_next = swap(features_in, "tok", 1)
    cots = [d_hidden] + [swap(d_hidden, "blk", s) for s in range(1, owners)]

    def tile_shape(columns):
        return pltpu.VMEM((columns, 1, slots, tile, tile), BF16)

    def from_hbm(*arrays):
        return [pltpu.with_memory_space_constraint(array, pltpu.HBM) for array in arrays]

    near_a, *weights_a, rows_held, counts_held = pl.pallas_call(
        forward_own_kernel,
        out_shape=(
            shape(half, shard_rows, 2 * tile),
            tile_shape(half),
            tile_shape(half),
            pltpu.SMEM(lists[0].shape, jnp.int32),
            pltpu.SMEM(lists[1].shape, jnp.int32),
        ),
        in_specs=[ANY_SPEC] * 5,
        out_specs=(VMEM_SPEC,) * 3 + (SMEM_SPEC,) * 2,
        scratch_shapes=[
            pltpu.VMEM((shard_rows, width), BF16),
            pltpu.SemaphoreType.DMA((2, 3)),
            pltpu.SemaphoreType.DMA((3,)),
        ],
        compiler_params=limit(8),
        cost_estimate=cost(shard_rows, half, 1, 1),
        name="forward_own_a",
    )(*from_hbm(features_in, *lists, gate_tiles, up_tiles))
    near_a = to_owners(near_a)
    lists = (rows_held, counts_held)

    members = [0, 1, *range(2, shards, 2), *range(3, shards, 2)]
    far_members = members[2:]
    own_rows, far_rows = shard_rows, row_total - near_rows
    before_swap = [
        pl.pallas_call(
            copy_kernel,
            out_shape=shape(shard_rows, width),
            in_specs=[VMEM_SPEC, ANY_SPEC],
            out_specs=VMEM_SPEC,
            compiler_params=limit(8),
            cost_estimate=pl.CostEstimate(flops=0, bytes_accessed=0, transcendentals=0),
            name="after_own",
        )(far, near_a[0])
        for far in fars
    ]
    fetched = [features_next, *fars]
    swapped = [swap(far, "sub", 1) for far in before_swap]
    xs = [features_in, *fetched, *swapped]

    def forward_a(name, shard_xs, after):
        tokens = len(shard_xs) * shard_rows
        return to_owners(
            pl.pallas_call(
                functools.partial(forward_kernel, len(shard_xs)),
                out_shape=shape(half, tokens, 2 * tile),
                in_specs=[SMEM_SPEC] * 2 + [VMEM_SPEC] * (len(shard_xs) + 2) + [ANY_SPEC] * len(after),
                out_specs=VMEM_SPEC,
                compiler_params=limit(8),
                cost_estimate=cost(tokens, half, 1, 1),
                name=name,
            )(*lists, *shard_xs, *weights_a, *after)
        )

    rest_a = forward_a("forward_rest_a", [*fetched, *swapped], [cots[-1]])

    rest = cols - half
    groups = ((near_rows, row_total), (own_rows, near_rows), (0, own_rows))
    far_b, next_b, own_b, gate_b, up_b, turned = pl.pallas_call(
        functools.partial(load_forward_kernel, shards, groups, half, 1),
        out_shape=(
            *[shape(rest, stop - start, 2 * tile) for start, stop in groups],
            tile_shape(rest),
            tile_shape(rest),
            pltpu.VMEM((row_blocks, tile, row_total), BF16),
        ),
        in_specs=[SMEM_SPEC] * 2 + [VMEM_SPEC] * shards + [ANY_SPEC] * 4,
        out_specs=(VMEM_SPEC,) * 6,
        scratch_shapes=[pltpu.SemaphoreType.DMA((2, 3))],
        compiler_params=limit(8),
        cost_estimate=cost(row_total, rest, 1, 1, 5),
        name="forward_b",
    )(*lists, *xs, *from_hbm(gate_tiles, up_tiles), rest_a[0], near_a[-1])
    own_b, next_b, far_b = to_owners(own_b), to_owners(next_b), to_owners(far_b)

    turned_b = pl.pallas_call(
        turn_kernel,
        out_shape=shape(rest, 2 * tile, slots * tile),
        in_specs=[VMEM_SPEC] * 2 + [ANY_SPEC],
        out_specs=VMEM_SPEC,
        compiler_params=limit(8),
        cost_estimate=cost(2 * tile, rest, 1, 1, 0),
        name="turn_b",
    )(gate_b, up_b, far_b[0])

    out_tiles = shape(*gate_tiles.shape)
    tile_bytes = slots * tile * tile * 2
    gate_out, up_out, hidden_a, acc_own, acc_next, acc_far = pl.pallas_call(
        functools.partial(first_half_kernel, members, owners),
        out_shape=(
            out_tiles,
            out_tiles,
            shape(row_total, half * tile),
            *[shape(row_blocks, rows, tile, dtype=F32) for rows in (own_rows, own_rows, far_rows)],
        ),
        in_specs=[SMEM_SPEC] * 2 + [VMEM_SPEC] * (3 + 3 * owners) + [ANY_SPEC] * 3,
        out_specs=(ANY_SPEC,) * 2 + (VMEM_SPEC,) * 4,
        scratch_shapes=[
            pltpu.VMEM((half, row_total, 2 * tile), BF16),
            tile_shape(half),
            tile_shape(half),
            pltpu.SemaphoreType.DMA((2, half)),
        ],
        compiler_params=limit(8 + 2 * half * tile_bytes // MIB),
        cost_estimate=cost(row_total, half, 2, 1, 1),
        name="first_half",
    )(
        *lists, *weights_a, turned, *near_a, *rest_a, *cots, far_b[0], next_b[0], turned_b
    )

    def second_half(name, chunk, acc, parts, after, weight):
        rows_here = len(chunk) * shard_rows
        return pl.pallas_call(
            functools.partial(second_half_kernel, chunk, owners, half, slots),
            out_shape=(
                shape(rest, rows_here, 2 * tile),
                shape(rows_here, rest * tile),
                *[shape(shard_rows, max(width, 2 * rest * tile) if m >= 2 and m % 2 else width) for m in chunk],
            ),
            in_specs=[SMEM_SPEC] * 2 + [VMEM_SPEC] * (2 + 2 * owners) + [ANY_SPEC],
            out_specs=(VMEM_SPEC,) * (2 + len(chunk)),
            scratch_shapes=[pltpu.VMEM((row_blocks, rows_here, tile), F32)],
            compiler_params=limit(8),
            cost_estimate=cost(rows_here, rest, 1, 1, weight),
            name=name,
        )(*lists, turned_b, acc, *parts, *cots, after)

    far_grads, far_hidden, *far_dxs = second_half("far_b", far_members, acc_far, far_b, acc_own, 1)
    both_cores = []
    for mine, others in zip(far_dxs[: len(bases)], far_dxs[len(bases) :]):
        both_cores.append(
            pl.pallas_call(
                add_kernel,
                out_shape=shape(shard_rows, width),
                in_specs=[VMEM_SPEC] * 2 + [ANY_SPEC],
                out_specs=VMEM_SPEC,
                compiler_params=limit(8),
                cost_estimate=pl.CostEstimate(flops=0, bytes_accessed=0, transcendentals=0),
                name="add_cores",
            )(mine, swap(others, "sub", 1), next_b[-1])
        )
    back_far = [swap_far(total, base) for total, base in zip(both_cores, bases)]
    next_grads, next_hidden, next_dx = second_half("next_b", [1], acc_next, next_b, both_cores[-1], 1)
    back_next = swap(next_dx, "tok", 1)
    gate_out, up_out, hidden_out, own_dx = pl.pallas_call(
        functools.partial(last_half_kernel, members, owners, half),
        out_shape=(out_tiles, out_tiles, shape(*d_hidden.shape), shape(shard_rows, width)),
        in_specs=[SMEM_SPEC] * 2 + [VMEM_SPEC] * (8 + 2 * owners) + [ANY_SPEC] * 3,
        out_specs=(ANY_SPEC,) * 3 + (VMEM_SPEC,),
        scratch_shapes=[
            pltpu.VMEM((row_blocks, shard_rows, tile), F32),
            pltpu.VMEM((rest, shard_rows, 2 * tile), BF16),
            pltpu.VMEM((shard_rows, rest * tile), BF16),
            tile_shape(rest),
            tile_shape(rest),
            pltpu.SemaphoreType.DMA((2, rest)),
            pltpu.SemaphoreType.DMA((2, d_hidden.shape[0] // shard_rows)),
        ],
        input_output_aliases={10 + 2 * owners: 0, 11 + 2 * owners: 1},
        compiler_params=limit(8 + 2 * rest * tile_bytes // MIB),
        cost_estimate=cost(row_total, rest, 1, 1, 10),
        name="last_half",
    )(
        *lists,
        turned_b,
        turned,
        acc_own,
        *own_b,
        *cots,
        next_grads,
        far_grads,
        hidden_a,
        next_hidden,
        far_hidden,
        gate_out,
        up_out,
        both_cores[-1],
    )
    arrived = [own_dx, back_next, *back_far]
    mine, mine_sent = pl.pallas_call(
        functools.partial(sum_kernel, len(arrived)),
        out_shape=(shape(shard_rows, width, dtype=F32), shape(shard_rows, width)),
        in_specs=[VMEM_SPEC] * len(arrived),
        out_specs=(VMEM_SPEC,) * 2,
        compiler_params=limit(8),
        name="sum_shards",
    )(*arrived)
    features_grad = (mine + swap(mine_sent, "sub", 1).astype(F32)).astype(BF16)
    return (hidden_out, gate_out, up_out, features_grad)


def solution(mesh):
    return jax.shard_map(
        on_device,
        mesh=mesh,
        in_specs=(
            P(("groups", "tok"), "blk"),
            P(("tok", "sub"), "blk", None, None, None),
            P(("tok", "sub"), "blk", None, None, None),
            P(("tok", "sub"), "blk", None),
            P(("tok", "sub"), "blk"),
            P(("groups", "blk"), ("tok", "sub")),
        ),
        out_specs=(
            P(("groups", "blk"), ("tok", "sub")),
            P(("groups", "tok", "sub"), "blk", None, None, None),
            P(("groups", "tok", "sub"), "blk", None, None, None),
            P(("groups", "tok"), "blk"),
        ),
        check_vma=False,
    )
```

```python
import functools

import jax
import jax.numpy as jnp
from jax import lax
from jax.experimental import pallas as pl
from jax.experimental.pallas import tpu as pltpu
from jax.sharding import PartitionSpec as P

F32 = jnp.float32
BF16 = jnp.bfloat16
MIB = 1 << 20
VMEM_SPEC = pl.BlockSpec(memory_space=pltpu.VMEM)
SMEM_SPEC = pl.BlockSpec(memory_space=pltpu.SMEM)
ANY_SPEC = pl.BlockSpec(memory_space=pl.ANY)


def limit(mib):
    return pltpu.CompilerParams(vmem_limit_bytes=mib * MIB)


def lanes(index, width):
    return pl.ds(pl.multiple_of(index * width, width), width)


def weights_of(c, gate_ref, up_ref):
    slots, rows, cols = gate_ref.shape[2:]
    return jnp.concatenate(
        [gate_ref[c, 0].reshape(slots * rows, cols), up_ref[c, 0].reshape(slots * rows, cols)], axis=1
    )


def keep(k, count, block):
    return jnp.where(k < count, block, jnp.zeros_like(block))


def forward_column(c, first, lists, xs, gate_ref, up_ref):
    rows_ref, counts_ref = lists
    slots, tile = gate_ref.shape[2:4]
    count = counts_ref[0, first + c]
    picked = []
    for k in range(slots):
        where = lanes(rows_ref[k, 0, first + c], tile)
        picked.append(keep(k, count, jnp.concatenate([x[:, where] for x in xs], axis=0)))
    return jnp.dot(
        jnp.concatenate(picked, axis=1), weights_of(c, gate_ref, up_ref), preferred_element_type=F32
    ).astype(BF16)


def groups_of(cols):
    edges = [0, -(-cols * 3 // 8), -(-cols * 6 // 8), cols]
    return [(start, stop) for start, stop in zip(edges, edges[1:]) if start < stop]


def load_tiles(first, cols, gate_hbm, up_hbm, gate_ref, up_ref, sems):
    def copies(i, start, stop):
        return [
            pltpu.make_async_copy(
                source.at[pl.ds(first + start, stop - start)], target.at[pl.ds(start, stop - start)], sems.at[j, i]
            )
            for j, (source, target) in enumerate(((gate_hbm, gate_ref), (up_hbm, up_ref)))
        ]

    started = {start: copies(i, start, stop) for i, (start, stop) in enumerate(groups_of(cols))}
    for group in started.values():
        for copy in group:
            copy.start()

    def arrive(c):
        for copy in started.get(c, ()):
            copy.wait()

    return arrive


def store_tiles(first, c, gate_ref, up_ref, gate_hbm, up_hbm, sems):
    copies = [
        pltpu.make_async_copy(gate_ref.at[c], gate_hbm.at[first + c], sems.at[0, c]),
        pltpu.make_async_copy(up_ref.at[c], up_hbm.at[first + c], sems.at[1, c]),
    ]
    for copy in copies:
        copy.start()
    return copies


def forward_own_kernel(x_hbm, rows_hbm, counts_hbm, gate_hbm, up_hbm, part_ref, gate_ref, up_ref, rows_ref, counts_ref, *scratch):
    x_ref, sems, small_sems = scratch
    cols = gate_ref.shape[0]
    small = [
        pltpu.make_async_copy(source, target, small_sems.at[i])
        for i, (source, target) in enumerate(((rows_hbm, rows_ref), (counts_hbm, counts_ref), (x_hbm, x_ref)))
    ]
    for copy in small:
        copy.start()
    arrive = load_tiles(0, cols, gate_hbm, up_hbm, gate_ref, up_ref, sems)
    for copy in small:
        copy.wait()
    for c in range(cols):
        arrive(c)
        part_ref[c] = forward_column(c, 0, (rows_ref, counts_ref), [x_ref], gate_ref, up_ref)


def forward_kernel(members, rows_ref, counts_ref, *refs):
    xs = refs[:members]
    gate_ref, up_ref = refs[members : members + 2]
    part_ref = refs[-1]
    for c in range(gate_ref.shape[0]):
        part_ref[c] = forward_column(c, 0, (rows_ref, counts_ref), xs, gate_ref, up_ref)


def unit(size):
    row, column = (lax.broadcasted_iota(jnp.int32, (size, size), axis) for axis in (0, 1))
    return (row == column).astype(F32).astype(BF16)


def load_forward_kernel(members, groups, first, turn, rows_ref, counts_ref, *refs):
    xs = refs[:members]
    gate_hbm, up_hbm = refs[members : members + 2]
    outs = refs[-(len(groups) + 3 + turn) :]
    parts, gate_ref, up_ref, sems = outs[: len(groups)], outs[-3 - turn], outs[-2 - turn], outs[-1]
    cols, _, _, tile, _ = gate_ref.shape
    arrive = load_tiles(first, cols, gate_hbm, up_hbm, gate_ref, up_ref, sems)
    if turn:
        turned_ref = outs[-2]
        identity = unit(tile)
        for r in range(turned_ref.shape[0]):
            block = jnp.concatenate([x[:, r * tile : (r + 1) * tile] for x in xs], axis=0)
            turned_ref[r] = lax.dot_general(
                identity, block, (((1,), (1,)), ((), ())), preferred_element_type=F32
            ).astype(BF16)
    for c in range(cols):
        arrive(c)
        part = forward_column(c, first, (rows_ref, counts_ref), xs, gate_ref, up_ref)
        for (start, stop), part_ref in zip(groups, parts):
            part_ref[c] = part[start:stop]


def shard_of(member):
    if member < 2:
        return lax.axis_index("tok") ^ member
    return lax.axis_index("tok") ^ ((member & ~1) + ((member & 1) ^ lax.axis_index("sub")))


def cotangent_of(members, cots, shard_rows, where):
    shards_each = cots[0].shape[0] // shard_rows
    blocks = []
    for member in members:
        shard = shard_of(member)
        source = (shard // shards_each) ^ lax.axis_index("blk")
        rows = pl.ds(pl.multiple_of((shard % shards_each) * shard_rows, shard_rows), shard_rows)
        block = cots[0][rows, where]
        for j, cot in enumerate(cots[1:], 1):
            block = jnp.where(source == j, cot[rows, where], block)
        blocks.append(block.astype(F32))
    return jnp.concatenate(blocks, axis=0)


def nonlinear(total, cotangent):
    tile = total.shape[1] // 2
    gate_value, up_value = total[:, :tile], total[:, tile:]
    sig_gate = jax.nn.sigmoid(gate_value)
    act_gate = gate_value * sig_gate
    hidden = (act_gate * up_value).astype(BF16)
    gate_grad = (cotangent * up_value * sig_gate * (1.0 + gate_value * (1.0 - sig_gate))).astype(BF16)
    up_grad = (cotangent * act_gate).astype(BF16)
    return hidden, jnp.concatenate([gate_grad, up_grad], axis=1)


def total_of(c, parts):
    total = parts[0][c].astype(F32)
    for part in parts[1:]:
        total = total + part[c].astype(F32)
    return total


def back_terms(c, grads, gate_ref, up_ref):
    return lax.dot_general(
        grads, weights_of(c, gate_ref, up_ref), (((1,), (1,)), ((), ())), preferred_element_type=F32
    )


def turn_kernel(gate_ref, up_ref, _, turned_ref):
    cols, _, slots, rows, tile = gate_ref.shape
    identity = unit(tile)
    for c in range(cols):
        for i, tiles in enumerate((gate_ref, up_ref)):
            turned_ref[c, i * tile : (i + 1) * tile] = lax.dot_general(
                identity,
                tiles[c, 0].reshape(slots * rows, tile),
                (((1,), (1,)), ((), ())),
                preferred_element_type=F32,
            ).astype(BF16)


def add_back(c, lists, back, accs, slots, tile):
    rows_ref, counts_ref = lists
    rows = [rows_ref[k, 0, c] for k in range(slots)]
    start = 0
    for acc in accs:
        stop = start + acc.shape[1]
        sums = [
            acc[rows[k]] + keep(k, counts_ref[0, c], back[start:stop, k * tile : (k + 1) * tile])
            for k in range(slots)
        ]
        for k in range(slots):
            acc[rows[k]] = sums[k]
        start = stop


def tile_grads(c, first, lists, turned_ref, grads, gate_ref, up_ref):
    rows_ref, counts_ref = lists
    slots, tile = gate_ref.shape[2:4]
    picked = jnp.concatenate([turned_ref[rows_ref[k, 0, first + c]] for k in range(slots)], axis=0)
    found = jnp.dot(picked, grads, preferred_element_type=F32)
    for k in range(slots):
        term = keep(k, counts_ref[0, first + c], found[k * tile : (k + 1) * tile]).astype(BF16)
        gate_ref[c, 0, k] = term[:, :tile]
        up_ref[c, 0, k] = term[:, tile:]


def start_hidden(members, parts, hidden_hbm, shard_rows, sems):
    shards_each = hidden_hbm.shape[0] // shard_rows

    def copies(i, member):
        rows = pl.ds(i * shard_rows, shard_rows)
        return [
            pltpu.make_async_copy(
                array.at[pl.ds(row, shard_rows)], hidden_hbm.at[rows, pl.ds(first, array.shape[1])], sems.at[j, i]
            )
            for j, (array, row, first) in enumerate(parts(member))
        ]

    for i in range(shards_each):
        wanted = lax.axis_index("blk") * shards_each + i
        for member in members:

            @pl.when(shard_of(member) == wanted)
            def _(i=i, member=member):
                for copy in copies(i, member):
                    copy.start()

    return [copy for i in range(shards_each) for copy in copies(i, 0)]


def first_half_kernel(members, owners, rows_ref, counts_ref, gate_w, up_w, turned_ref, *refs):
    groups = [refs[start : start + owners] for start in range(0, 2 * owners, owners)]
    cots = refs[2 * owners : 3 * owners]
    gate_hbm, up_hbm, hidden_ref = refs[-10:-7]
    accs = refs[-7:-4]
    grads_ref, gate_ref, up_ref, sems = refs[-4:]
    cols, _, slots, tile, _ = gate_ref.shape
    shard_rows = hidden_ref.shape[0] // len(members)
    lists = (rows_ref, counts_ref)
    for acc in accs:
        acc[...] = jnp.zeros_like(acc)
    copies = []
    for c in range(cols):
        total = jnp.concatenate([total_of(c, parts) for parts in groups], axis=0)
        where = slice(c * tile, (c + 1) * tile)
        hidden, grads = nonlinear(total, cotangent_of(members, cots, shard_rows, where))
        hidden_ref[:, where] = hidden
        grads_ref[c] = grads
        tile_grads(c, 0, lists, turned_ref, grads, gate_ref, up_ref)
        copies += store_tiles(0, c, gate_ref, up_ref, gate_hbm, up_hbm, sems)
    for c in range(cols):
        add_back(c, lists, back_terms(c, grads_ref[c], gate_w, up_w), accs, slots, tile)
    for copy in copies:
        copy.wait()


def second_half_kernel(members, owners, first, slots, rows_ref, counts_ref, turned_w, acc_in, *refs):
    parts, cots = refs[:owners], refs[owners : 2 * owners]
    outs = refs[-(2 + len(members) + 1) :]
    grads_ref, hidden_ref = outs[:2]
    dxs, acc_ref = outs[2:-1], outs[-1]
    cols, tile = turned_w.shape[0], turned_w.shape[1] // 2
    shard_rows = hidden_ref.shape[0] // len(members)
    acc_ref[...] = acc_in[...]
    for c in range(cols):
        where = slice((first + c) * tile, (first + c + 1) * tile)
        hidden, grads = nonlinear(total_of(c, parts), cotangent_of(members, cots, shard_rows, where))
        hidden_ref[:, c * tile : (c + 1) * tile] = hidden
        grads_ref[c] = grads
        back = jnp.dot(grads, turned_w[c], preferred_element_type=F32)
        add_back(first + c, (rows_ref, counts_ref), back, (acc_ref,), slots, tile)
    for r in range(acc_ref.shape[0]):
        block = acc_ref[r].astype(BF16)
        for m, dx in enumerate(dxs):
            dx[:, r * tile : (r + 1) * tile] = block[m * shard_rows : (m + 1) * shard_rows]
    width = acc_ref.shape[0] * tile
    for dx in dxs:
        if dx.shape[1] > width:
            dx[:, width:] = jnp.zeros_like(dx[:, width:])


def last_half_kernel(members, owners, first, rows_ref, counts_ref, turned_w, turned_ref, acc_in, *refs):
    parts, cots = refs[:owners], refs[owners : 2 * owners]
    next_grads, far_grads, hidden_a, next_hidden, far_hidden = refs[2 * owners : 2 * owners + 5]
    gate_hbm, up_hbm, hidden_hbm, dx_ref = refs[-11:-7]
    acc_ref, grads_ref, hidden_ref, gate_ref, up_ref, sems, hidden_sems = refs[-7:]
    cols, _, slots, tile, _ = gate_ref.shape
    shard_rows = hidden_ref.shape[0]
    lists = (rows_ref, counts_ref)

    def hidden_of(member):
        at = members.index(member)
        mine = ((hidden_ref, 0), (next_hidden, 0))[at] if at < 2 else (far_hidden, (at - 2) * shard_rows)
        return (hidden_a, at * shard_rows, 0), (*mine, first * tile)

    acc_ref[...] = acc_in[...]
    copies = []
    for c in range(cols):
        where = slice((first + c) * tile, (first + c + 1) * tile)
        hidden, grads = nonlinear(total_of(c, parts), cotangent_of(members[:1], cots, shard_rows, where))
        hidden_ref[:, c * tile : (c + 1) * tile] = hidden
        grads_ref[c] = grads
        grads = jnp.concatenate([grads, next_grads[c], far_grads[c]], axis=0)
        tile_grads(c, first, lists, turned_ref, grads, gate_ref, up_ref)
        copies += store_tiles(first, c, gate_ref, up_ref, gate_hbm, up_hbm, sems)
    copies += start_hidden(members, hidden_of, hidden_hbm, shard_rows, hidden_sems)
    for c in range(cols):
        back = jnp.dot(grads_ref[c], turned_w[c], preferred_element_type=F32)
        add_back(first + c, lists, back, (acc_ref,), slots, tile)
    for r in range(acc_ref.shape[0]):
        dx_ref[:, r * tile : (r + 1) * tile] = acc_ref[r].astype(BF16)
    for copy in copies:
        copy.wait()


def copy_kernel(x_ref, _, out_ref):
    out_ref[...] = x_ref[...]


def add_kernel(left_ref, right_ref, _, out_ref):
    right = right_ref[:, : left_ref.shape[1]]
    out_ref[...] = (left_ref[...].astype(F32) + right.astype(F32)).astype(BF16)


def sum_kernel(count, *refs):
    total = sum(ref[...].astype(F32) for ref in refs[:count])
    refs[-2][...] = total
    refs[-1][...] = total.astype(BF16)


def swap(x, axis, step):
    return lax.ppermute(x, axis, [(i, i ^ step) for i in range(lax.axis_size(axis))])


def swap_far(x, base):
    shards, cores = lax.axis_size("tok"), lax.axis_size("sub")
    pairs = [(t * cores + s, (t ^ (base + s)) * cores + s) for t in range(shards) for s in range(cores)]
    return lax.ppermute(x, ("tok", "sub"), pairs)


def on_device(features_in, gate_tiles, up_tiles, block_rows, block_counts, d_hidden):
    shards, owners = lax.axis_size("tok"), lax.axis_size("blk")
    cols, _, slots, tile, _ = gate_tiles.shape
    shard_rows, width = features_in.shape
    row_blocks = width // tile
    row_total = shards * shard_rows
    near_rows = 2 * shard_rows
    half = max(1, cols * 7 // 16)
    bases = range(2, shards, 2)
    lists = (jnp.transpose(block_rows, (2, 1, 0)), jnp.transpose(block_counts, (1, 0)))

    def shape(*dims, dtype=BF16):
        return jax.ShapeDtypeStruct(dims, dtype)

    def cost(tokens, columns, products, tile_bytes, weight=1):
        tiles = weight * columns * slots
        return pl.CostEstimate(
            flops=4 * tokens * tiles * tile * tile * products,
            bytes_accessed=4 * tiles * tile * tile * tile_bytes,
            transcendentals=0,
        )

    def to_owners(part):
        return [part] + [swap(part, "blk", s) for s in range(1, owners)]

    fars = [swap_far(features_in, base) for base in bases]
    features_next = swap(features_in, "tok", 1)
    cots = [d_hidden] + [swap(d_hidden, "blk", s) for s in range(1, owners)]

    def tile_shape(columns):
        return pltpu.VMEM((columns, 1, slots, tile, tile), BF16)

    def from_hbm(*arrays):
        return [pltpu.with_memory_space_constraint(array, pltpu.HBM) for array in arrays]

    near_a, *weights_a, rows_held, counts_held = pl.pallas_call(
        forward_own_kernel,
        out_shape=(
            shape(half, shard_rows, 2 * tile),
            tile_shape(half),
            tile_shape(half),
            pltpu.SMEM(lists[0].shape, jnp.int32),
            pltpu.SMEM(lists[1].shape, jnp.int32),
        ),
        in_specs=[ANY_SPEC] * 5,
        out_specs=(VMEM_SPEC,) * 3 + (SMEM_SPEC,) * 2,
        scratch_shapes=[
            pltpu.VMEM((shard_rows, width), BF16),
            pltpu.SemaphoreType.DMA((2, 3)),
            pltpu.SemaphoreType.DMA((3,)),
        ],
        compiler_params=limit(8),
        cost_estimate=cost(shard_rows, half, 1, 1),
        name="forward_own_a",
    )(*from_hbm(features_in, *lists, gate_tiles, up_tiles))
    near_a = to_owners(near_a)
    lists = (rows_held, counts_held)

    members = [0, 1, *range(2, shards, 2), *range(3, shards, 2)]
    far_members = members[2:]
    own_rows, far_rows = shard_rows, row_total - near_rows
    before_swap = [
        pl.pallas_call(
            copy_kernel,
            out_shape=shape(shard_rows, width),
            in_specs=[VMEM_SPEC, ANY_SPEC],
            out_specs=VMEM_SPEC,
            compiler_params=limit(8),
            cost_estimate=pl.CostEstimate(flops=0, bytes_accessed=0, transcendentals=0),
            name="after_own",
        )(far, near_a[0])
        for far in fars
    ]
    fetched = [features_next, *fars]
    swapped = [swap(far, "sub", 1) for far in before_swap]
    xs = [features_in, *fetched, *swapped]

    def forward_a(name, shard_xs, after):
        tokens = len(shard_xs) * shard_rows
        return to_owners(
            pl.pallas_call(
                functools.partial(forward_kernel, len(shard_xs)),
                out_shape=shape(half, tokens, 2 * tile),
                in_specs=[SMEM_SPEC] * 2 + [VMEM_SPEC] * (len(shard_xs) + 2) + [ANY_SPEC] * len(after),
                out_specs=VMEM_SPEC,
                compiler_params=limit(8),
                cost_estimate=cost(tokens, half, 1, 1),
                name=name,
            )(*lists, *shard_xs, *weights_a, *after)
        )

    rest_a = forward_a("forward_rest_a", [*fetched, *swapped], [cots[-1]])

    rest = cols - half
    groups = ((near_rows, row_total), (own_rows, near_rows), (0, own_rows))
    far_b, next_b, own_b, gate_b, up_b, turned = pl.pallas_call(
        functools.partial(load_forward_kernel, shards, groups, half, 1),
        out_shape=(
            *[shape(rest, stop - start, 2 * tile) for start, stop in groups],
            tile_shape(rest),
            tile_shape(rest),
            pltpu.VMEM((row_blocks, tile, row_total), BF16),
        ),
        in_specs=[SMEM_SPEC] * 2 + [VMEM_SPEC] * shards + [ANY_SPEC] * 4,
        out_specs=(VMEM_SPEC,) * 6,
        scratch_shapes=[pltpu.SemaphoreType.DMA((2, 3))],
        compiler_params=limit(8),
        cost_estimate=cost(row_total, rest, 1, 1, 5),
        name="forward_b",
    )(*lists, *xs, *from_hbm(gate_tiles, up_tiles), rest_a[0], near_a[-1])
    own_b, next_b, far_b = to_owners(own_b), to_owners(next_b), to_owners(far_b)

    turned_b = pl.pallas_call(
        turn_kernel,
        out_shape=shape(rest, 2 * tile, slots * tile),
        in_specs=[VMEM_SPEC] * 2 + [ANY_SPEC],
        out_specs=VMEM_SPEC,
        compiler_params=limit(8),
        cost_estimate=cost(2 * tile, rest, 1, 1, 0),
        name="turn_b",
    )(gate_b, up_b, far_b[0])

    out_tiles = shape(*gate_tiles.shape)
    tile_bytes = slots * tile * tile * 2
    gate_out, up_out, hidden_a, acc_own, acc_next, acc_far = pl.pallas_call(
        functools.partial(first_half_kernel, members, owners),
        out_shape=(
            out_tiles,
            out_tiles,
            shape(row_total, half * tile),
            *[shape(row_blocks, rows, tile, dtype=F32) for rows in (own_rows, own_rows, far_rows)],
        ),
        in_specs=[SMEM_SPEC] * 2 + [VMEM_SPEC] * (3 + 3 * owners) + [ANY_SPEC] * 3,
        out_specs=(ANY_SPEC,) * 2 + (VMEM_SPEC,) * 4,
        scratch_shapes=[
            pltpu.VMEM((half, row_total, 2 * tile), BF16),
            tile_shape(half),
            tile_shape(half),
            pltpu.SemaphoreType.DMA((2, half)),
        ],
        compiler_params=limit(8 + 2 * half * tile_bytes // MIB),
        cost_estimate=cost(row_total, half, 2, 1, 1),
        name="first_half",
    )(
        *lists, *weights_a, turned, *near_a, *rest_a, *cots, far_b[0], next_b[0], turned_b
    )

    def second_half(name, chunk, acc, parts, after, weight):
        rows_here = len(chunk) * shard_rows
        return pl.pallas_call(
            functools.partial(second_half_kernel, chunk, owners, half, slots),
            out_shape=(
                shape(rest, rows_here, 2 * tile),
                shape(rows_here, rest * tile),
                *[shape(shard_rows, max(width, 2 * rest * tile) if m >= 2 and m % 2 else width) for m in chunk],
            ),
            in_specs=[SMEM_SPEC] * 2 + [VMEM_SPEC] * (2 + 2 * owners) + [ANY_SPEC],
            out_specs=(VMEM_SPEC,) * (2 + len(chunk)),
            scratch_shapes=[pltpu.VMEM((row_blocks, rows_here, tile), F32)],
            compiler_params=limit(8),
            cost_estimate=cost(rows_here, rest, 1, 1, weight),
            name=name,
        )(*lists, turned_b, acc, *parts, *cots, after)

    far_grads, far_hidden, *far_dxs = second_half("far_b", far_members, acc_far, far_b, acc_own, 1)
    both_cores = []
    for mine, others in zip(far_dxs[: len(bases)], far_dxs[len(bases) :]):
        both_cores.append(
            pl.pallas_call(
                add_kernel,
                out_shape=shape(shard_rows, width),
                in_specs=[VMEM_SPEC] * 2 + [ANY_SPEC],
                out_specs=VMEM_SPEC,
                compiler_params=limit(8),
                cost_estimate=pl.CostEstimate(flops=0, bytes_accessed=0, transcendentals=0),
                name="add_cores",
            )(mine, swap(others, "sub", 1), next_b[-1])
        )
    back_far = [swap_far(total, base) for total, base in zip(both_cores, bases)]
    next_grads, next_hidden, next_dx = second_half("next_b", [1], acc_next, next_b, both_cores[-1], 1)
    back_next = swap(next_dx, "tok", 1)
    gate_out, up_out, hidden_out, own_dx = pl.pallas_call(
        functools.partial(last_half_kernel, members, owners, half),
        out_shape=(out_tiles, out_tiles, shape(*d_hidden.shape), shape(shard_rows, width)),
        in_specs=[SMEM_SPEC] * 2 + [VMEM_SPEC] * (8 + 2 * owners) + [ANY_SPEC] * 3,
        out_specs=(ANY_SPEC,) * 3 + (VMEM_SPEC,),
        scratch_shapes=[
            pltpu.VMEM((row_blocks, shard_rows, tile), F32),
            pltpu.VMEM((rest, shard_rows, 2 * tile), BF16),
            pltpu.VMEM((shard_rows, rest * tile), BF16),
            tile_shape(rest),
            tile_shape(rest),
            pltpu.SemaphoreType.DMA((2, rest)),
            pltpu.SemaphoreType.DMA((2, d_hidden.shape[0] // shard_rows)),
        ],
        input_output_aliases={10 + 2 * owners: 0, 11 + 2 * owners: 1},
        compiler_params=limit(8 + 2 * rest * tile_bytes // MIB),
        cost_estimate=cost(row_total, rest, 1, 1, 10),
        name="last_half",
    )(
        *lists,
        turned_b,
        turned,
        acc_own,
        *own_b,
        *cots,
        next_grads,
        far_grads,
        hidden_a,
        next_hidden,
        far_hidden,
        gate_out,
        up_out,
        both_cores[-1],
    )
    arrived = [own_dx, back_next, *back_far]
    mine, mine_sent = pl.pallas_call(
        functools.partial(sum_kernel, len(arrived)),
        out_shape=(shape(shard_rows, width, dtype=F32), shape(shard_rows, width)),
        in_specs=[VMEM_SPEC] * len(arrived),
        out_specs=(VMEM_SPEC,) * 2,
        compiler_params=limit(8),
        name="sum_shards",
    )(*arrived)
    features_grad = (mine + swap(mine_sent, "sub", 1).astype(F32)).astype(BF16)
    return (hidden_out, gate_out, up_out, features_grad)


def solution(mesh):
    return jax.shard_map(
        on_device,
        mesh=mesh,
        in_specs=(
            P(("groups", "tok"), "blk"),
            P(("tok", "sub"), "blk", None, None, None),
            P(("tok", "sub"), "blk", None, None, None),
            P(("tok", "sub"), "blk", None),
            P(("tok", "sub"), "blk"),
            P(("groups", "blk"), ("tok", "sub")),
        ),
        out_specs=(
            P(("groups", "blk"), ("tok", "sub")),
            P(("groups", "tok", "sub"), "blk", None, None, None),
            P(("groups", "tok", "sub"), "blk", None, None, None),
            P(("groups", "tok"), "blk"),
        ),
        check_vma=False,
    )
```

```python
import functools

import jax
import jax.numpy as jnp
from jax import lax
from jax.experimental import pallas as pl
from jax.experimental.pallas import tpu as pltpu
from jax.sharding import PartitionSpec as P

F32 = jnp.float32
BF16 = jnp.bfloat16
MIB = 1 << 20
VMEM_SPEC = pl.BlockSpec(memory_space=pltpu.VMEM)
SMEM_SPEC = pl.BlockSpec(memory_space=pltpu.SMEM)
ANY_SPEC = pl.BlockSpec(memory_space=pl.ANY)


def limit(mib):
    return pltpu.CompilerParams(vmem_limit_bytes=mib * MIB)


def lanes(index, width):
    return pl.ds(pl.multiple_of(index * width, width), width)


def weights_of(c, gate_ref, up_ref):
    slots, rows, cols = gate_ref.shape[2:]
    return jnp.concatenate(
        [gate_ref[c, 0].reshape(slots * rows, cols), up_ref[c, 0].reshape(slots * rows, cols)], axis=1
    )


def keep(k, count, block):
    return jnp.where(k < count, block, jnp.zeros_like(block))


def forward_column(c, first, lists, xs, gate_ref, up_ref):
    rows_ref, counts_ref = lists
    slots, tile = gate_ref.shape[2:4]
    count = counts_ref[0, first + c]
    picked = []
    for k in range(slots):
        where = lanes(rows_ref[k, 0, first + c], tile)
        picked.append(keep(k, count, jnp.concatenate([x[:, where] for x in xs], axis=0)))
    return jnp.dot(
        jnp.concatenate(picked, axis=1), weights_of(c, gate_ref, up_ref), preferred_element_type=F32
    ).astype(BF16)


def groups_of(cols):
    edges = [0, -(-cols * 3 // 8), -(-cols * 6 // 8), cols]
    return [(start, stop) for start, stop in zip(edges, edges[1:]) if start < stop]


def load_tiles(first, cols, gate_hbm, up_hbm, gate_ref, up_ref, sems):
    def copies(i, start, stop):
        return [
            pltpu.make_async_copy(
                source.at[pl.ds(first + start, stop - start)], target.at[pl.ds(start, stop - start)], sems.at[j, i]
            )
            for j, (source, target) in enumerate(((gate_hbm, gate_ref), (up_hbm, up_ref)))
        ]

    started = {start: copies(i, start, stop) for i, (start, stop) in enumerate(groups_of(cols))}
    for group in started.values():
        for copy in group:
            copy.start()

    def arrive(c):
        for copy in started.get(c, ()):
            copy.wait()

    return arrive


def store_tiles(first, c, gate_ref, up_ref, gate_hbm, up_hbm, sems):
    copies = [
        pltpu.make_async_copy(gate_ref.at[c], gate_hbm.at[first + c], sems.at[0, c]),
        pltpu.make_async_copy(up_ref.at[c], up_hbm.at[first + c], sems.at[1, c]),
    ]
    for copy in copies:
        copy.start()
    return copies


def forward_own_kernel(x_hbm, rows_hbm, counts_hbm, gate_hbm, up_hbm, part_ref, gate_ref, up_ref, rows_ref, counts_ref, *scratch):
    x_ref, sems, small_sems = scratch
    cols = gate_ref.shape[0]
    small = [
        pltpu.make_async_copy(source, target, small_sems.at[i])
        for i, (source, target) in enumerate(((rows_hbm, rows_ref), (counts_hbm, counts_ref), (x_hbm, x_ref)))
    ]
    for copy in small:
        copy.start()
    arrive = load_tiles(0, cols, gate_hbm, up_hbm, gate_ref, up_ref, sems)
    for copy in small:
        copy.wait()
    for c in range(cols):
        arrive(c)
        part_ref[c] = forward_column(c, 0, (rows_ref, counts_ref), [x_ref], gate_ref, up_ref)


def forward_kernel(members, rows_ref, counts_ref, *refs):
    xs = refs[:members]
    gate_ref, up_ref = refs[members : members + 2]
    part_ref = refs[-1]
    for c in range(gate_ref.shape[0]):
        part_ref[c] = forward_column(c, 0, (rows_ref, counts_ref), xs, gate_ref, up_ref)


def unit(size):
    row, column = (lax.broadcasted_iota(jnp.int32, (size, size), axis) for axis in (0, 1))
    return (row == column).astype(F32).astype(BF16)


def load_forward_kernel(members, groups, first, turn, rows_ref, counts_ref, *refs):
    xs = refs[:members]
    gate_hbm, up_hbm = refs[members : members + 2]
    outs = refs[-(len(groups) + 3 + turn) :]
    parts, gate_ref, up_ref, sems = outs[: len(groups)], outs[-3 - turn], outs[-2 - turn], outs[-1]
    cols, _, _, tile, _ = gate_ref.shape
    arrive = load_tiles(first, cols, gate_hbm, up_hbm, gate_ref, up_ref, sems)
    if turn:
        turned_ref = outs[-2]
        identity = unit(tile)
        for r in range(turned_ref.shape[0]):
            block = jnp.concatenate([x[:, r * tile : (r + 1) * tile] for x in xs], axis=0)
            turned_ref[r] = lax.dot_general(
                identity, block, (((1,), (1,)), ((), ())), preferred_element_type=F32
            ).astype(BF16)
    for c in range(cols):
        arrive(c)
        part = forward_column(c, first, (rows_ref, counts_ref), xs, gate_ref, up_ref)
        for (start, stop), part_ref in zip(groups, parts):
            part_ref[c] = part[start:stop]


def shard_of(member):
    if member < 2:
        return lax.axis_index("tok") ^ member
    return lax.axis_index("tok") ^ ((member & ~1) + ((member & 1) ^ lax.axis_index("sub")))


def cotangent_of(members, cots, shard_rows, where):
    shards_each = cots[0].shape[0] // shard_rows
    blocks = []
    for member in members:
        shard = shard_of(member)
        source = (shard // shards_each) ^ lax.axis_index("blk")
        rows = pl.ds(pl.multiple_of((shard % shards_each) * shard_rows, shard_rows), shard_rows)
        block = cots[0][rows, where]
        for j, cot in enumerate(cots[1:], 1):
            block = jnp.where(source == j, cot[rows, where], block)
        blocks.append(block.astype(F32))
    return jnp.concatenate(blocks, axis=0)


def nonlinear(total, cotangent):
    tile = total.shape[1] // 2
    gate_value, up_value = total[:, :tile], total[:, tile:]
    sig_gate = jax.nn.sigmoid(gate_value)
    act_gate = gate_value * sig_gate
    hidden = (act_gate * up_value).astype(BF16)
    gate_grad = (cotangent * up_value * sig_gate * (1.0 + gate_value * (1.0 - sig_gate))).astype(BF16)
    up_grad = (cotangent * act_gate).astype(BF16)
    return hidden, jnp.concatenate([gate_grad, up_grad], axis=1)


def total_of(c, parts):
    total = parts[0][c].astype(F32)
    for part in parts[1:]:
        total = total + part[c].astype(F32)
    return total


def back_terms(c, grads, gate_ref, up_ref):
    return lax.dot_general(
        grads, weights_of(c, gate_ref, up_ref), (((1,), (1,)), ((), ())), preferred_element_type=F32
    )


def turn_kernel(gate_ref, up_ref, _, turned_ref):
    cols, _, slots, rows, tile = gate_ref.shape
    identity = unit(tile)
    for c in range(cols):
        for i, tiles in enumerate((gate_ref, up_ref)):
            turned_ref[c, i * tile : (i + 1) * tile] = lax.dot_general(
                identity,
                tiles[c, 0].reshape(slots * rows, tile),
                (((1,), (1,)), ((), ())),
                preferred_element_type=F32,
            ).astype(BF16)


def add_back(c, lists, back, accs, slots, tile):
    rows_ref, counts_ref = lists
    rows = [rows_ref[k, 0, c] for k in range(slots)]
    start = 0
    for acc in accs:
        stop = start + acc.shape[1]
        sums = [
            acc[rows[k]] + keep(k, counts_ref[0, c], back[start:stop, k * tile : (k + 1) * tile])
            for k in range(slots)
        ]
        for k in range(slots):
            acc[rows[k]] = sums[k]
        start = stop


def tile_grads(c, first, lists, turned_ref, grads, gate_ref, up_ref):
    rows_ref, counts_ref = lists
    slots, tile = gate_ref.shape[2:4]
    picked = jnp.concatenate([turned_ref[rows_ref[k, 0, first + c]] for k in range(slots)], axis=0)
    found = jnp.dot(picked, grads, preferred_element_type=F32)
    for k in range(slots):
        term = keep(k, counts_ref[0, first + c], found[k * tile : (k + 1) * tile]).astype(BF16)
        gate_ref[c, 0, k] = term[:, :tile]
        up_ref[c, 0, k] = term[:, tile:]


def start_hidden(members, parts, hidden_hbm, shard_rows, sems):
    shards_each = hidden_hbm.shape[0] // shard_rows

    def copies(i, member):
        rows = pl.ds(i * shard_rows, shard_rows)
        return [
            pltpu.make_async_copy(
                array.at[pl.ds(row, shard_rows)], hidden_hbm.at[rows, pl.ds(first, array.shape[1])], sems.at[j, i]
            )
            for j, (array, row, first) in enumerate(parts(member))
        ]

    for i in range(shards_each):
        wanted = lax.axis_index("blk") * shards_each + i
        for member in members:

            @pl.when(shard_of(member) == wanted)
            def _(i=i, member=member):
                for copy in copies(i, member):
                    copy.start()

    return [copy for i in range(shards_each) for copy in copies(i, 0)]


def first_half_kernel(members, owners, rows_ref, counts_ref, gate_w, up_w, turned_ref, *refs):
    groups = [refs[start : start + owners] for start in range(0, 2 * owners, owners)]
    cots = refs[2 * owners : 3 * owners]
    gate_hbm, up_hbm, hidden_ref = refs[-10:-7]
    accs = refs[-7:-4]
    grads_ref, gate_ref, up_ref, sems = refs[-4:]
    cols, _, slots, tile, _ = gate_ref.shape
    shard_rows = hidden_ref.shape[0] // len(members)
    lists = (rows_ref, counts_ref)
    for acc in accs:
        acc[...] = jnp.zeros_like(acc)
    copies = []
    for c in range(cols):
        total = jnp.concatenate([total_of(c, parts) for parts in groups], axis=0)
        where = slice(c * tile, (c + 1) * tile)
        hidden, grads = nonlinear(total, cotangent_of(members, cots, shard_rows, where))
        hidden_ref[:, where] = hidden
        grads_ref[c] = grads
        tile_grads(c, 0, lists, turned_ref, grads, gate_ref, up_ref)
        copies += store_tiles(0, c, gate_ref, up_ref, gate_hbm, up_hbm, sems)
    for c in range(cols):
        add_back(c, lists, back_terms(c, grads_ref[c], gate_w, up_w), accs, slots, tile)
    for copy in copies:
        copy.wait()


def second_half_kernel(members, owners, first, slots, rows_ref, counts_ref, turned_w, acc_in, *refs):
    parts, cots = refs[:owners], refs[owners : 2 * owners]
    outs = refs[-(2 + len(members) + 1) :]
    grads_ref, hidden_ref = outs[:2]
    dxs, acc_ref = outs[2:-1], outs[-1]
    cols, tile = turned_w.shape[0], turned_w.shape[1] // 2
    shard_rows = hidden_ref.shape[0] // len(members)
    acc_ref[...] = acc_in[...]
    for c in range(cols):
        where = slice((first + c) * tile, (first + c + 1) * tile)
        hidden, grads = nonlinear(total_of(c, parts), cotangent_of(members, cots, shard_rows, where))
        hidden_ref[:, c * tile : (c + 1) * tile] = hidden
        grads_ref[c] = grads
        back = jnp.dot(grads, turned_w[c], preferred_element_type=F32)
        add_back(first + c, (rows_ref, counts_ref), back, (acc_ref,), slots, tile)
    for r in range(acc_ref.shape[0]):
        block = acc_ref[r].astype(BF16)
        for m, dx in enumerate(dxs):
            dx[:, r * tile : (r + 1) * tile] = block[m * shard_rows : (m + 1) * shard_rows]
    width = acc_ref.shape[0] * tile
    for dx in dxs:
        if dx.shape[1] > width:
            dx[:, width:] = jnp.zeros_like(dx[:, width:])


def last_half_kernel(members, owners, first, rows_ref, counts_ref, turned_w, turned_ref, acc_in, *refs):
    parts, cots = refs[:owners], refs[owners : 2 * owners]
    next_grads, far_grads, hidden_a, next_hidden, far_hidden = refs[2 * owners : 2 * owners + 5]
    gate_hbm, up_hbm, hidden_hbm, dx_ref = refs[-11:-7]
    acc_ref, grads_ref, hidden_ref, gate_ref, up_ref, sems, hidden_sems = refs[-7:]
    cols, _, slots, tile, _ = gate_ref.shape
    shard_rows = hidden_ref.shape[0]
    lists = (rows_ref, counts_ref)

    def hidden_of(member):
        at = members.index(member)
        mine = ((hidden_ref, 0), (next_hidden, 0))[at] if at < 2 else (far_hidden, (at - 2) * shard_rows)
        return (hidden_a, at * shard_rows, 0), (*mine, first * tile)

    acc_ref[...] = acc_in[...]
    copies = []
    for c in range(cols):
        where = slice((first + c) * tile, (first + c + 1) * tile)
        hidden, grads = nonlinear(total_of(c, parts), cotangent_of(members[:1], cots, shard_rows, where))
        hidden_ref[:, c * tile : (c + 1) * tile] = hidden
        grads_ref[c] = grads
    copies += start_hidden(members, hidden_of, hidden_hbm, shard_rows, hidden_sems)
    for c in range(cols):
        grads = jnp.concatenate([grads_ref[c], next_grads[c], far_grads[c]], axis=0)
        tile_grads(c, first, lists, turned_ref, grads, gate_ref, up_ref)
        copies += store_tiles(first, c, gate_ref, up_ref, gate_hbm, up_hbm, sems)
    for c in range(cols):
        back = jnp.dot(grads_ref[c], turned_w[c], preferred_element_type=F32)
        add_back(first + c, lists, back, (acc_ref,), slots, tile)
    for r in range(acc_ref.shape[0]):
        dx_ref[:, r * tile : (r + 1) * tile] = acc_ref[r].astype(BF16)
    for copy in copies:
        copy.wait()


def copy_kernel(x_ref, _, out_ref):
    out_ref[...] = x_ref[...]


def add_kernel(left_ref, right_ref, _, out_ref):
    right = right_ref[:, : left_ref.shape[1]]
    out_ref[...] = (left_ref[...].astype(F32) + right.astype(F32)).astype(BF16)


def sum_kernel(count, *refs):
    total = sum(ref[...].astype(F32) for ref in refs[:count])
    refs[-2][...] = total
    refs[-1][...] = total.astype(BF16)


def swap(x, axis, step):
    return lax.ppermute(x, axis, [(i, i ^ step) for i in range(lax.axis_size(axis))])


def swap_far(x, base):
    shards, cores = lax.axis_size("tok"), lax.axis_size("sub")
    pairs = [(t * cores + s, (t ^ (base + s)) * cores + s) for t in range(shards) for s in range(cores)]
    return lax.ppermute(x, ("tok", "sub"), pairs)


def on_device(features_in, gate_tiles, up_tiles, block_rows, block_counts, d_hidden):
    shards, owners = lax.axis_size("tok"), lax.axis_size("blk")
    cols, _, slots, tile, _ = gate_tiles.shape
    shard_rows, width = features_in.shape
    row_blocks = width // tile
    row_total = shards * shard_rows
    near_rows = 2 * shard_rows
    half = max(1, cols * 6 // 16)
    bases = range(2, shards, 2)
    lists = (jnp.transpose(block_rows, (2, 1, 0)), jnp.transpose(block_counts, (1, 0)))

    def shape(*dims, dtype=BF16):
        return jax.ShapeDtypeStruct(dims, dtype)

    def cost(tokens, columns, products, tile_bytes, weight=1):
        tiles = weight * columns * slots
        return pl.CostEstimate(
            flops=4 * tokens * tiles * tile * tile * products,
            bytes_accessed=4 * tiles * tile * tile * tile_bytes,
            transcendentals=0,
        )

    def to_owners(part):
        return [part] + [swap(part, "blk", s) for s in range(1, owners)]

    fars = [swap_far(features_in, base) for base in bases]
    features_next = swap(features_in, "tok", 1)
    cots = [d_hidden] + [swap(d_hidden, "blk", s) for s in range(1, owners)]

    def tile_shape(columns):
        return pltpu.VMEM((columns, 1, slots, tile, tile), BF16)

    def from_hbm(*arrays):
        return [pltpu.with_memory_space_constraint(array, pltpu.HBM) for array in arrays]

    near_a, *weights_a, rows_held, counts_held = pl.pallas_call(
        forward_own_kernel,
        out_shape=(
            shape(half, shard_rows, 2 * tile),
            tile_shape(half),
            tile_shape(half),
            pltpu.SMEM(lists[0].shape, jnp.int32),
            pltpu.SMEM(lists[1].shape, jnp.int32),
        ),
        in_specs=[ANY_SPEC] * 5,
        out_specs=(VMEM_SPEC,) * 3 + (SMEM_SPEC,) * 2,
        scratch_shapes=[
            pltpu.VMEM((shard_rows, width), BF16),
            pltpu.SemaphoreType.DMA((2, 3)),
            pltpu.SemaphoreType.DMA((3,)),
        ],
        compiler_params=limit(8),
        cost_estimate=cost(shard_rows, half, 1, 1),
        name="forward_own_a",
    )(*from_hbm(features_in, *lists, gate_tiles, up_tiles))
    near_a = to_owners(near_a)
    lists = (rows_held, counts_held)

    members = [0, 1, *range(2, shards, 2), *range(3, shards, 2)]
    far_members = members[2:]
    own_rows, far_rows = shard_rows, row_total - near_rows
    before_swap = [
        pl.pallas_call(
            copy_kernel,
            out_shape=shape(shard_rows, width),
            in_specs=[VMEM_SPEC, ANY_SPEC],
            out_specs=VMEM_SPEC,
            compiler_params=limit(8),
            cost_estimate=pl.CostEstimate(flops=0, bytes_accessed=0, transcendentals=0),
            name="after_own",
        )(far, near_a[0])
        for far in fars
    ]
    fetched = [features_next, *fars]
    swapped = [swap(far, "sub", 1) for far in before_swap]
    xs = [features_in, *fetched, *swapped]

    def forward_a(name, shard_xs, after):
        tokens = len(shard_xs) * shard_rows
        return to_owners(
            pl.pallas_call(
                functools.partial(forward_kernel, len(shard_xs)),
                out_shape=shape(half, tokens, 2 * tile),
                in_specs=[SMEM_SPEC] * 2 + [VMEM_SPEC] * (len(shard_xs) + 2) + [ANY_SPEC] * len(after),
                out_specs=VMEM_SPEC,
                compiler_params=limit(8),
                cost_estimate=cost(tokens, half, 1, 1),
                name=name,
            )(*lists, *shard_xs, *weights_a, *after)
        )

    rest_a = forward_a("forward_rest_a", [*fetched, *swapped], [cots[-1]])

    rest = cols - half
    groups = ((near_rows, row_total), (own_rows, near_rows), (0, own_rows))
    far_b, next_b, own_b, gate_b, up_b, turned = pl.pallas_call(
        functools.partial(load_forward_kernel, shards, groups, half, 1),
        out_shape=(
            *[shape(rest, stop - start, 2 * tile) for start, stop in groups],
            tile_shape(rest),
            tile_shape(rest),
            pltpu.VMEM((row_blocks, tile, row_total), BF16),
        ),
        in_specs=[SMEM_SPEC] * 2 + [VMEM_SPEC] * shards + [ANY_SPEC] * 4,
        out_specs=(VMEM_SPEC,) * 6,
        scratch_shapes=[pltpu.SemaphoreType.DMA((2, 3))],
        compiler_params=limit(8),
        cost_estimate=cost(row_total, rest, 1, 1, 5),
        name="forward_b",
    )(*lists, *xs, *from_hbm(gate_tiles, up_tiles), rest_a[0], near_a[-1])
    own_b, next_b, far_b = to_owners(own_b), to_owners(next_b), to_owners(far_b)

    turned_b = pl.pallas_call(
        turn_kernel,
        out_shape=shape(rest, 2 * tile, slots * tile),
        in_specs=[VMEM_SPEC] * 2 + [ANY_SPEC],
        out_specs=VMEM_SPEC,
        compiler_params=limit(8),
        cost_estimate=cost(2 * tile, rest, 1, 1, 0),
        name="turn_b",
    )(gate_b, up_b, far_b[0])

    out_tiles = shape(*gate_tiles.shape)
    tile_bytes = slots * tile * tile * 2
    gate_out, up_out, hidden_a, acc_own, acc_next, acc_far = pl.pallas_call(
        functools.partial(first_half_kernel, members, owners),
        out_shape=(
            out_tiles,
            out_tiles,
            shape(row_total, half * tile),
            *[shape(row_blocks, rows, tile, dtype=F32) for rows in (own_rows, own_rows, far_rows)],
        ),
        in_specs=[SMEM_SPEC] * 2 + [VMEM_SPEC] * (3 + 3 * owners) + [ANY_SPEC] * 3,
        out_specs=(ANY_SPEC,) * 2 + (VMEM_SPEC,) * 4,
        scratch_shapes=[
            pltpu.VMEM((half, row_total, 2 * tile), BF16),
            tile_shape(half),
            tile_shape(half),
            pltpu.SemaphoreType.DMA((2, half)),
        ],
        compiler_params=limit(8 + 2 * half * tile_bytes // MIB),
        cost_estimate=cost(row_total, half, 2, 1, 1),
        name="first_half",
    )(
        *lists, *weights_a, turned, *near_a, *rest_a, *cots, far_b[0], next_b[0], turned_b
    )

    def second_half(name, chunk, acc, parts, after, weight):
        rows_here = len(chunk) * shard_rows
        return pl.pallas_call(
            functools.partial(second_half_kernel, chunk, owners, half, slots),
            out_shape=(
                shape(rest, rows_here, 2 * tile),
                shape(rows_here, rest * tile),
                *[shape(shard_rows, max(width, 2 * rest * tile) if m >= 2 and m % 2 else width) for m in chunk],
            ),
            in_specs=[SMEM_SPEC] * 2 + [VMEM_SPEC] * (2 + 2 * owners) + [ANY_SPEC],
            out_specs=(VMEM_SPEC,) * (2 + len(chunk)),
            scratch_shapes=[pltpu.VMEM((row_blocks, rows_here, tile), F32)],
            compiler_params=limit(8),
            cost_estimate=cost(rows_here, rest, 1, 1, weight),
            name=name,
        )(*lists, turned_b, acc, *parts, *cots, after)

    far_grads, far_hidden, *far_dxs = second_half("far_b", far_members, acc_far, far_b, acc_own, 1)
    both_cores = []
    for mine, others in zip(far_dxs[: len(bases)], far_dxs[len(bases) :]):
        both_cores.append(
            pl.pallas_call(
                add_kernel,
                out_shape=shape(shard_rows, width),
                in_specs=[VMEM_SPEC] * 2 + [ANY_SPEC],
                out_specs=VMEM_SPEC,
                compiler_params=limit(8),
                cost_estimate=pl.CostEstimate(flops=0, bytes_accessed=0, transcendentals=0),
                name="add_cores",
            )(mine, swap(others, "sub", 1), next_b[-1])
        )
    back_far = [swap_far(total, base) for total, base in zip(both_cores, bases)]
    next_grads, next_hidden, next_dx = second_half("next_b", [1], acc_next, next_b, both_cores[-1], 1)
    back_next = swap(next_dx, "tok", 1)
    gate_out, up_out, hidden_out, own_dx = pl.pallas_call(
        functools.partial(last_half_kernel, members, owners, half),
        out_shape=(out_tiles, out_tiles, shape(*d_hidden.shape), shape(shard_rows, width)),
        in_specs=[SMEM_SPEC] * 2 + [VMEM_SPEC] * (8 + 2 * owners) + [ANY_SPEC] * 3,
        out_specs=(ANY_SPEC,) * 3 + (VMEM_SPEC,),
        scratch_shapes=[
            pltpu.VMEM((row_blocks, shard_rows, tile), F32),
            pltpu.VMEM((rest, shard_rows, 2 * tile), BF16),
            pltpu.VMEM((shard_rows, rest * tile), BF16),
            tile_shape(rest),
            tile_shape(rest),
            pltpu.SemaphoreType.DMA((2, rest)),
            pltpu.SemaphoreType.DMA((2, d_hidden.shape[0] // shard_rows)),
        ],
        input_output_aliases={10 + 2 * owners: 0, 11 + 2 * owners: 1},
        compiler_params=limit(8 + 2 * rest * tile_bytes // MIB),
        cost_estimate=cost(row_total, rest, 1, 1, 10),
        name="last_half",
    )(
        *lists,
        turned_b,
        turned,
        acc_own,
        *own_b,
        *cots,
        next_grads,
        far_grads,
        hidden_a,
        next_hidden,
        far_hidden,
        gate_out,
        up_out,
        both_cores[-1],
    )
    arrived = [own_dx, back_next, *back_far]
    mine, mine_sent = pl.pallas_call(
        functools.partial(sum_kernel, len(arrived)),
        out_shape=(shape(shard_rows, width, dtype=F32), shape(shard_rows, width)),
        in_specs=[VMEM_SPEC] * len(arrived),
        out_specs=(VMEM_SPEC,) * 2,
        compiler_params=limit(8),
        name="sum_shards",
    )(*arrived)
    features_grad = (mine + swap(mine_sent, "sub", 1).astype(F32)).astype(BF16)
    return (hidden_out, gate_out, up_out, features_grad)


def solution(mesh):
    return jax.shard_map(
        on_device,
        mesh=mesh,
        in_specs=(
            P(("groups", "tok"), "blk"),
            P(("tok", "sub"), "blk", None, None, None),
            P(("tok", "sub"), "blk", None, None, None),
            P(("tok", "sub"), "blk", None),
            P(("tok", "sub"), "blk"),
            P(("groups", "blk"), ("tok", "sub")),
        ),
        out_specs=(
            P(("groups", "blk"), ("tok", "sub")),
            P(("groups", "tok", "sub"), "blk", None, None, None),
            P(("groups", "tok", "sub"), "blk", None, None, None),
            P(("groups", "tok"), "blk"),
        ),
        check_vma=False,
    )
```
